32 devices in a mesh: seq: 16 (over z, y, x), chan: 2 (over core).
Axes of the slice: x: 2, y: 2, z: 4, core: 2. Of those that a mesh axis runs over, the one named last changes fastest.
Arguments:
- gate_acts: bfloat16 [16384, 2048], P('seq', 'chan'), may hold values from -40 to 40
- value_acts: bfloat16 [16384, 2048], P('seq', 'chan'), may hold values from -6 to 6
- kernel: bfloat16 [32, 2048], P('chan'), may hold values from -0.125 to 0.125
- norm_gain: float32 [2048], P('chan'), may hold values from 0.1 to 1.9
- out_grad: bfloat16 [16384, 2048], P('seq', 'chan'), may hold values from -30 to 30
Outputs:
- normed: bfloat16 [16384, 2048], P('seq', 'chan')
- gate_grad: bfloat16 [16384, 2048], P('seq', 'chan')
- value_grad: bfloat16 [16384, 2048], P('seq', 'chan')
- kernel_grad: float32 [32, 2048], P('chan')
- gain_grad: float32 [2048], P('chan')
The draws below stay inside these ranges and needn't reach their ends.
All inputs are finite; a program needn't handle non-finite values.
Results may differ from the reference program's by a relative error of at most 0.0085.
Values may be sent and summed in bfloat16 or wider, within the bound.
No kernel may reach another device: no remote copies, remote signals or barrier semaphores. Data moves between devices by JAX's collectives and lax.ppermute only.
A program may use at most 256 MiB of HBM per device.

```python
import math
import jax
import jax.numpy as jnp
from jax import lax

D = 2048
HEAD_DIM = 64
LAG = 1024
TOK_DEV = 1024
HEADS = 32
TOKENS = 16384


def log_scales(scale_key, shape):
    return jnp.exp(jax.random.uniform(scale_key, shape, jnp.float32, 0.0, math.log(10.0)))


def draw_gate_acts(key, part):
    row_key, col_key, val_key = jax.random.split(jax.random.fold_in(key, 11), 3)
    values_raw = jnp.clip(jax.random.normal(val_key, (TOKENS, D), jnp.float32), -4.0, 4.0)
    rise_factor = 3.0
    col_scale = rise_factor ** (jnp.arange(D, dtype=jnp.float32) / D)[None, :] * log_scales(col_key, (1, D))
    row_scale = log_scales(row_key, (TOKENS, 1))
    return jnp.clip(0.1 * values_raw * row_scale * col_scale, -40.0, 40.0).astype(jnp.bfloat16)


def draw_out_grad(key, part):
    row_key, col_key, val_key = jax.random.split(jax.random.fold_in(key, 23), 3)
    values_raw = jnp.clip(jax.random.normal(val_key, (TOKENS, D), jnp.float32), -4.0, 4.0)
    rise_factor = 3.0
    row_scale = rise_factor ** (jnp.arange(TOKENS, dtype=jnp.float32) / TOKENS)[:, None] * log_scales(row_key, (TOKENS, 1))
    col_scale = log_scales(col_key, (1, D))
    return jnp.clip(0.05 * values_raw * row_scale * col_scale, -30.0, 30.0).astype(jnp.bfloat16)


def shard_levels(key, dims, shards, least, top_value):
    def one(dim, shards_of):
        heights = jax.random.uniform(jax.random.fold_in(jax.random.fold_in(key, 6), dim), (shards_of,), jnp.float32, least / len(shards), top_value / len(shards))
        return jnp.repeat(jnp.exp(heights), dims[dim] // shards_of).reshape((-1,) + (1,) * (len(dims) - dim - 1))

    gain = one(*shards[0])
    for cut in shards[1:]:
        gain = gain * one(*cut)
    return gain


def noise(own_key, shape, width, reach, cuts=(), kind=jnp.bfloat16):
    level = shard_levels(own_key, shape, cuts, -0.22, 0.18) if cuts else 1.0
    values = jax.random.normal(own_key, shape, jnp.float32) * width * level
    return jnp.minimum(jnp.maximum(values, -reach), reach).astype(kind)


def setup_inputs(seed: int = 0) -> dict:
    key_of = jax.random.split(jax.random.key(seed), 6)
    return {
        "gate_acts": draw_gate_acts(jax.random.fold_in(key_of[5], 71), 0),
        "value_acts": noise(key_of[1], (TOKENS, D), 1.0, 6.0, ((0, 16), (1, 2))),
        "kernel": noise(key_of[2], (HEADS, 2 * LAG), (2 * LAG) ** -0.5, 0.125, ((0, 2),)),
        "norm_gain": jnp.clip(1.0 + 0.18 * jax.random.normal(key_of[3], (D,), jnp.float32), 0.1, 1.9),
        "out_grad": draw_out_grad(jax.random.fold_in(key_of[5], 71), 0),
    }


def circular(kernel_row, places, fft_size):
    return jnp.zeros((fft_size,), kernel_row.dtype).at[places].set(kernel_row)

def reference(gate_acts, value_acts, kernel, norm_gain, out_grad):
    head_count = D // HEAD_DIM
    fft_size = 1 << (TOKENS + 2 * LAG).bit_length()
    lag_index = jnp.arange(2 * LAG, dtype=jnp.int32) - LAG
    ahead = jnp.mod(lag_index, fft_size).astype(jnp.int32)
    behind = jnp.mod(-lag_index, fft_size).astype(jnp.int32)
    kernel_wide = kernel.astype(jnp.float32)

    def spectrum(head_block):
        return jnp.fft.rfft(jnp.pad(head_block, ((0, fft_size - TOKENS), (0, 0))), axis=0)

    def to_heads(values):
        return values.astype(jnp.float32).reshape(TOKENS, head_count, HEAD_DIM).transpose(1, 0, 2)

    def from_heads(values):
        return values.transpose(1, 0, 2).reshape(TOKENS, D)
    value_heads = to_heads(value_acts)

    def forward_head(pieces):
        kernel_row, head_block = pieces
        taps = jnp.fft.rfft(circular(kernel_row, ahead, fft_size))
        return jnp.fft.irfft(spectrum(head_block) * taps[:, None], n=fft_size, axis=0)[:TOKENS]
    mixed_sum = from_heads(lax.map(forward_head, (kernel_wide, value_heads)))

    def norm_block(pieces):
        gate_block, mixed_block, grad_block = pieces
        hidden = gate_block.astype(jnp.float32) * mixed_block
        squares = lax.optimization_barrier(jnp.sum(hidden * hidden, axis=1))
        scale = lax.rsqrt(squares / D + 1e-06)
        normed = (hidden * scale[:, None] * norm_gain[None, :]).astype(jnp.bfloat16)
        weighted = norm_gain[None, :] * grad_block.astype(jnp.float32)
        inner = lax.optimization_barrier(jnp.sum(weighted * hidden, axis=1))
        hidden_grad = scale[:, None] * (weighted - hidden * (scale * scale * inner / D)[:, None])
        gate_grad = (hidden_grad * mixed_block).astype(jnp.bfloat16)
        mix_grad = (hidden_grad * gate_block.astype(jnp.float32)).astype(jnp.bfloat16)
        gain_part = lax.optimization_barrier(jnp.sum(grad_block.astype(jnp.float32) * hidden * scale[:, None], axis=0))
        return (normed, gate_grad, mix_grad, gain_part)
    block_count = TOKENS // TOK_DEV
    normed, gate_grad, mix_grad, gain_parts = lax.map(norm_block, (gate_acts.reshape(block_count, TOK_DEV, D), mixed_sum.reshape(block_count, TOK_DEV, D), out_grad.reshape(block_count, TOK_DEV, D)))
    normed = normed.reshape(TOKENS, D)
    gate_grad = gate_grad.reshape(TOKENS, D)
    mix_heads = to_heads(mix_grad.reshape(TOKENS, D))

    def backward_head(pieces):
        kernel_row, grad_block, head_block = pieces
        taps = jnp.fft.rfft(circular(kernel_row, behind, fft_size))
        grad_spec = spectrum(grad_block)
        value_part = jnp.fft.irfft(grad_spec * taps[:, None], n=fft_size, axis=0)[:TOKENS]
        cross = jnp.fft.irfft(lax.optimization_barrier(jnp.sum(grad_spec * jnp.conj(spectrum(head_block)), axis=1)), n=fft_size)
        return (value_part, cross[ahead])
    value_parts, kernel_sums = lax.map(backward_head, (kernel_wide, mix_heads, value_heads))
    value_grad = from_heads(value_parts).astype(jnp.bfloat16)
    kernel_grad = kernel_sums / math.sqrt(TOKENS * HEAD_DIM)
    gain_grad = lax.optimization_barrier(jnp.sum(gain_parts, axis=0)) / math.sqrt(TOKENS)
    return (normed, gate_grad, value_grad, kernel_grad, gain_grad)
```

```python
import functools
import math

import jax
import jax.numpy as jnp
from jax import lax
from jax.experimental import pallas as pl
from jax.experimental.pallas import tpu as pltpu
from jax.sharding import PartitionSpec as P

norm_eps = 1e-06
TILE = 256
LANES = 128
HEAD = 64
CHUNKS = 4
MIB = 1 << 20


def params(mib, rank=1):
    return pltpu.CompilerParams(
        vmem_limit_bytes=mib * MIB, dimension_semantics=("arbitrary",) * rank
    )


def lane_iota(rows):
    return lax.broadcasted_iota(jnp.int32, (rows, LANES), 1)


def band_body(row_ref, band_ref):
    tiles = row_ref.shape[2] // LANES
    upper = lane_iota(LANES) >= lax.broadcasted_iota(jnp.int32, (LANES, LANES), 0)
    for head in range(row_ref.shape[1]):
        before = jnp.zeros((LANES, LANES), jnp.float32)
        band_ref[head, :, :LANES] = before.astype(band_ref.dtype)
        for tile in range(tiles):
            segment = row_ref[0, head : head + 1, tile * LANES : (tile + 1) * LANES]
            turned = pltpu.roll(
                jnp.broadcast_to(segment, (LANES, LANES)), 0, 1, stride=1, stride_axis=0
            )
            cell = jnp.where(upper, turned, before)
            band_ref[head, :, (tile + 1) * LANES : (tile + 2) * LANES] = cell.astype(
                band_ref.dtype
            )
            before = turned


def bands(rows):
    heads, length = rows.shape
    return pl.pallas_call(
        band_body,
        grid=(heads // 2,),
        in_specs=[pl.BlockSpec((1, 2, length), lambda g: (g, 0, 0))],
        out_specs=pl.BlockSpec((2, LANES, length + LANES), lambda g: (g, 0, 0)),
        out_shape=jax.ShapeDtypeStruct((heads, LANES, length + LANES), jnp.bfloat16),
        compiler_params=params(16),
        name="bands",
    )(rows.reshape(heads // 2, 2, length))


def lay_out(slabs, even_ref, odd_ref):
    low = lane_iota(TILE) < HEAD
    turned = [pltpu.roll(slab, HEAD, 1) for slab in slabs]
    for tile in range(len(slabs) // 2):
        cols = slice(tile * LANES, (tile + 1) * LANES)
        first, second = 2 * tile, 2 * tile + 1
        even_ref[0, :, cols] = jnp.where(low, slabs[first], turned[second])
        even_ref[1, :, cols] = jnp.where(low, turned[first], slabs[second])
        if odd_ref is not None and second + 1 < len(slabs):
            odd_ref[0, :, cols] = jnp.where(low, slabs[second], turned[second + 1])
            odd_ref[1, :, cols] = jnp.where(low, turned[second], slabs[second + 1])


def window(even_ref, odd_ref, head, start, width):
    if start % 2 == 0:
        return even_ref[head, :, start * HEAD : start * HEAD + width]
    return odd_ref[head, :, (start - 1) * HEAD : (start - 1) * HEAD + width]


def gather_slabs(odd_dev, own_ref, near_refs, far_refs):
    def pieces(refs):
        return [
            ref[row : row + TILE, :] for ref in refs for row in range(0, ref.shape[0], TILE)
        ]

    near, far, own = pieces(near_refs), pieces(far_refs), pieces([own_ref])
    left = [jnp.where(odd_dev, n, f) for n, f in zip(near, far)]
    right = [jnp.where(odd_dev, f, n) for n, f in zip(near, far)]
    return left + own + right


def band_product(band_ref, even_ref, odd_ref, head, slots, width):
    total = None
    for slot in range(slots):
        at = slot * TILE
        tile = jnp.concatenate(
            [
                band_ref[head, :, LANES + at : LANES + at + TILE],
                band_ref[head, :, at : at + TILE],
            ],
            axis=0,
        )
        part = jnp.dot(
            tile,
            window(even_ref, odd_ref, head, slot, width),
            preferred_element_type=jnp.float32,
        )
        total = part if total is None else total + part
    return total


def token_blocks(first, second):
    low = lane_iota(TILE) < HEAD
    blocks = []
    for tile in range(first.shape[1] // LANES):
        cols = slice(tile * LANES, (tile + 1) * LANES)
        one, two = first[:, cols], second[:, cols]
        blocks.append(jnp.where(low, one, pltpu.roll(two, HEAD, 1)))
        blocks.append(jnp.where(low, pltpu.roll(one, HEAD, 1), two))
    return blocks


def forward_body(slots, odd_ref_scalar, band_ref, own_ref, *refs):
    near_refs, far_refs = refs[:CHUNKS], refs[CHUNKS : 2 * CHUNKS]
    gate_ref, grad_ref, gain_ref, mixed_ref, sums_ref = refs[2 * CHUNKS : 2 * CHUNKS + 5]
    even_ref, odd_ref, square_ref, inner_ref = refs[2 * CHUNKS + 5 :]
    step = pl.program_id(0)

    @pl.when(step == 0)
    def _():
        square_ref[...] = jnp.zeros_like(square_ref)
        inner_ref[...] = jnp.zeros_like(inner_ref)

    rows = own_ref.shape[0]
    width = rows // TILE * HEAD
    lay_out(
        gather_slabs(odd_ref_scalar[0] == 1, own_ref, near_refs, far_refs), even_ref, odd_ref
    )
    results = [
        band_product(band_ref, even_ref, odd_ref, head, slots, width) for head in range(2)
    ]
    for index, mixed in enumerate(token_blocks(*results)):
        at = slice(index * TILE, (index + 1) * TILE)
        mixed_ref[at, :] = mixed
        hidden = gate_ref[at, :].astype(jnp.float32) * mixed
        weighted = gain_ref[...] * grad_ref[at, :].astype(jnp.float32)
        square_ref[at, :] += hidden * hidden
        inner_ref[at, :] += weighted * hidden

    @pl.when(step == pl.num_programs(0) - 1)
    def _():
        for at in range(0, rows, LANES):
            cols = slice(at, at + LANES)
            sums_ref[0:1, cols] = jnp.sum(square_ref[cols, :].T, axis=0, keepdims=True)
            sums_ref[1:2, cols] = jnp.sum(inner_ref[cols, :].T, axis=0, keepdims=True)


def slab_spec(rows):
    return pl.BlockSpec((rows, LANES), lambda g: (0, g))


def band_spec(band):
    return pl.BlockSpec((2,) + band.shape[1:], lambda g: (g, 0, 0))


def chunk_specs(chunks):
    return [slab_spec(chunk.shape[0]) for chunk in chunks]


SCALAR = pl.BlockSpec(memory_space=pltpu.SMEM)


def layout_scratch(rows, lag):
    blocks = (rows + 2 * lag) // TILE
    return [
        pltpu.VMEM((2, TILE, blocks * HEAD), jnp.bfloat16),
        pltpu.VMEM((2, TILE, blocks * HEAD - LANES), jnp.bfloat16),
    ]


def forward(odd_dev, band, own, near, far, gate, grad, gain, lag):
    rows, width = own.shape
    slots = 1 + 2 * lag // TILE
    flops = 2 * (width // HEAD) * TILE * TILE * slots * rows // TILE * HEAD
    return pl.pallas_call(
        functools.partial(forward_body, slots),
        grid=(width // LANES,),
        in_specs=[SCALAR, band_spec(band), slab_spec(rows)]
        + chunk_specs(near)
        + chunk_specs(far)
        + [slab_spec(rows), slab_spec(rows), slab_spec(1)],
        out_specs=[slab_spec(rows), pl.BlockSpec((2, rows), lambda g: (0, 0))],
        out_shape=[
            jax.ShapeDtypeStruct((rows, width), jnp.float32),
            jax.ShapeDtypeStruct((2, rows), jnp.float32),
        ],
        scratch_shapes=layout_scratch(rows, lag)
        + [pltpu.VMEM((rows, LANES), jnp.float32)] * 2,
        compiler_params=params(32),
        cost_estimate=pl.CostEstimate(
            flops=flops, bytes_accessed=16 * rows * width, transcendentals=0
        ),
        name="forward",
    )(odd_dev, band, own, *near, *far, gate, grad, gain)


def token_columns(full_width, sums_ref, scale_ref, pull_ref):
    for at in range(0, sums_ref.shape[1], LANES):
        cols = slice(at, at + LANES)
        scale = lax.rsqrt(sums_ref[0:1, cols] / full_width + norm_eps)
        pull = scale * scale * sums_ref[1:2, cols] / full_width
        scale_ref[cols, :] = jnp.broadcast_to(scale, (LANES, LANES)).T
        pull_ref[cols, :] = jnp.broadcast_to(pull, (LANES, LANES)).T


def mix_grad_body(full_width, sums_ref, mixed_ref, gate_ref, grad_ref, gain_ref, out_ref, *scratch):
    scale_ref, pull_ref = scratch

    @pl.when(pl.program_id(0) == 0)
    def _():
        token_columns(full_width, sums_ref, scale_ref, pull_ref)

    for at in range(0, mixed_ref.shape[0], LANES):
        rows = slice(at, at + LANES)
        gate = gate_ref[rows, :].astype(jnp.float32)
        hidden = gate * mixed_ref[rows, :]
        weighted = gain_ref[...] * grad_ref[rows, :].astype(jnp.float32)
        hidden_grad = scale_ref[rows, :] * (weighted - hidden * pull_ref[rows, :])
        out_ref[rows, :] = (hidden_grad * gate).astype(out_ref.dtype)


def norm_body(full_width, sums_ref, mixed_ref, gate_ref, grad_ref, gain_ref, *refs):
    normed_ref, gate_grad_ref, gain_grad_ref, scale_ref, pull_ref = refs

    @pl.when(pl.program_id(0) == 0)
    def _():
        token_columns(full_width, sums_ref, scale_ref, pull_ref)

    gain = gain_ref[...]
    total = jnp.zeros((8, LANES), jnp.float32)
    for at in range(0, mixed_ref.shape[0], LANES):
        rows = slice(at, at + LANES)
        gate = gate_ref[rows, :].astype(jnp.float32)
        mixed = mixed_ref[rows, :]
        grad = grad_ref[rows, :].astype(jnp.float32)
        scale = scale_ref[rows, :]
        hidden = gate * mixed
        scaled = hidden * scale
        normed_ref[rows, :] = (scaled * gain).astype(normed_ref.dtype)
        hidden_grad = scale * (gain * grad - hidden * pull_ref[rows, :])
        gate_grad_ref[rows, :] = (hidden_grad * mixed).astype(gate_grad_ref.dtype)
        total += jnp.sum((grad * scaled).reshape(LANES // 8, 8, LANES), axis=0)
    gain_grad_ref[...] = jnp.sum(total, axis=0, keepdims=True)


def norm_call(body, out_shape, name, full_width, sums, mixed, gate, grad, gain):
    rows, width = mixed.shape
    return pl.pallas_call(
        functools.partial(body, full_width),
        grid=(width // LANES,),
        in_specs=[pl.BlockSpec((2, rows), lambda g: (0, 0))]
        + [slab_spec(rows)] * 3
        + [slab_spec(1)],
        out_specs=jax.tree.map(lambda s: slab_spec(s.shape[0]), out_shape),
        out_shape=out_shape,
        scratch_shapes=[pltpu.VMEM((rows, LANES), jnp.float32)] * 2,
        compiler_params=params(24),
        cost_estimate=pl.CostEstimate(
            flops=10 * rows * width, bytes_accessed=12 * rows * width, transcendentals=0
        ),
        name=name,
    )(sums, mixed, gate, grad, gain)


def kernel_grad_body(slots, odd_ref_scalar, mix_ref, own_ref, *refs):
    near_refs, far_refs = refs[:CHUNKS], refs[CHUNKS : 2 * CHUNKS]
    out_ref, even_ref, odd_ref, mix_even_ref, cells_ref = refs[2 * CHUNKS :]
    rows = own_ref.shape[0]
    width = rows // TILE * HEAD
    lay_out(
        gather_slabs(odd_ref_scalar[0] == 1, own_ref, near_refs, far_refs), even_ref, odd_ref
    )
    lay_out([mix_ref[at : at + TILE, :] for at in range(0, rows, TILE)], mix_even_ref, None)
    span = cells_ref.shape[1]
    for head in range(2):
        mix = mix_even_ref[head]
        carry = None
        for lag_slot in range(slots):
            cross = lax.dot_general(
                window(even_ref, odd_ref, head, slots - 1 - lag_slot, width),
                mix,
                (((1,), (1,)), ((), ())),
                preferred_element_type=jnp.float32,
            )
            at = 2 * lag_slot * LANES
            upper, lower = cross[:LANES], cross[LANES:]
            if carry is not None:
                cells_ref[:, at - LANES : at] = carry + lower[:, :LANES]
            cells_ref[:, at : at + LANES] = upper[:, :LANES] + lower[:, LANES:]
            carry = upper[:, LANES:]
        total = cells_ref[0:8, :]
        for group in range(1, LANES // 8):
            total += pltpu.roll(cells_ref[8 * group : 8 * group + 8, :], span - 8 * group, 1)
        row = lax.broadcasted_iota(jnp.int32, (8, span), 0)
        for bit in (1, 2, 4):
            total = jnp.where((row & bit) != 0, pltpu.roll(total, span - bit, 1), total)
        out_ref[0, head : head + 1, :] = jnp.sum(total, axis=0, keepdims=True)[
            :, : out_ref.shape[2]
        ]


def kernel_grad_local(odd_dev, mix_grad, own, near, far, lag):
    rows, width = own.shape
    slots = 1 + 2 * lag // TILE
    pairs = width // LANES
    flops = 2 * (width // HEAD) * TILE * TILE * slots * rows // TILE * HEAD
    out = pl.pallas_call(
        functools.partial(kernel_grad_body, slots),
        grid=(pairs,),
        in_specs=[SCALAR, slab_spec(rows), slab_spec(rows)]
        + chunk_specs(near)
        + chunk_specs(far),
        out_specs=pl.BlockSpec((1, 2, 2 * lag), lambda g: (g, 0, 0)),
        out_shape=jax.ShapeDtypeStruct((pairs, 2, 2 * lag), jnp.float32),
        scratch_shapes=layout_scratch(rows, lag)
        + [
            pltpu.VMEM((2, TILE, rows // TILE * HEAD), jnp.bfloat16),
            pltpu.VMEM((LANES, 2 * lag + LANES), jnp.float32),
        ],
        compiler_params=params(32),
        cost_estimate=pl.CostEstimate(
            flops=flops, bytes_accessed=8 * rows * width, transcendentals=0
        ),
        name="kernel_grad",
    )(odd_dev, mix_grad, own, *near, *far)
    return out.reshape(2 * pairs, 2 * lag)


def value_grad_body(slots, odd_ref_scalar, band_ref, own_ref, *refs):
    near_refs, far_refs = refs[:CHUNKS], refs[CHUNKS : 2 * CHUNKS]
    out_ref, even_ref, odd_ref = refs[2 * CHUNKS :]
    width = own_ref.shape[0] // TILE * HEAD
    lay_out(
        gather_slabs(odd_ref_scalar[0] == 1, own_ref, near_refs, far_refs), even_ref, odd_ref
    )
    results = [
        band_product(band_ref, even_ref, odd_ref, head, slots, width) for head in range(2)
    ]
    for index, block in enumerate(token_blocks(*results)):
        out_ref[index * TILE : (index + 1) * TILE, :] = block.astype(out_ref.dtype)


def value_grad_of(odd_dev, band, own, near, far, lag):
    rows, width = own.shape
    slots = 1 + 2 * lag // TILE
    flops = 2 * (width // HEAD) * TILE * TILE * slots * rows // TILE * HEAD
    return pl.pallas_call(
        functools.partial(value_grad_body, slots),
        grid=(width // LANES,),
        in_specs=[SCALAR, band_spec(band), slab_spec(rows)]
        + chunk_specs(near)
        + chunk_specs(far),
        out_specs=slab_spec(rows),
        out_shape=jax.ShapeDtypeStruct((rows, width), jnp.bfloat16),
        scratch_shapes=layout_scratch(rows, lag),
        compiler_params=params(32),
        cost_estimate=pl.CostEstimate(
            flops=flops, bytes_accessed=12 * rows * width, transcendentals=0
        ),
        name="value_grad",
    )(odd_dev, band, own, *near, *far)


def neighbours(block):
    count = lax.axis_size("seq")
    swap = [(i, i ^ 1) for i in range(count)]
    relay = [(i, i + 2) if i % 2 == 0 else (i, i - 2) for i in range(count)]
    relay = [(source, target) for source, target in relay if 0 <= target < count]
    size = block.shape[0] // CHUNKS
    near = [
        lax.ppermute(block[c * size : (c + 1) * size], "seq", swap) for c in range(CHUNKS)
    ]
    far = [lax.ppermute(piece, "seq", relay) for piece in near]
    return near, far


def sum_over_seq(value):
    count = lax.axis_size("seq")
    if count & (count - 1):
        return lax.psum(value, "seq")
    step = 1
    while step < count:
        value = value + lax.ppermute(value, "seq", [(i, i ^ step) for i in range(count)])
        step *= 2
    return value


def on_device(gate_acts, value_acts, kernel, norm_gain, out_grad):
    rows, width = value_acts.shape
    heads = kernel.shape[0]
    lag = kernel.shape[1] // 2
    assert width == heads * HEAD and rows == lag and rows % TILE == 0
    full_width = width * lax.axis_size("chan")
    odd_dev = (lax.axis_index("seq") % 2).astype(jnp.int32).reshape(1)
    gain = norm_gain.reshape(1, width)

    near, far = neighbours(value_acts)
    taps = kernel.astype(jnp.float32)
    band = bands(jnp.pad(taps[:, ::-1], ((0, 0), (1, TILE - 1))))
    mixed, sums = forward(
        odd_dev, band, value_acts, near, far, gate_acts, out_grad, gain, lag
    )
    sums = lax.psum(sums, "chan")
    big = jax.ShapeDtypeStruct((rows, width), jnp.bfloat16)
    args = (full_width, sums, mixed, gate_acts, out_grad, gain)
    mix_grad = norm_call(mix_grad_body, big, "mix_grad", *args)
    grad_near, grad_far = neighbours(mix_grad)
    normed, gate_grad, gain_local = norm_call(
        norm_body, [big, big, jax.ShapeDtypeStruct((1, width), jnp.float32)], "norm", *args
    )
    kernel_local = kernel_grad_local(odd_dev, mix_grad, value_acts, near, far, lag)
    totals = sum_over_seq(
        jnp.concatenate([kernel_local, gain_local.reshape(heads, HEAD)], axis=1)
    )
    back_band = bands(jnp.pad(taps, ((0, 0), (0, TILE))))
    value_grad = value_grad_of(odd_dev, back_band, mix_grad, grad_near, grad_far, lag)
    tokens = rows * lax.axis_size("seq")
    kernel_grad = totals[:, : 2 * lag] / math.sqrt(tokens * HEAD)
    gain_grad = totals[:, 2 * lag :].reshape(width) / math.sqrt(tokens)
    return (normed, gate_grad, value_grad, kernel_grad, gain_grad)


def solution(mesh):
    placed = (P("seq", "chan"), P("seq", "chan"), P("chan", None), P("chan"), P("seq", "chan"))
    return jax.shard_map(
        on_device,
        mesh=mesh,
        in_specs=placed,
        out_specs=(
            P("seq", "chan"),
            P("seq", "chan"),
            P("seq", "chan"),
            P("chan", None),
            P("chan"),
        ),
        check_vma=False,
    )
```

```python
import functools
import math

import jax
import jax.numpy as jnp
from jax import lax
from jax.experimental import pallas as pl
from jax.experimental.pallas import tpu as pltpu
from jax.sharding import PartitionSpec as P

norm_eps = 1e-06
TILE = 256
LANES = 128
HEAD = 64
VALUE_CHUNKS = 8
GRAD_CHUNKS = 4
MIB = 1 << 20


def params(mib):
    return pltpu.CompilerParams(
        vmem_limit_bytes=mib * MIB, dimension_semantics=("arbitrary",)
    )


def cost(flops, moved):
    return pl.CostEstimate(flops=flops, bytes_accessed=moved, transcendentals=0)


def lane_iota(rows):
    return lax.broadcasted_iota(jnp.int32, (rows, LANES), 1)


def slab(first=0):
    return pl.ds(pl.multiple_of((first + pl.program_id(0)) * LANES, LANES), LANES)


VMEM = pl.BlockSpec(memory_space=pltpu.VMEM)


def held(*arrays):
    return [pltpu.with_memory_space_constraint(array, pltpu.VMEM) for array in arrays]


def after(value, *others):
    return lax.optimization_barrier((value, *others))[0]


def band_body(row_ref, band_ref):
    tiles = row_ref.shape[2] // LANES
    step = pl.program_id(0)
    upper = lane_iota(LANES) >= lax.broadcasted_iota(jnp.int32, (LANES, LANES), 0)
    for half in range(2):
        head = 2 * step + half
        before = jnp.zeros((LANES, LANES), jnp.float32)
        band_ref[head, :, :LANES] = before.astype(band_ref.dtype)
        for tile in range(tiles):
            segment = row_ref[step, half : half + 1, tile * LANES : (tile + 1) * LANES]
            turned = pltpu.roll(
                jnp.broadcast_to(segment, (LANES, LANES)), 0, 1, stride=1, stride_axis=0
            )
            cell = jnp.where(upper, turned, before)
            band_ref[head, :, (tile + 1) * LANES : (tile + 2) * LANES] = cell.astype(
                band_ref.dtype
            )
            before = turned


def band_rows(taps, low, high):
    heads = taps.shape[0]
    return jnp.pad(taps, ((0, 0), (low, high))).reshape(heads // 2, 2, -1)


def bands(rows):
    heads, length = 2 * rows.shape[0], rows.shape[2]
    return pl.pallas_call(
        band_body,
        grid=(heads // 2,),
        in_specs=[VMEM],
        out_specs=VMEM,
        out_shape=pltpu.VMEM((heads, LANES, length + LANES), jnp.bfloat16),
        compiler_params=params(4),
        cost_estimate=cost(heads * LANES * length, 2 * heads * LANES * length),
        name="bands",
    )(*held(rows))


def blocks_of(refs, first=0):
    pieces = []
    for ref in refs:
        size = min(TILE, ref.shape[0])
        pieces += [ref[row : row + size, slab(first)] for row in range(0, ref.shape[0], size)]
    per = TILE // pieces[0].shape[0]
    return [
        pieces[at] if per == 1 else jnp.concatenate(pieces[at : at + per], axis=0)
        for at in range(0, len(pieces), per)
    ]


def layout_scratch(rows, lag):
    wide = (rows + 2 * lag) // TILE * HEAD
    return [
        pltpu.VMEM((2, TILE, wide), jnp.bfloat16),
        pltpu.VMEM((2, TILE, wide - LANES), jnp.bfloat16),
    ]


def lay_out(blocks, even_ref, odd_ref):
    low = lane_iota(TILE) < HEAD
    turned = [pltpu.roll(block, HEAD, 1) for block in blocks]
    for tile in range(len(blocks) // 2):
        cols = slice(tile * LANES, (tile + 1) * LANES)
        first, second = 2 * tile, 2 * tile + 1
        even_ref[0, :, cols] = jnp.where(low, blocks[first], turned[second])
        even_ref[1, :, cols] = jnp.where(low, turned[first], blocks[second])
        if odd_ref is not None and second + 1 < len(blocks):
            odd_ref[0, :, cols] = jnp.where(low, blocks[second], turned[second + 1])
            odd_ref[1, :, cols] = jnp.where(low, turned[second], blocks[second + 1])


def window(even_ref, odd_ref, head, start, width):
    if start % 2 == 0:
        return even_ref[head, :, start * HEAD : start * HEAD + width]
    return odd_ref[head, :, (start - 1) * HEAD : (start - 1) * HEAD + width]


def extended(own_refs, near_refs, far_refs, first=0):
    odd_dev = lax.axis_index("seq") % 2 == 1
    near, far = blocks_of(near_refs, first), blocks_of(far_refs, first)
    left = [jnp.where(odd_dev, n, f) for n, f in zip(near, far)]
    right = [jnp.where(odd_dev, f, n) for n, f in zip(near, far)]
    return left + blocks_of(own_refs, first) + right


def band_product(band_ref, band_head, even_ref, odd_ref, head, slots, width):
    span = slots * TILE
    tile = jnp.concatenate(
        [band_ref[band_head, :, LANES : LANES + span], band_ref[band_head, :, :span]], axis=0
    )
    data = jnp.concatenate(
        [window(even_ref, odd_ref, head, slot, width) for slot in range(slots)], axis=0
    )
    return jnp.dot(tile, data, preferred_element_type=jnp.float32)


def token_blocks(first, second):
    low = lane_iota(TILE) < HEAD
    blocks = []
    for tile in range(first.shape[1] // LANES):
        cols = slice(tile * LANES, (tile + 1) * LANES)
        one, two = first[:, cols], second[:, cols]
        blocks.append(jnp.where(low, one, pltpu.roll(two, HEAD, 1)))
        blocks.append(jnp.where(low, pltpu.roll(one, HEAD, 1), two))
    return blocks


def product_flops(rows, width, lag):
    return 2 * (width // HEAD) * TILE * (TILE + 2 * lag) * rows // TILE * HEAD


def forward_body(slots, sizes, band_ref, *refs):
    own_refs, refs = refs[: sizes[0]], refs[sizes[0] :]
    near_refs, refs = refs[: sizes[1]], refs[sizes[1] :]
    far_refs, refs = refs[: sizes[2]], refs[sizes[2] :]
    gate_ref, grad_ref, gain_ref, mixed_ref, sums_ref = refs[:5]
    even_ref, odd_ref, square_ref, inner_ref = refs[5:]
    step = pl.program_id(0)

    @pl.when(step == 0)
    def _():
        square_ref[...] = jnp.zeros_like(square_ref)
        inner_ref[...] = jnp.zeros_like(inner_ref)

    rows = mixed_ref.shape[0]
    width = rows // TILE * HEAD
    blocks = extended(own_refs, near_refs, far_refs)
    lay_out(blocks, even_ref, odd_ref)
    results = [
        band_product(band_ref, 2 * step + half, even_ref, odd_ref, half, slots, width)
        for half in range(2)
    ]
    for index, mixed in enumerate(token_blocks(*results)):
        at = slice(index * TILE, (index + 1) * TILE)
        mixed_ref[at, slab()] = mixed
        hidden = gate_ref[at, slab()].astype(jnp.float32) * mixed
        weighted = gain_ref[:, slab()] * grad_ref[at, slab()].astype(jnp.float32)
        square_ref[at, :] += hidden * hidden
        inner_ref[at, :] += weighted * hidden

    @pl.when(step == pl.num_programs(0) - 1)
    def _():
        for at in range(0, rows, LANES):
            cols = slice(at, at + LANES)
            sums_ref[0:1, cols] = jnp.sum(square_ref[cols, :].T, axis=0, keepdims=True)
            sums_ref[1:2, cols] = jnp.sum(inner_ref[cols, :].T, axis=0, keepdims=True)


def forward(band, own, near, far, gate, grad, gain, lag):
    rows, width = gate.shape
    slots = 1 + 2 * lag // TILE
    operands = held(band, *own, *near, *far, gate, grad, gain)
    sizes = (len(own), len(near), len(far))
    return pl.pallas_call(
        functools.partial(forward_body, slots, sizes),
        grid=(width // LANES,),
        in_specs=[VMEM] * len(operands),
        out_specs=[VMEM] * 2,
        out_shape=[
            pltpu.VMEM((rows, width), jnp.float32),
            pltpu.VMEM((2, rows), jnp.float32),
        ],
        scratch_shapes=layout_scratch(rows, lag)
        + [pltpu.VMEM((rows, LANES), jnp.float32)] * 2,
        compiler_params=params(10),
        cost_estimate=cost(product_flops(rows, width, lag), 16 * rows * width),
        name="forward",
    )(*operands)


def token_columns(full_width, sums_ref, at):
    cols = slice(at, at + LANES)
    scale = lax.rsqrt(sums_ref[0:1, cols] / full_width + norm_eps)
    pull = scale * scale * sums_ref[1:2, cols] / full_width
    return (
        jnp.broadcast_to(scale, (LANES, LANES)).T,
        jnp.broadcast_to(pull, (LANES, LANES)).T,
    )


def mix_grad_body(full_width, sums_ref, mixed_ref, gate_ref, grad_ref, gain_ref, *out_refs):
    size = out_refs[0].shape[0]
    for at in range(0, mixed_ref.shape[0], LANES):
        scale, pull = token_columns(full_width, sums_ref, at)
        rows = slice(at, at + LANES)
        out_ref, start = out_refs[at // size], at % size
        for lane in range(0, mixed_ref.shape[1], LANES):
            cols = slice(lane, lane + LANES)
            gate = gate_ref[rows, cols].astype(jnp.float32)
            hidden = gate * mixed_ref[rows, cols]
            weighted = gain_ref[:, cols] * grad_ref[rows, cols].astype(jnp.float32)
            hidden_grad = scale * (weighted - hidden * pull)
            out_ref[start : start + LANES, cols] = (hidden_grad * gate).astype(out_ref.dtype)


def mix_grad_of(full_width, chunks, sums, mixed, gate, grad, gain):
    rows, width = mixed.shape
    operands = held(sums, mixed, gate, grad, gain)
    return pl.pallas_call(
        functools.partial(mix_grad_body, full_width),
        in_specs=[VMEM] * len(operands),
        out_specs=[VMEM] * chunks,
        out_shape=[pltpu.VMEM((rows // chunks, width), jnp.bfloat16)] * chunks,
        compiler_params=pltpu.CompilerParams(vmem_limit_bytes=4 * MIB),
        cost_estimate=cost(10 * rows * width, 10 * rows * width),
        name="mix_grad",
    )(*operands)


def norm_body(full_width, sums_ref, mixed_ref, gate_ref, grad_ref, gain_ref, *refs):
    normed_ref, gate_grad_ref, gain_grad_ref, total_ref = refs
    step = pl.program_id(0)

    @pl.when(step == 0)
    def _():
        total_ref[...] = jnp.zeros_like(total_ref)

    tokens = pl.ds(pl.multiple_of(step * LANES, LANES), LANES)
    scale_row = lax.rsqrt(sums_ref[0:1, tokens] / full_width + norm_eps)
    pull_row = scale_row * scale_row * sums_ref[1:2, tokens] / full_width
    scale = jnp.broadcast_to(scale_row, (LANES, LANES)).T
    pull = jnp.broadcast_to(pull_row, (LANES, LANES)).T
    for lane in range(0, mixed_ref.shape[1], LANES):
        cols = slice(lane, lane + LANES)
        gain = gain_ref[:, cols]
        gate = gate_ref[tokens, cols].astype(jnp.float32)
        mixed = mixed_ref[tokens, cols]
        grad = grad_ref[tokens, cols].astype(jnp.float32)
        hidden = gate * mixed
        scaled = hidden * scale
        normed_ref[:, cols] = (scaled * gain).astype(normed_ref.dtype)
        hidden_grad = scale * (gain * grad - hidden * pull)
        gate_grad_ref[:, cols] = (hidden_grad * mixed).astype(gate_grad_ref.dtype)
        total_ref[:, cols] += jnp.sum((grad * scaled).reshape(LANES // 8, 8, LANES), axis=0)

    @pl.when(step == pl.num_programs(0) - 1)
    def _():
        gain_grad_ref[...] = jnp.sum(total_ref[...], axis=0, keepdims=True)


def norm(full_width, sums, mixed, gate, grad, gain):
    rows, width = mixed.shape
    operands = held(sums, mixed, gate, grad, gain)
    big = jax.ShapeDtypeStruct((rows, width), jnp.bfloat16)
    return pl.pallas_call(
        functools.partial(norm_body, full_width),
        grid=(rows // LANES,),
        in_specs=[VMEM] * len(operands),
        out_specs=[pl.BlockSpec((LANES, width), lambda g: (g, 0))] * 2 + [VMEM],
        out_shape=[big, big, pltpu.VMEM((1, width), jnp.float32)],
        scratch_shapes=[pltpu.VMEM((8, width), jnp.float32)],
        compiler_params=params(6),
        cost_estimate=cost(14 * rows * width, 12 * rows * width),
        name="norm",
    )(*operands)


def kernel_grad_body(first, slots, sizes, gain_ref, *refs):
    own_refs, refs = refs[: sizes[0]], refs[sizes[0] :]
    near_refs, refs = refs[: sizes[1]], refs[sizes[1] :]
    far_refs, refs = refs[: sizes[2]], refs[sizes[2] :]
    mix_refs, (out_ref, even_ref, odd_ref, mix_even_ref, cells_ref) = refs[:-5], refs[-5:]
    step = pl.program_id(0)
    blocks = extended(own_refs, near_refs, far_refs, first)
    lay_out(blocks, even_ref, odd_ref)
    blocks = blocks_of(mix_refs, first)
    lay_out(blocks, mix_even_ref, None)
    width = len(blocks) * HEAD
    span = cells_ref.shape[1]
    lags = span - LANES
    gains = gain_ref[:, slab(first)]
    for half in range(2):
        mix = mix_even_ref[half]
        carry = None
        for lag_slot in range(slots):
            cross = lax.dot_general(
                window(even_ref, odd_ref, half, slots - 1 - lag_slot, width),
                mix,
                (((1,), (1,)), ((), ())),
                preferred_element_type=jnp.float32,
            )
            at = 2 * lag_slot * LANES
            upper, lower = cross[:LANES], cross[LANES:]
            if carry is not None:
                cells_ref[:, at - LANES : at] = carry + lower[:, :LANES]
            cells_ref[:, at : at + LANES] = upper[:, :LANES] + lower[:, LANES:]
            carry = upper[:, LANES:]
        total = cells_ref[0:8, :]
        for group in range(1, LANES // 8):
            total += pltpu.roll(cells_ref[8 * group : 8 * group + 8, :], span - 8 * group, 1)
        row = lax.broadcasted_iota(jnp.int32, (8, span), 0)
        for bit in (1, 2, 4):
            total = jnp.where((row & bit) != 0, pltpu.roll(total, span - bit, 1), total)
        sums = jnp.concatenate(
            [
                jnp.sum(total, axis=0, keepdims=True)[:, :lags],
                gains if half == 0 else pltpu.roll(gains, HEAD, 1),
            ],
            axis=1,
        )
        own_row = lax.broadcasted_iota(jnp.int32, out_ref.shape, 0) == 2 * step + half
        out_ref[...] = jnp.where(own_row, sums, out_ref[...])


def kernel_grad_local(first, pairs, gain_sums, own, near, far, mix_grad, lag):
    rows, width = sum(chunk.shape[0] for chunk in mix_grad), 2 * pairs * HEAD
    slots = 1 + 2 * lag // TILE
    operands = held(gain_sums, *own, *near, *far, *mix_grad)
    sizes = (len(own), len(near), len(far))
    return pl.pallas_call(
        functools.partial(kernel_grad_body, first, slots, sizes),
        grid=(pairs,),
        in_specs=[VMEM] * len(operands),
        out_specs=VMEM,
        out_shape=pltpu.VMEM((2 * pairs, 2 * lag + LANES), jnp.float32),
        scratch_shapes=layout_scratch(rows, lag)
        + [
            pltpu.VMEM((2, TILE, rows // TILE * HEAD), jnp.bfloat16),
            pltpu.VMEM((LANES, 2 * lag + LANES), jnp.float32),
        ],
        compiler_params=params(10),
        cost_estimate=cost(product_flops(rows, width, lag), 8 * rows * width),
        name="kernel_grad",
    )(*operands)


def value_grad_body(slots, sizes, band_ref, *refs):
    own_refs, refs = refs[: sizes[0]], refs[sizes[0] :]
    near_refs, refs = refs[: sizes[1]], refs[sizes[1] :]
    far_refs, (out_ref, even_ref, odd_ref) = refs[: sizes[2]], refs[sizes[2] :]
    step = pl.program_id(0)
    width = out_ref.shape[0] // TILE * HEAD
    blocks = extended(own_refs, near_refs, far_refs)
    lay_out(blocks, even_ref, odd_ref)
    results = [
        band_product(band_ref, 2 * step + half, even_ref, odd_ref, half, slots, width)
        for half in range(2)
    ]
    for index, block in enumerate(token_blocks(*results)):
        out_ref[index * TILE : (index + 1) * TILE, :] = block.astype(out_ref.dtype)


def value_grad_of(band, own, near, far, lag):
    rows, width = sum(chunk.shape[0] for chunk in own), own[0].shape[1]
    slots = 1 + 2 * lag // TILE
    operands = held(band, *own, *near, *far)
    sizes = (len(own), len(near), len(far))
    return pl.pallas_call(
        functools.partial(value_grad_body, slots, sizes),
        grid=(width // LANES,),
        in_specs=[VMEM] * len(operands),
        out_specs=pl.BlockSpec((rows, LANES), lambda g: (0, g)),
        out_shape=jax.ShapeDtypeStruct((rows, width), jnp.bfloat16),
        scratch_shapes=layout_scratch(rows, lag),
        compiler_params=params(10),
        cost_estimate=cost(product_flops(rows, width, lag), 12 * rows * width),
        name="value_grad",
    )(*operands)


def swapped(chunk):
    count = lax.axis_size("seq")
    return lax.ppermute(chunk, "seq", [(i, i ^ 1) for i in range(count)])


def relayed(chunk):
    count = lax.axis_size("seq")
    pairs = [(i, i + 2) if i % 2 == 0 else (i, i - 2) for i in range(count)]
    return lax.ppermute(chunk, "seq", [(i, j) for i, j in pairs if 0 <= j < count])


def sum_over(value, axis):
    count = lax.axis_size(axis)
    if count & (count - 1):
        return lax.psum(value, axis)
    for bit in range(count.bit_length() - 1):
        value += lax.ppermute(value, axis, [(i, i ^ (1 << bit)) for i in range(count)])
    return value


def on_device(gate_acts, value_acts, kernel, norm_gain, out_grad):
    rows, width = value_acts.shape
    heads = kernel.shape[0]
    lag = kernel.shape[1] // 2
    count = lax.axis_size("seq")
    assert width == heads * HEAD and rows == lag and rows % TILE == 0
    assert count & (count - 1) == 0
    full_width = width * lax.axis_size("chan")
    gain = norm_gain.reshape(1, width)
    taps = kernel.astype(jnp.float32)

    size = rows // VALUE_CHUNKS
    ahead, behind = lax.optimization_barrier(
        (band_rows(taps[:, ::-1], 1, TILE - 1), band_rows(taps, 0, TILE))
    )
    band = bands(ahead)
    near, far = [], []
    for index in range(VALUE_CHUNKS):
        chunk = value_acts[index * size : (index + 1) * size]
        if index == 4:
            chunk = after(chunk, near[1])
        elif index > 4:
            chunk = after(chunk, far[index - 5])
        near.append(swapped(chunk))
        if index == 0:
            near[0], band = lax.optimization_barrier((near[0], band))
        far.append(relayed(near[index]))
    mixed, sums = forward(band, [value_acts], near, far, gate_acts, out_grad, gain, lag)
    sums = sum_over(sums, "chan")
    args = (sums, mixed, gate_acts, out_grad, gain)
    mix_grad = mix_grad_of(full_width, GRAD_CHUNKS, *args)

    grad_near = [swapped(chunk) for chunk in mix_grad]
    normed, gate_grad, gain_sums = norm(full_width, *args)
    pairs = heads // 2
    early = pairs // 2
    args = (gain_sums, [value_acts], near, far, mix_grad, lag)
    first = kernel_grad_local(0, early, *args)
    back_band = bands(after(behind, mix_grad[0]))
    grad_near[0], first, back_band = lax.optimization_barrier((grad_near[0], first, back_band))
    second = kernel_grad_local(early, pairs - early, *args)
    grad_near[1], first, second = lax.optimization_barrier((grad_near[1], first, second))
    grad_far = [relayed(chunk) for chunk in grad_near]
    totals = jnp.concatenate([first, second], axis=0)
    for bit in range(count.bit_length() - 1):
        if bit + 1 < GRAD_CHUNKS:
            totals, grad_far[bit] = lax.optimization_barrier((totals, grad_far[bit]))
        totals += lax.ppermute(totals, "seq", [(i, i ^ (1 << bit)) for i in range(count)])
    value_grad = value_grad_of(back_band, mix_grad, grad_near, grad_far, lag)
    tokens = rows * count
    kernel_grad = totals[:, : 2 * lag] / math.sqrt(tokens * HEAD)
    gain_grad = totals[:, 2 * lag : 2 * lag + HEAD].reshape(width) / math.sqrt(tokens)
    return (normed, gate_grad, value_grad, kernel_grad, gain_grad)


def solution(mesh):
    placed = (P("seq", "chan"), P("seq", "chan"), P("chan", None), P("chan"), P("seq", "chan"))
    return jax.shard_map(
        on_device,
        mesh=mesh,
        in_specs=placed,
        out_specs=(
            P("seq", "chan"),
            P("seq", "chan"),
            P("seq", "chan"),
            P("chan", None),
            P("chan"),
        ),
        check_vma=False,
    )
```

```python
import functools
import math

import jax
import jax.numpy as jnp
from jax import lax
from jax.experimental import pallas as pl
from jax.experimental.pallas import tpu as pltpu
from jax.sharding import PartitionSpec as P

norm_eps = 1e-06
TILE = 256
LANES = 128
HEAD = 64
CHUNKS = 4
MIB = 1 << 20


def params(mib):
    return pltpu.CompilerParams(
        vmem_limit_bytes=mib * MIB, dimension_semantics=("arbitrary",)
    )


def cost(flops, moved):
    return pl.CostEstimate(flops=flops, bytes_accessed=moved, transcendentals=0)


def lane_iota(rows):
    return lax.broadcasted_iota(jnp.int32, (rows, LANES), 1)


def slab(pair):
    return pl.ds(pl.multiple_of(pair * LANES, LANES), LANES)


def two_by_two(lay, finish):
    step = pl.program_id(0)
    one, two = 2 * step, 2 * step + 1

    @pl.when(step == 0)
    def _():
        lay(one, 0)

    lay(two, 1)
    finish(one, 0)
    lay(jnp.minimum(two + 1, 2 * pl.num_programs(0) - 1), 0)
    finish(two, 1)


VMEM = pl.BlockSpec(memory_space=pltpu.VMEM)


def held(*arrays):
    return [pltpu.with_memory_space_constraint(array, pltpu.VMEM) for array in arrays]


def after(value, *others):
    return lax.optimization_barrier((value, *others))[0]


def band_body(row_ref, band_ref):
    tiles = row_ref.shape[2] // LANES
    step = pl.program_id(0)
    upper = lane_iota(LANES) >= lax.broadcasted_iota(jnp.int32, (LANES, LANES), 0)
    for half in range(2):
        head = 2 * step + half
        before = jnp.zeros((LANES, LANES), jnp.float32)
        band_ref[head, :, :LANES] = before.astype(band_ref.dtype)
        for tile in range(tiles):
            segment = row_ref[step, half : half + 1, tile * LANES : (tile + 1) * LANES]
            turned = pltpu.roll(
                jnp.broadcast_to(segment, (LANES, LANES)), 0, 1, stride=1, stride_axis=0
            )
            cell = jnp.where(upper, turned, before)
            band_ref[head, :, (tile + 1) * LANES : (tile + 2) * LANES] = cell.astype(
                band_ref.dtype
            )
            before = turned


def band_rows(taps, low, high):
    heads = taps.shape[0]
    return jnp.pad(taps, ((0, 0), (low, high))).reshape(heads // 2, 2, -1)


def bands(rows):
    heads, length = 2 * rows.shape[0], rows.shape[2]
    return pl.pallas_call(
        band_body,
        grid=(heads // 2,),
        in_specs=[VMEM],
        out_specs=VMEM,
        out_shape=pltpu.VMEM((heads, LANES, length + LANES), jnp.bfloat16),
        compiler_params=params(4),
        cost_estimate=cost(heads * LANES * length, 2 * heads * LANES * length),
        name="bands",
    )(*held(rows))


def blocks_of(refs, pair):
    pieces, start = [[] for _ in range(sum(ref.shape[0] for ref in refs) // TILE)], 0
    for ref in refs:
        row = 0
        while row < ref.shape[0]:
            size = min(TILE - (start + row) % TILE, ref.shape[0] - row)
            pieces[(start + row) // TILE].append(ref[row : row + size, slab(pair)])
            row += size
        start += ref.shape[0]
    return [p[0] if len(p) == 1 else jnp.concatenate(p, axis=0) for p in pieces]


def layout_scratch(rows, lag):
    wide = (rows + 2 * lag) // TILE * HEAD
    return [
        pltpu.VMEM((2, TILE, wide), jnp.bfloat16),
        pltpu.VMEM((2, TILE, wide - LANES), jnp.bfloat16),
    ] * 2


def lay_out(blocks, even_ref, odd_ref):
    low = lane_iota(TILE) < HEAD
    turned = [pltpu.roll(block, HEAD, 1) for block in blocks]
    for tile in range(len(blocks) // 2):
        cols = slice(tile * LANES, (tile + 1) * LANES)
        first, second = 2 * tile, 2 * tile + 1
        even_ref[0, :, cols] = jnp.where(low, blocks[first], turned[second])
        even_ref[1, :, cols] = jnp.where(low, turned[first], blocks[second])
        if odd_ref is not None and second + 1 < len(blocks):
            odd_ref[0, :, cols] = jnp.where(low, blocks[second], turned[second + 1])
            odd_ref[1, :, cols] = jnp.where(low, turned[second], blocks[second + 1])


def window(even_ref, odd_ref, head, start, width):
    if start % 2 == 0:
        return even_ref[head, :, start * HEAD : start * HEAD + width]
    return odd_ref[head, :, (start - 1) * HEAD : (start - 1) * HEAD + width]


def extended(own_refs, near_refs, far_refs, pair):
    odd_dev = lax.axis_index("seq") % 2 == 1
    near, far = blocks_of(near_refs, pair), blocks_of(far_refs, pair)
    left = [jnp.where(odd_dev, n, f) for n, f in zip(near, far)]
    right = [jnp.where(odd_dev, f, n) for n, f in zip(near, far)]
    return left + blocks_of(own_refs, pair) + right


def band_product(band_ref, band_head, even_ref, odd_ref, head, slots, width):
    span = slots * TILE
    tile = jnp.concatenate(
        [band_ref[band_head, :, LANES : LANES + span], band_ref[band_head, :, :span]], axis=0
    )
    data = jnp.concatenate(
        [window(even_ref, odd_ref, head, slot, width) for slot in range(slots)], axis=0
    )
    return jnp.dot(tile, data, preferred_element_type=jnp.float32)


def token_blocks(first, second):
    low = lane_iota(TILE) < HEAD
    blocks = []
    for tile in range(first.shape[1] // LANES):
        cols = slice(tile * LANES, (tile + 1) * LANES)
        one, two = first[:, cols], second[:, cols]
        blocks.append(jnp.where(low, one, pltpu.roll(two, HEAD, 1)))
        blocks.append(jnp.where(low, pltpu.roll(one, HEAD, 1), two))
    return blocks


def product_flops(rows, width, lag):
    return 2 * (width // HEAD) * TILE * (TILE + 2 * lag) * rows // TILE * HEAD


def forward_body(slots, sizes, band_ref, *refs):
    own_refs, refs = refs[: sizes[0]], refs[sizes[0] :]
    near_refs, refs = refs[: sizes[1]], refs[sizes[1] :]
    far_refs, refs = refs[: sizes[2]], refs[sizes[2] :]
    gate_ref, grad_ref, gain_ref, mixed_ref, sums_ref = refs[:5]
    laid, (square_ref, inner_ref) = (refs[5:7], refs[7:9]), refs[9:]
    step = pl.program_id(0)

    @pl.when(step == 0)
    def _():
        square_ref[...] = jnp.zeros_like(square_ref)
        inner_ref[...] = jnp.zeros_like(inner_ref)

    rows = mixed_ref.shape[0]
    width = rows // TILE * HEAD

    def lay(pair, side):
        lay_out(extended(own_refs, near_refs, far_refs, pair), *laid[side])

    def finish(pair, side):
        results = [
            band_product(band_ref, 2 * pair + half, *laid[side], half, slots, width)
            for half in range(2)
        ]
        lanes = slab(pair)
        for index, mixed in enumerate(token_blocks(*results)):
            at = slice(index * TILE, (index + 1) * TILE)
            mixed_ref[at, lanes] = mixed
            hidden = gate_ref[at, lanes].astype(jnp.float32) * mixed
            weighted = gain_ref[:, lanes] * grad_ref[at, lanes].astype(jnp.float32)
            square_ref[at, :] += hidden * hidden
            inner_ref[at, :] += weighted * hidden

    two_by_two(lay, finish)

    @pl.when(step == pl.num_programs(0) - 1)
    def _():
        for at in range(0, rows, LANES):
            cols = slice(at, at + LANES)
            sums_ref[0:1, cols] = jnp.sum(square_ref[cols, :].T, axis=0, keepdims=True)
            sums_ref[1:2, cols] = jnp.sum(inner_ref[cols, :].T, axis=0, keepdims=True)


def forward(band, own, near, far, gate, grad, gain, lag):
    rows, width = gate.shape
    slots = 1 + 2 * lag // TILE
    operands = held(band, *own, *near, *far, gate, grad, gain)
    sizes = (len(own), len(near), len(far))
    return pl.pallas_call(
        functools.partial(forward_body, slots, sizes),
        grid=(width // LANES // 2,),
        in_specs=[VMEM] * len(operands),
        out_specs=[VMEM] * 2,
        out_shape=[
            pltpu.VMEM((rows, width), jnp.float32),
            pltpu.VMEM((2, rows), jnp.float32),
        ],
        scratch_shapes=layout_scratch(rows, lag)
        + [pltpu.VMEM((rows, LANES), jnp.float32)] * 2,
        compiler_params=params(10),
        cost_estimate=cost(product_flops(rows, width, lag), 16 * rows * width),
        name="forward",
    )(*operands)


def token_columns(full_width, sums_ref, at):
    cols = slice(at, at + LANES)
    scale = lax.rsqrt(sums_ref[0:1, cols] / full_width + norm_eps)
    pull = scale * scale * sums_ref[1:2, cols] / full_width
    return (
        jnp.broadcast_to(scale, (LANES, LANES)).T,
        jnp.broadcast_to(pull, (LANES, LANES)).T,
    )


def mix_grad_body(full_width, sums_ref, mixed_ref, gate_ref, grad_ref, gain_ref, *refs):
    out_refs, gain_grad_ref, total_ref = refs[:-2], refs[-2], refs[-1]
    size = out_refs[0].shape[0]
    for at in range(0, mixed_ref.shape[0], LANES):
        scale, pull = token_columns(full_width, sums_ref, at)
        rows = slice(at, at + LANES)
        out_ref, start = out_refs[at // size], at % size
        for lane in range(0, mixed_ref.shape[1], LANES):
            cols = slice(lane, lane + LANES)
            gate = gate_ref[rows, cols].astype(jnp.float32)
            grad = grad_ref[rows, cols].astype(jnp.float32)
            hidden = gate * mixed_ref[rows, cols]
            hidden_grad = scale * (gain_ref[:, cols] * grad - hidden * pull)
            out_ref[start : start + LANES, cols] = (hidden_grad * gate).astype(out_ref.dtype)
            part = jnp.sum((grad * (hidden * scale)).reshape(LANES // 8, 8, LANES), axis=0)
            total_ref[:, cols] = part if at == 0 else total_ref[:, cols] + part
    gain_grad_ref[...] = jnp.sum(total_ref[...], axis=0, keepdims=True)


def mix_grad_of(full_width, sums, mixed, gate, grad, gain):
    rows, width = mixed.shape
    operands = held(sums, mixed, gate, grad, gain)
    *chunks, gain_sums = pl.pallas_call(
        functools.partial(mix_grad_body, full_width),
        in_specs=[VMEM] * len(operands),
        out_specs=[VMEM] * (CHUNKS + 1),
        out_shape=[pltpu.VMEM((rows // CHUNKS, width), jnp.bfloat16)] * CHUNKS
        + [pltpu.VMEM((1, width), jnp.float32)],
        scratch_shapes=[pltpu.VMEM((8, width), jnp.float32)],
        compiler_params=pltpu.CompilerParams(vmem_limit_bytes=4 * MIB),
        cost_estimate=cost(14 * rows * width, 10 * rows * width),
        name="mix_grad",
    )(*operands)
    return chunks, gain_sums


def norm_body(full_width, sums_ref, mixed_ref, gate_ref, grad_ref, gain_ref, *refs):
    normed_ref, gate_grad_ref = refs
    step = pl.program_id(0)
    tokens = pl.ds(pl.multiple_of(step * LANES, LANES), LANES)
    scale_row = lax.rsqrt(sums_ref[0:1, tokens] / full_width + norm_eps)
    pull_row = scale_row * scale_row * sums_ref[1:2, tokens] / full_width
    scale = jnp.broadcast_to(scale_row, (LANES, LANES)).T
    pull = jnp.broadcast_to(pull_row, (LANES, LANES)).T
    for lane in range(0, mixed_ref.shape[1], LANES):
        cols = slice(lane, lane + LANES)
        gain = gain_ref[:, cols]
        gate = gate_ref[tokens, cols].astype(jnp.float32)
        mixed = mixed_ref[tokens, cols]
        grad = grad_ref[tokens, cols].astype(jnp.float32)
        hidden = gate * mixed
        scaled = hidden * scale
        normed_ref[:, cols] = (scaled * gain).astype(normed_ref.dtype)
        hidden_grad = scale * (gain * grad - hidden * pull)
        gate_grad_ref[:, cols] = (hidden_grad * mixed).astype(gate_grad_ref.dtype)


def norm(full_width, sums, mixed, gate, grad, gain):
    rows, width = mixed.shape
    operands = held(sums, mixed, gate, grad, gain)
    big = jax.ShapeDtypeStruct((rows, width), jnp.bfloat16)
    return pl.pallas_call(
        functools.partial(norm_body, full_width),
        grid=(rows // LANES,),
        in_specs=[VMEM] * len(operands),
        out_specs=[pl.BlockSpec((LANES, width), lambda g: (g, 0))] * 2,
        out_shape=[big, big],
        compiler_params=params(6),
        cost_estimate=cost(14 * rows * width, 12 * rows * width),
        name="norm",
    )(*operands)


def kernel_grad_body(slots, sizes, gain_ref, *refs):
    own_refs, refs = refs[: sizes[0]], refs[sizes[0] :]
    near_refs, refs = refs[: sizes[1]], refs[sizes[1] :]
    far_refs, refs = refs[: sizes[2]], refs[sizes[2] :]
    mix_refs, (out_ref, even_ref, odd_ref, mix_even_ref, cells_ref) = refs[:-5], refs[-5:]
    step = pl.program_id(0)
    pair = step
    blocks = extended(own_refs, near_refs, far_refs, pair)
    lay_out(blocks, even_ref, odd_ref)
    blocks = blocks_of(mix_refs, pair)
    lay_out(blocks, mix_even_ref, None)
    width = len(blocks) * HEAD
    span = cells_ref.shape[1]
    lags = span - LANES
    gains = gain_ref[:, slab(pair)]
    for half in range(2):
        mix = mix_even_ref[half]
        carry = None
        for lag_slot in range(slots):
            cross = lax.dot_general(
                window(even_ref, odd_ref, half, slots - 1 - lag_slot, width),
                mix,
                (((1,), (1,)), ((), ())),
                preferred_element_type=jnp.float32,
            )
            at = 2 * lag_slot * LANES
            upper, lower = cross[:LANES], cross[LANES:]
            if carry is not None:
                cells_ref[:, at - LANES : at] = carry + lower[:, :LANES]
            cells_ref[:, at : at + LANES] = upper[:, :LANES] + lower[:, LANES:]
            carry = upper[:, LANES:]
        total = cells_ref[0:8, :]
        for group in range(1, LANES // 8):
            total += pltpu.roll(cells_ref[8 * group : 8 * group + 8, :], span - 8 * group, 1)
        row = lax.broadcasted_iota(jnp.int32, (8, span), 0)
        for bit in (1, 2, 4):
            total = jnp.where((row & bit) != 0, pltpu.roll(total, span - bit, 1), total)
        sums = jnp.concatenate(
            [
                jnp.sum(total, axis=0, keepdims=True)[:, :lags],
                gains if half == 0 else pltpu.roll(gains, HEAD, 1),
            ],
            axis=1,
        )
        own_row = lax.broadcasted_iota(jnp.int32, out_ref.shape, 0) == 2 * step + half
        out_ref[...] = jnp.where(own_row, sums, out_ref[...])


def kernel_grad_local(gain_sums, own, near, far, mix_grad, lag):
    rows, width = own[0].shape
    pairs = width // LANES
    slots = 1 + 2 * lag // TILE
    operands = held(gain_sums, *own, *near, *far, *mix_grad)
    sizes = (len(own), len(near), len(far))
    return pl.pallas_call(
        functools.partial(kernel_grad_body, slots, sizes),
        grid=(pairs,),
        in_specs=[VMEM] * len(operands),
        out_specs=VMEM,
        out_shape=pltpu.VMEM((2 * pairs, 2 * lag + LANES), jnp.float32),
        scratch_shapes=layout_scratch(rows, lag)[:2]
        + [
            pltpu.VMEM((2, TILE, rows // TILE * HEAD), jnp.bfloat16),
            pltpu.VMEM((LANES, 2 * lag + LANES), jnp.float32),
        ],
        compiler_params=params(10),
        cost_estimate=cost(product_flops(rows, width, lag), 8 * rows * width),
        name="kernel_grad",
    )(*operands)


def value_grad_body(slots, sizes, band_ref, *refs):
    own_refs, refs = refs[: sizes[0]], refs[sizes[0] :]
    near_refs, refs = refs[: sizes[1]], refs[sizes[1] :]
    far_refs, refs = refs[: sizes[2]], refs[sizes[2] :]
    out_ref, laid = refs[0], (refs[1:3], refs[3:5])
    width = out_ref.shape[0] // TILE * HEAD

    def lay(pair, side):
        lay_out(extended(own_refs, near_refs, far_refs, pair), *laid[side])

    def finish(pair, side):
        results = [
            band_product(band_ref, 2 * pair + half, *laid[side], half, slots, width)
            for half in range(2)
        ]
        cols = slice(side * LANES, (side + 1) * LANES)
        for index, block in enumerate(token_blocks(*results)):
            out_ref[index * TILE : (index + 1) * TILE, cols] = block.astype(out_ref.dtype)

    two_by_two(lay, finish)


def value_grad_of(band, own, near, far, lag):
    rows, width = sum(chunk.shape[0] for chunk in own), own[0].shape[1]
    slots = 1 + 2 * lag // TILE
    operands = held(band, *own, *near, *far)
    sizes = (len(own), len(near), len(far))
    return pl.pallas_call(
        functools.partial(value_grad_body, slots, sizes),
        grid=(width // LANES // 2,),
        in_specs=[VMEM] * len(operands),
        out_specs=pl.BlockSpec((rows, 2 * LANES), lambda g: (0, g)),
        out_shape=jax.ShapeDtypeStruct((rows, width), jnp.bfloat16),
        scratch_shapes=layout_scratch(rows, lag),
        compiler_params=params(10),
        cost_estimate=cost(product_flops(rows, width, lag), 12 * rows * width),
        name="value_grad",
    )(*operands)


def swapped(chunk):
    count = lax.axis_size("seq")
    return lax.ppermute(chunk, "seq", [(i, i ^ 1) for i in range(count)])


def relayed(chunk):
    count = lax.axis_size("seq")
    pairs = [(i, i + 2) if i % 2 == 0 else (i, i - 2) for i in range(count)]
    return lax.ppermute(chunk, "seq", [(i, j) for i, j in pairs if 0 <= j < count])


def sum_over(value, axis):
    count = lax.axis_size(axis)
    if count & (count - 1):
        return lax.psum(value, axis)
    for bit in range(count.bit_length() - 1):
        value += lax.ppermute(value, axis, [(i, i ^ (1 << bit)) for i in range(count)])
    return value


def on_device(gate_acts, value_acts, kernel, norm_gain, out_grad):
    rows, width = value_acts.shape
    heads = kernel.shape[0]
    lag = kernel.shape[1] // 2
    count = lax.axis_size("seq")
    assert width == heads * HEAD and rows == lag and rows % TILE == 0
    assert count & (count - 1) == 0
    full_width = width * lax.axis_size("chan")
    gain = norm_gain.reshape(1, width)
    taps = kernel.astype(jnp.float32)

    ahead, behind = lax.optimization_barrier(
        (band_rows(taps[:, ::-1], 1, TILE - 1), band_rows(taps, 0, TILE))
    )
    band = bands(ahead)
    size = rows // CHUNKS
    near = [swapped(value_acts[at : at + size]) for at in range(0, rows, size)]
    far = [relayed(chunk) for chunk in near]
    mixed, sums = forward(band, [value_acts], near, far, gate_acts, out_grad, gain, lag)
    sums = sum_over(sums, "chan")
    args = (sums, mixed, gate_acts, out_grad, gain)
    mix_grad, gain_sums = mix_grad_of(full_width, *args)

    grad_near = [swapped(chunk) for chunk in mix_grad]
    back_band = bands(after(behind, mix_grad[0]))
    totals = kernel_grad_local(gain_sums, [value_acts], near, far, mix_grad, lag)
    grad_near[0], totals, back_band = lax.optimization_barrier((grad_near[0], totals, back_band))
    grad_far = [relayed(grad_near[0])]
    bits = list(range(count.bit_length() - 1))
    for step, bit in enumerate(bits[2:] + bits[:2]):
        if 2 <= step < CHUNKS:
            totals, *grad_far[:step] = lax.optimization_barrier((totals, *grad_far[:step]))
        totals += lax.ppermute(totals, "seq", [(i, i ^ (1 << bit)) for i in range(count)])
        if step < 2:
            grad_near[step + 1], totals = lax.optimization_barrier((grad_near[step + 1], totals))
            grad_far.append(relayed(grad_near[step + 1]))
    grad_far += [relayed(chunk) for chunk in grad_near[len(grad_far) :]]
    normed, gate_grad = norm(full_width, after(sums, grad_far[0]), *args[1:])
    grad_far[0], normed, gate_grad = lax.optimization_barrier((grad_far[0], normed, gate_grad))
    value_grad = value_grad_of(back_band, mix_grad, grad_near, grad_far, lag)
    tokens = rows * count
    kernel_grad = totals[:, : 2 * lag] / math.sqrt(tokens * HEAD)
    gain_grad = totals[:, 2 * lag : 2 * lag + HEAD].reshape(width) / math.sqrt(tokens)
    return (normed, gate_grad, value_grad, kernel_grad, gain_grad)


def solution(mesh):
    placed = (P("seq", "chan"), P("seq", "chan"), P("chan", None), P("chan"), P("seq", "chan"))
    return jax.shard_map(
        on_device,
        mesh=mesh,
        in_specs=placed,
        out_specs=(
            P("seq", "chan"),
            P("seq", "chan"),
            P("seq", "chan"),
            P("chan", None),
            P("chan"),
        ),
        check_vma=False,
    )
```

```python
import functools
import math

import jax
import jax.numpy as jnp
from jax import lax
from jax.experimental import pallas as pl
from jax.experimental.pallas import tpu as pltpu
from jax.sharding import PartitionSpec as P

norm_eps = 1e-06
TILE = 256
LANES = 128
HEAD = 64
CHUNKS = 4
MIB = 1 << 20


def params(mib):
    return pltpu.CompilerParams(
        vmem_limit_bytes=mib * MIB, dimension_semantics=("arbitrary",)
    )


def cost(flops, moved):
    return pl.CostEstimate(flops=flops, bytes_accessed=moved, transcendentals=0)


def lane_iota(rows):
    return lax.broadcasted_iota(jnp.int32, (rows, LANES), 1)


def slab(pair):
    return pl.ds(pl.multiple_of(pair * LANES, LANES), LANES)


def odd_device():
    return lax.axis_index("seq") % 2 == 1


def own_row(chunk):
    row = jnp.where(odd_device(), (CHUNKS - 1 - chunk) * TILE, chunk * TILE)
    return pl.multiple_of(row, TILE)


VMEM = pl.BlockSpec(memory_space=pltpu.VMEM)


def held(*arrays):
    return [pltpu.with_memory_space_constraint(array, pltpu.VMEM) for array in arrays]


def after(value, *others):
    return lax.optimization_barrier((value, *others))[0]


def band_body(row_ref, band_ref):
    tiles = row_ref.shape[2] // LANES
    step = pl.program_id(0)
    upper = lane_iota(LANES) >= lax.broadcasted_iota(jnp.int32, (LANES, LANES), 0)
    for half in range(2):
        head = 2 * step + half
        before = jnp.zeros((LANES, LANES), jnp.float32)
        band_ref[head, :, :LANES] = before.astype(band_ref.dtype)
        for tile in range(tiles):
            segment = row_ref[step, half : half + 1, tile * LANES : (tile + 1) * LANES]
            turned = pltpu.roll(
                jnp.broadcast_to(segment, (LANES, LANES)), 0, 1, stride=1, stride_axis=0
            )
            cell = jnp.where(upper, turned, before)
            band_ref[head, :, (tile + 1) * LANES : (tile + 2) * LANES] = cell.astype(
                band_ref.dtype
            )
            before = turned


def band_rows(taps, low, high):
    heads = taps.shape[0]
    return jnp.pad(taps, ((0, 0), (low, high))).reshape(heads // 2, 2, -1)


def bands(rows):
    heads, length = 2 * rows.shape[0], rows.shape[2]
    return pl.pallas_call(
        band_body,
        grid=(heads // 2,),
        in_specs=[VMEM],
        out_specs=VMEM,
        out_shape=pltpu.VMEM((heads, LANES, length + LANES), jnp.bfloat16),
        compiler_params=params(4),
        cost_estimate=cost(heads * LANES * length, 2 * heads * LANES * length),
        name="bands",
    )(*held(rows))


def natural(chunks):
    return [jnp.where(odd_device(), *pair) for pair in zip(chunks[::-1], chunks)]


def extended(own, near, far):
    if len(far) < CHUNKS:
        far = [*far, jnp.zeros_like(near[0])]
    odd = odd_device()
    left = [jnp.where(odd, n, f) for n, f in zip(near, far[::-1])]
    right = [jnp.where(odd, f, n) for n, f in zip(near[::-1], far)]
    return left + own + right


def at_pair(refs, pair):
    return [ref[:, slab(pair)] for ref in refs]


def rows_of(ref, pair):
    return [ref[at : at + TILE, slab(pair)] for at in range(0, ref.shape[0], TILE)]


def layout_scratch(rows, lag):
    wide = (rows + 2 * lag) // TILE * HEAD
    return [
        pltpu.VMEM((2, TILE, wide), jnp.bfloat16),
        pltpu.VMEM((2, TILE, wide - LANES), jnp.bfloat16),
    ]


def lay_out(blocks, even_ref, odd_ref):
    low = lane_iota(TILE) < HEAD
    turned = [pltpu.roll(block, HEAD, 1) for block in blocks]
    for tile in range(len(blocks) // 2):
        cols = slice(tile * LANES, (tile + 1) * LANES)
        first, second = 2 * tile, 2 * tile + 1
        even_ref[0, :, cols] = jnp.where(low, blocks[first], turned[second])
        even_ref[1, :, cols] = jnp.where(low, turned[first], blocks[second])
        if odd_ref is not None and second + 1 < len(blocks):
            odd_ref[0, :, cols] = jnp.where(low, blocks[second], turned[second + 1])
            odd_ref[1, :, cols] = jnp.where(low, turned[second], blocks[second + 1])


def window(even_ref, odd_ref, head, start, width):
    if start % 2 == 0:
        return even_ref[head, :, start * HEAD : start * HEAD + width]
    return odd_ref[head, :, (start - 1) * HEAD : (start - 1) * HEAD + width]


def band_product(band_ref, band_head, even_ref, odd_ref, head, slots, width):
    span = slots * TILE
    tile = jnp.concatenate(
        [band_ref[band_head, :, LANES : LANES + span], band_ref[band_head, :, :span]], axis=0
    )
    data = jnp.concatenate(
        [window(even_ref, odd_ref, head, slot, width) for slot in range(slots)], axis=0
    )
    return jnp.dot(tile, data, preferred_element_type=jnp.float32)


def token_blocks(first, second):
    low = lane_iota(TILE) < HEAD
    blocks = []
    for tile in range(first.shape[1] // LANES):
        cols = slice(tile * LANES, (tile + 1) * LANES)
        one, two = first[:, cols], second[:, cols]
        blocks.append(jnp.where(low, one, pltpu.roll(two, HEAD, 1)))
        blocks.append(jnp.where(low, pltpu.roll(one, HEAD, 1), two))
    return blocks


def last_term(band_ref, pair, last):
    low = lane_iota(TILE) < HEAD
    at = jnp.where(odd_device(), band_ref.shape[2] - LANES - TILE, 0)
    parts = []
    for half in range(2):
        head = 2 * pair + half
        tile = jnp.concatenate(
            [
                band_ref[head, :, pl.ds(pl.multiple_of(at + LANES, LANES), TILE)],
                band_ref[head, :, pl.ds(pl.multiple_of(at, LANES), TILE)],
            ],
            axis=0,
        )
        parts.append(jnp.dot(tile, last, preferred_element_type=jnp.float32))
    return jnp.where(low, *parts)


def split_body(value_ref, *refs):
    chunk_refs, sems = refs[:CHUNKS], refs[CHUNKS]
    copies = []
    for chunk, ref in enumerate(chunk_refs):
        copies.append(
            pltpu.make_async_copy(
                value_ref.at[pl.ds(own_row(chunk), TILE), :], ref, sems.at[chunk]
            )
        )
        copies[-1].start()
    for copy in copies:
        copy.wait()


def split(value):
    rows, width = value.shape
    return pl.pallas_call(
        split_body,
        in_specs=[pl.BlockSpec(memory_space=pltpu.HBM)],
        out_specs=[VMEM] * CHUNKS,
        out_shape=[pltpu.VMEM((TILE, width), value.dtype)] * CHUNKS,
        scratch_shapes=[pltpu.SemaphoreType.DMA((CHUNKS,))],
        compiler_params=pltpu.CompilerParams(vmem_limit_bytes=2 * MIB),
        cost_estimate=cost(0, 4 * rows * width),
        name="split",
    )(pltpu.with_memory_space_constraint(value, pltpu.HBM))


def product_flops(rows, width, lag):
    return 2 * (width // HEAD) * TILE * (TILE + 2 * lag) * rows // TILE * HEAD


def token_sums(square_ref, inner_ref, sums_ref, start):
    for at in range(0, square_ref.shape[0], LANES):
        rows = slice(at, at + LANES)
        cols = pl.ds(pl.multiple_of(start + at, LANES), LANES)
        sums_ref[0:1, cols] = jnp.sum(square_ref[rows, :].T, axis=0, keepdims=True)
        sums_ref[1:2, cols] = jnp.sum(inner_ref[rows, :].T, axis=0, keepdims=True)


def add_sums(mixed, gate, grad, gain, square_ref, inner_ref, at):
    hidden = gate.astype(jnp.float32) * mixed
    square_ref[at, :] += hidden * hidden
    inner_ref[at, :] += gain * grad.astype(jnp.float32) * hidden


def forward_body(slots, band_ref, own_ref, gate_ref, grad_ref, gain_ref, *refs):
    near_refs, far_refs, refs = refs[:CHUNKS], refs[CHUNKS : 2 * CHUNKS - 1], refs[2 * CHUNKS - 1 :]
    mixed_ref, sums_ref, even_ref, odd_ref, square_ref, inner_ref = refs
    pair = pl.program_id(0)

    @pl.when(pair == 0)
    def _():
        square_ref[...] = jnp.zeros_like(square_ref)
        inner_ref[...] = jnp.zeros_like(inner_ref)

    blocks = extended(rows_of(own_ref, pair), at_pair(near_refs, pair), at_pair(far_refs, pair))
    lay_out(blocks, even_ref, odd_ref)
    width = mixed_ref.shape[0] // TILE * HEAD
    results = [
        band_product(band_ref, 2 * pair + half, even_ref, odd_ref, half, slots, width)
        for half in range(2)
    ]
    lanes = slab(pair)
    for index, mixed in enumerate(token_blocks(*results)):
        at = slice(index * TILE, (index + 1) * TILE)
        mixed_ref[at, lanes] = mixed
        add_sums(
            mixed, gate_ref[at, lanes], grad_ref[at, lanes], gain_ref[:, lanes], square_ref, inner_ref, at
        )

    @pl.when(pair == pl.num_programs(0) - 1)
    def _():
        token_sums(square_ref, inner_ref, sums_ref, 0)


def forward(band, own, near, far, gate, grad, gain, lag):
    rows, width = gate.shape
    slots = 1 + 2 * lag // TILE
    operands = held(band, own, gate, grad, gain, *near, *far)
    return pl.pallas_call(
        functools.partial(forward_body, slots),
        grid=(width // LANES,),
        in_specs=[VMEM] * len(operands),
        out_specs=[VMEM] * 2,
        out_shape=[
            pltpu.VMEM((rows, width), jnp.float32),
            pltpu.VMEM((2, rows), jnp.float32),
        ],
        scratch_shapes=layout_scratch(rows, lag)
        + [pltpu.VMEM((rows, LANES), jnp.float32)] * 2,
        compiler_params=params(10),
        cost_estimate=cost(product_flops(rows, width, lag), 16 * rows * width),
        name="forward",
    )(*operands)


def forward_last_body(band_ref, last_ref, gate_ref, grad_ref, gain_ref, mixed_ref, sums_ref, *refs):
    first_ref, out_ref, square_ref, inner_ref = refs
    pair = pl.program_id(0)

    @pl.when(pair == 0)
    def _():
        square_ref[...] = jnp.zeros_like(square_ref)
        inner_ref[...] = jnp.zeros_like(inner_ref)
        out_ref[...] = sums_ref[...]

    lanes, rows = slab(pair), pl.ds(own_row(0), TILE)
    mixed = mixed_ref[rows, lanes] + last_term(band_ref, pair, last_ref[:, lanes])
    first_ref[:, lanes] = mixed
    add_sums(
        mixed,
        gate_ref[rows, lanes],
        grad_ref[rows, lanes],
        gain_ref[:, lanes],
        square_ref,
        inner_ref,
        slice(None),
    )

    @pl.when(pair == pl.num_programs(0) - 1)
    def _():
        token_sums(square_ref, inner_ref, out_ref, own_row(0))


def forward_last(band, last, gate, grad, gain, mixed, sums):
    rows, width = gate.shape
    operands = held(band, last, gate, grad, gain, mixed, sums)
    return pl.pallas_call(
        forward_last_body,
        grid=(width // LANES,),
        in_specs=[VMEM] * len(operands),
        out_specs=[VMEM] * 2,
        out_shape=[
            pltpu.VMEM((TILE, width), jnp.float32),
            pltpu.VMEM((2, rows), jnp.float32),
        ],
        scratch_shapes=[pltpu.VMEM((TILE, LANES), jnp.float32)] * 2,
        compiler_params=params(6),
        cost_estimate=cost(8 * TILE * TILE * width, 6 * TILE * width),
        name="forward_last",
    )(*operands)


def token_columns(full_width, sums_ref, tokens):
    scale = lax.rsqrt(sums_ref[0:1, tokens] / full_width + norm_eps)
    pull = scale * scale * sums_ref[1:2, tokens] / full_width
    return (
        jnp.broadcast_to(scale, (LANES, LANES)).T,
        jnp.broadcast_to(pull, (LANES, LANES)).T,
    )


def mix_grad_body(full_width, sums_ref, mixed_ref, first_ref, gate_ref, grad_ref, gain_ref, *refs):
    out_refs, gain_grad_ref, total_ref = refs[:-2], refs[-2], refs[-1]
    total_ref[...] = jnp.zeros_like(total_ref)
    for chunk, out_ref in enumerate(out_refs):
        for at in range(0, TILE, LANES):
            tokens = pl.ds(pl.multiple_of(own_row(chunk) + at, LANES), LANES)
            rows = slice(at, at + LANES)
            scale, pull = token_columns(full_width, sums_ref, tokens)
            for lane in range(0, mixed_ref.shape[1], LANES):
                cols = slice(lane, lane + LANES)
                gate = gate_ref[tokens, cols].astype(jnp.float32)
                grad = grad_ref[tokens, cols].astype(jnp.float32)
                mixed = mixed_ref[tokens, cols] if chunk else first_ref[rows, cols]
                hidden = gate * mixed
                hidden_grad = scale * (gain_ref[:, cols] * grad - hidden * pull)
                out_ref[rows, cols] = (hidden_grad * gate).astype(out_ref.dtype)
                total_ref[:, cols] += jnp.sum(
                    (grad * (hidden * scale)).reshape(LANES // 8, 8, LANES), axis=0
                )
    gain_grad_ref[...] = jnp.sum(total_ref[...], axis=0, keepdims=True)


def mix_grad_of(full_width, *operands):
    rows, width = operands[1].shape
    operands = held(*operands)
    *chunks, gain_sums = pl.pallas_call(
        functools.partial(mix_grad_body, full_width),
        in_specs=[VMEM] * len(operands),
        out_specs=[VMEM] * (CHUNKS + 1),
        out_shape=[pltpu.VMEM((TILE, width), jnp.bfloat16)] * CHUNKS
        + [pltpu.VMEM((1, width), jnp.float32)],
        scratch_shapes=[pltpu.VMEM((8, width), jnp.float32)],
        compiler_params=pltpu.CompilerParams(vmem_limit_bytes=4 * MIB),
        cost_estimate=cost(14 * rows * width, 10 * rows * width),
        name="mix_grad",
    )(*operands)
    return chunks, gain_sums


def norm_body(full_width, sums_ref, mixed_ref, first_ref, gate_ref, grad_ref, gain_ref, *refs):
    normed_ref, gate_grad_ref = refs
    start = pl.program_id(0) * LANES
    tokens = pl.ds(pl.multiple_of(start, LANES), LANES)
    within = pl.ds(pl.multiple_of(lax.rem(start, TILE), LANES), LANES)
    first = start // TILE == own_row(0) // TILE
    scale, pull = token_columns(full_width, sums_ref, tokens)
    for lane in range(0, mixed_ref.shape[1], LANES):
        cols = slice(lane, lane + LANES)
        gain = gain_ref[:, cols]
        gate = gate_ref[tokens, cols].astype(jnp.float32)
        mixed = jnp.where(first, first_ref[within, cols], mixed_ref[tokens, cols])
        grad = grad_ref[tokens, cols].astype(jnp.float32)
        hidden = gate * mixed
        normed_ref[:, cols] = (hidden * scale * gain).astype(normed_ref.dtype)
        hidden_grad = scale * (gain * grad - hidden * pull)
        gate_grad_ref[:, cols] = (hidden_grad * mixed).astype(gate_grad_ref.dtype)


def norm(full_width, *operands):
    rows, width = operands[1].shape
    operands = held(*operands)
    big = jax.ShapeDtypeStruct((rows, width), jnp.bfloat16)
    return pl.pallas_call(
        functools.partial(norm_body, full_width),
        grid=(rows // LANES,),
        in_specs=[VMEM] * len(operands),
        out_specs=[pl.BlockSpec((LANES, width), lambda g: (g, 0))] * 2,
        out_shape=[big, big],
        compiler_params=params(6),
        cost_estimate=cost(14 * rows * width, 12 * rows * width),
        name="norm",
    )(*operands)


def kernel_grad_body(slots, gain_ref, own_ref, *refs):
    near_refs, far_refs, refs = refs[:CHUNKS], refs[CHUNKS : 2 * CHUNKS], refs[2 * CHUNKS :]
    mix_refs, (out_ref, even_ref, odd_ref, mix_even_ref, cells_ref) = refs[:CHUNKS], refs[CHUNKS:]
    pair = pl.program_id(0)
    blocks = extended(rows_of(own_ref, pair), at_pair(near_refs, pair), at_pair(far_refs, pair))
    lay_out(blocks, even_ref, odd_ref)
    blocks = natural(at_pair(mix_refs, pair))
    lay_out(blocks, mix_even_ref, None)
    width = len(blocks) * HEAD
    span = cells_ref.shape[1]
    lags = span - LANES
    gains = gain_ref[:, slab(pair)]
    for half in range(2):
        mix = mix_even_ref[half]
        carry = None
        for lag_slot in range(slots):
            cross = lax.dot_general(
                window(even_ref, odd_ref, half, slots - 1 - lag_slot, width),
                mix,
                (((1,), (1,)), ((), ())),
                preferred_element_type=jnp.float32,
            )
            at = 2 * lag_slot * LANES
            upper, lower = cross[:LANES], cross[LANES:]
            if carry is not None:
                cells_ref[:, at - LANES : at] = carry + lower[:, :LANES]
            cells_ref[:, at : at + LANES] = upper[:, :LANES] + lower[:, LANES:]
            carry = upper[:, LANES:]
        total = cells_ref[0:8, :]
        for group in range(1, LANES // 8):
            total += pltpu.roll(cells_ref[8 * group : 8 * group + 8, :], span - 8 * group, 1)
        row = lax.broadcasted_iota(jnp.int32, (8, span), 0)
        for bit in (1, 2, 4):
            total = jnp.where((row & bit) != 0, pltpu.roll(total, span - bit, 1), total)
        sums = jnp.concatenate(
            [
                jnp.sum(total, axis=0, keepdims=True)[:, :lags],
                gains if half == 0 else pltpu.roll(gains, HEAD, 1),
            ],
            axis=1,
        )
        tall = min(8, out_ref.shape[0])
        row = 2 * pair + half
        group = pl.ds(pl.multiple_of(row // tall * tall, tall), tall)
        here = lax.broadcasted_iota(jnp.int32, (tall, out_ref.shape[1]), 0) == lax.rem(row, tall)
        out_ref[group, :] = jnp.where(here, sums, out_ref[group, :])


def kernel_grad_local(gain_sums, own, near, far, mix_grad, lag):
    rows, width = own.shape
    pairs = width // LANES
    slots = 1 + 2 * lag // TILE
    operands = held(gain_sums, own, *near, *far, *mix_grad)
    return pl.pallas_call(
        functools.partial(kernel_grad_body, slots),
        grid=(pairs,),
        in_specs=[VMEM] * len(operands),
        out_specs=VMEM,
        out_shape=pltpu.VMEM((2 * pairs, 2 * lag + LANES), jnp.float32),
        scratch_shapes=layout_scratch(rows, lag)
        + [
            pltpu.VMEM((2, TILE, rows // TILE * HEAD), jnp.bfloat16),
            pltpu.VMEM((LANES, 2 * lag + LANES), jnp.float32),
        ],
        compiler_params=params(10),
        cost_estimate=cost(product_flops(rows, width, lag), 8 * rows * width),
        name="kernel_grad",
    )(*operands)


def value_grad_body(slots, band_ref, *refs):
    own_refs, near_refs, refs = refs[:CHUNKS], refs[CHUNKS : 2 * CHUNKS], refs[2 * CHUNKS :]
    far_refs, (out_ref, first_ref, even_ref, odd_ref) = refs[: CHUNKS - 1], refs[CHUNKS - 1 :]
    pair = pl.program_id(0)
    own = natural(at_pair(own_refs, pair))
    blocks = extended(own, at_pair(near_refs, pair), at_pair(far_refs, pair))
    lay_out(blocks, even_ref, odd_ref)
    width = len(own) * HEAD
    results = [
        band_product(band_ref, 2 * pair + half, even_ref, odd_ref, half, slots, width)
        for half in range(2)
    ]
    blocks = token_blocks(*results)
    first_ref[:, slab(pair)] = jnp.where(odd_device(), blocks[-1], blocks[0])
    for index, block in enumerate(blocks):
        out_ref[index * TILE : (index + 1) * TILE, :] = block.astype(out_ref.dtype)


def value_grad_of(band, own, near, far, lag):
    rows, width = len(own) * TILE, own[0].shape[1]
    slots = 1 + 2 * lag // TILE
    operands = held(band, *own, *near, *far)
    return pl.pallas_call(
        functools.partial(value_grad_body, slots),
        grid=(width // LANES,),
        in_specs=[VMEM] * len(operands),
        out_specs=[pl.BlockSpec((rows, LANES), lambda g: (0, g)), VMEM],
        out_shape=[
            jax.ShapeDtypeStruct((rows, width), jnp.bfloat16),
            pltpu.VMEM((TILE, width), jnp.float32),
        ],
        scratch_shapes=layout_scratch(rows, lag),
        compiler_params=params(10),
        cost_estimate=cost(product_flops(rows, width, lag), 12 * rows * width),
        name="value_grad",
    )(*operands)


def value_grad_last_body(band_ref, last_ref, first_ref, rest_ref, out_ref, block_ref, sem):
    pair = pl.program_id(0)
    lanes = slab(pair)
    block = first_ref[:, lanes] + last_term(band_ref, pair, last_ref[:, lanes])
    block_ref[:, lanes] = block.astype(block_ref.dtype)

    @pl.when(pair == pl.num_programs(0) - 1)
    def _():
        copy = pltpu.make_async_copy(block_ref, out_ref.at[pl.ds(own_row(0), TILE), :], sem)
        copy.start()
        copy.wait()


def value_grad_last(band, last, first, rest):
    width = first.shape[1]
    operands = held(band, last, first)
    return pl.pallas_call(
        value_grad_last_body,
        grid=(width // LANES,),
        in_specs=[VMEM] * len(operands) + [pl.BlockSpec(memory_space=pl.ANY)],
        out_specs=pl.BlockSpec(memory_space=pl.ANY),
        out_shape=jax.ShapeDtypeStruct(rest.shape, rest.dtype),
        input_output_aliases={len(operands): 0},
        scratch_shapes=[pltpu.VMEM((TILE, width), jnp.bfloat16), pltpu.SemaphoreType.DMA(())],
        compiler_params=params(6),
        cost_estimate=cost(8 * TILE * TILE * width, 6 * TILE * width),
        name="value_grad_last",
    )(*operands, rest)


def swapped(chunk):
    count = lax.axis_size("seq")
    return lax.ppermute(chunk, "seq", [(i, i ^ 1) for i in range(count)])


def relayed(chunk):
    count = lax.axis_size("seq")
    pairs = [(i, i + 2) if i % 2 == 0 else (i, i - 2) for i in range(count)]
    return lax.ppermute(chunk, "seq", [(i, j) for i, j in pairs if 0 <= j < count])


def sum_over_bits(value, bits):
    count = lax.axis_size("seq")
    total = value
    for mask in range(1, 1 << len(bits)):
        flip = sum(1 << bit for at, bit in enumerate(bits) if mask >> at & 1)
        total += lax.ppermute(value, "seq", [(i, i ^ flip) for i in range(count)])
    return total


def sum_over(value, axis):
    count = lax.axis_size(axis)
    if count & (count - 1):
        return lax.psum(value, axis)
    for bit in range(count.bit_length() - 1):
        value += lax.ppermute(value, axis, [(i, i ^ (1 << bit)) for i in range(count)])
    return value


def on_device(gate_acts, value_acts, kernel, norm_gain, out_grad):
    rows, width = value_acts.shape
    heads = kernel.shape[0]
    lag = kernel.shape[1] // 2
    count = lax.axis_size("seq")
    assert width == heads * HEAD and rows == lag == CHUNKS * TILE
    assert count & (count - 1) == 0
    full_width = width * lax.axis_size("chan")
    gain = norm_gain.reshape(1, width)
    taps = kernel.astype(jnp.float32)

    ahead, behind = lax.optimization_barrier(
        (band_rows(taps[:, ::-1], 1, TILE - 1), band_rows(taps, 0, TILE))
    )
    band = bands(ahead)
    *chunks, last = split(value_acts)
    near = [swapped(chunk) for chunk in [*chunks, after(last, band)]]
    far = [relayed(chunk) for chunk in near]
    mixed, sums = forward(band, value_acts, near, far[:-1], gate_acts, out_grad, gain, lag)
    first, sums = forward_last(band, far[-1], gate_acts, out_grad, gain, mixed, sums)
    sums = sum_over(sums, "chan")
    args = (mixed, first, gate_acts, out_grad, gain)
    mix_grad, gain_sums = mix_grad_of(full_width, sums, *args)

    grad_near = [swapped(chunk) for chunk in mix_grad]
    totals = kernel_grad_local(gain_sums, value_acts, near, far, mix_grad, lag)
    bits = list(range(count.bit_length() - 1))
    grad_near[0], totals = lax.optimization_barrier((grad_near[0], totals))
    back_band = bands(after(behind, grad_near[0]))
    normed, gate_grad = norm(full_width, after(sums, grad_near[1]), *args)
    for bit in bits[2:]:
        totals = sum_over_bits(totals, [bit])
    grad_near[1], totals = lax.optimization_barrier((grad_near[1], totals))
    grad_far = [relayed(chunk) for chunk in grad_near]
    totals, *grad_far[:2] = lax.optimization_barrier((totals, *grad_far[:2]))
    totals = sum_over_bits(totals, bits[:2])
    grad_far[0], normed, gate_grad = lax.optimization_barrier((grad_far[0], normed, gate_grad))
    value_grad, first = value_grad_of(back_band, mix_grad, grad_near, grad_far[:-1], lag)
    value_grad = value_grad_last(back_band, grad_far[-1], first, value_grad)
    tokens = rows * count
    kernel_grad = totals[:, : 2 * lag] / math.sqrt(tokens * HEAD)
    gain_grad = totals[:, 2 * lag : 2 * lag + HEAD].reshape(width) / math.sqrt(tokens)
    return (normed, gate_grad, value_grad, kernel_grad, gain_grad)


def solution(mesh):
    placed = (P("seq", "chan"), P("seq", "chan"), P("chan", None), P("chan"), P("seq", "chan"))
    return jax.shard_map(
        on_device,
        mesh=mesh,
        in_specs=placed,
        out_specs=(
            P("seq", "chan"),
            P("seq", "chan"),
            P("seq", "chan"),
            P("chan", None),
            P("chan"),
        ),
        check_vma=False,
    )
```

```python
import functools
import math

import jax
import jax.numpy as jnp
from jax import lax
from jax.experimental import pallas as pl
from jax.experimental.pallas import tpu as pltpu
from jax.sharding import PartitionSpec as P

norm_eps = 1e-06
TILE = 256
LANES = 128
HEAD = 64
CHUNKS = 4
MIB = 1 << 20


def params(mib):
    return pltpu.CompilerParams(
        vmem_limit_bytes=mib * MIB, dimension_semantics=("arbitrary",)
    )


def cost(flops, moved):
    return pl.CostEstimate(flops=flops, bytes_accessed=moved, transcendentals=0)


def lane_iota(rows):
    return lax.broadcasted_iota(jnp.int32, (rows, LANES), 1)


def slab(pair):
    return pl.ds(pl.multiple_of(pair * LANES, LANES), LANES)


def odd_device():
    return lax.axis_index("seq") % 2 == 1


def own_row(chunk):
    row = jnp.where(odd_device(), (CHUNKS - 1 - chunk) * TILE, chunk * TILE)
    return pl.multiple_of(row, TILE)


VMEM = pl.BlockSpec(memory_space=pltpu.VMEM)


def held(*arrays):
    return [pltpu.with_memory_space_constraint(array, pltpu.VMEM) for array in arrays]


def after(value, *others):
    return lax.optimization_barrier((value, *others))[0]


def band_body(row_ref, band_ref):
    tiles = row_ref.shape[2] // LANES
    step = pl.program_id(0)
    upper = lane_iota(LANES) >= lax.broadcasted_iota(jnp.int32, (LANES, LANES), 0)
    for half in range(2):
        head = 2 * step + half
        before = jnp.zeros((LANES, LANES), jnp.float32)
        band_ref[head, :, :LANES] = before.astype(band_ref.dtype)
        for tile in range(tiles):
            segment = row_ref[step, half : half + 1, tile * LANES : (tile + 1) * LANES]
            turned = pltpu.roll(
                jnp.broadcast_to(segment, (LANES, LANES)), 0, 1, stride=1, stride_axis=0
            )
            cell = jnp.where(upper, turned, before)
            band_ref[head, :, (tile + 1) * LANES : (tile + 2) * LANES] = cell.astype(
                band_ref.dtype
            )
            before = turned


def band_rows(taps, low, high):
    heads = taps.shape[0]
    return jnp.pad(taps, ((0, 0), (low, high))).reshape(heads // 2, 2, -1)


def bands(rows):
    heads, length = 2 * rows.shape[0], rows.shape[2]
    return pl.pallas_call(
        band_body,
        grid=(heads // 2,),
        in_specs=[VMEM],
        out_specs=VMEM,
        out_shape=pltpu.VMEM((heads, LANES, length + LANES), jnp.bfloat16),
        compiler_params=params(4),
        cost_estimate=cost(heads * LANES * length, 2 * heads * LANES * length),
        name="bands",
    )(*held(rows))


def natural(chunks):
    return [jnp.where(odd_device(), *pair) for pair in zip(chunks[::-1], chunks)]


def extended(own, near, far):
    if len(far) < CHUNKS:
        far = [*far, jnp.zeros_like(near[0])]
    odd = odd_device()
    left = [jnp.where(odd, n, f) for n, f in zip(near, far[::-1])]
    right = [jnp.where(odd, f, n) for n, f in zip(near[::-1], far)]
    return left + own + right


def at_pair(refs, pair):
    return [ref[:, slab(pair)] for ref in refs]


def rows_of(ref, pair):
    return [ref[at : at + TILE, slab(pair)] for at in range(0, ref.shape[0], TILE)]


def layout_scratch(rows, lag):
    wide = (rows + 2 * lag) // TILE * HEAD
    return [
        pltpu.VMEM((2, TILE, wide), jnp.bfloat16),
        pltpu.VMEM((2, TILE, wide - LANES), jnp.bfloat16),
    ]


def lay_out(blocks, even_ref, odd_ref):
    low = lane_iota(TILE) < HEAD
    turned = [pltpu.roll(block, HEAD, 1) for block in blocks]
    for tile in range(len(blocks) // 2):
        cols = slice(tile * LANES, (tile + 1) * LANES)
        first, second = 2 * tile, 2 * tile + 1
        even_ref[0, :, cols] = jnp.where(low, blocks[first], turned[second])
        even_ref[1, :, cols] = jnp.where(low, turned[first], blocks[second])
        if odd_ref is not None and second + 1 < len(blocks):
            odd_ref[0, :, cols] = jnp.where(low, blocks[second], turned[second + 1])
            odd_ref[1, :, cols] = jnp.where(low, turned[second], blocks[second + 1])


def window(even_ref, odd_ref, head, start, width):
    if start % 2 == 0:
        return even_ref[head, :, start * HEAD : start * HEAD + width]
    return odd_ref[head, :, (start - 1) * HEAD : (start - 1) * HEAD + width]


def band_product(band_ref, band_head, even_ref, odd_ref, head, slots, width):
    span = slots * TILE
    tile = jnp.concatenate(
        [band_ref[band_head, :, LANES : LANES + span], band_ref[band_head, :, :span]], axis=0
    )
    data = jnp.concatenate(
        [window(even_ref, odd_ref, head, slot, width) for slot in range(slots)], axis=0
    )
    return jnp.dot(tile, data, preferred_element_type=jnp.float32)


def token_blocks(first, second):
    low = lane_iota(TILE) < HEAD
    blocks = []
    for tile in range(first.shape[1] // LANES):
        cols = slice(tile * LANES, (tile + 1) * LANES)
        one, two = first[:, cols], second[:, cols]
        blocks.append(jnp.where(low, one, pltpu.roll(two, HEAD, 1)))
        blocks.append(jnp.where(low, pltpu.roll(one, HEAD, 1), two))
    return blocks


def last_term(band_ref, pair, last):
    low = lane_iota(TILE) < HEAD
    at = jnp.where(odd_device(), band_ref.shape[2] - LANES - TILE, 0)
    parts = []
    for half in range(2):
        head = 2 * pair + half
        tile = jnp.concatenate(
            [
                band_ref[head, :, pl.ds(pl.multiple_of(at + LANES, LANES), TILE)],
                band_ref[head, :, pl.ds(pl.multiple_of(at, LANES), TILE)],
            ],
            axis=0,
        )
        parts.append(jnp.dot(tile, last, preferred_element_type=jnp.float32))
    return jnp.where(low, *parts)


def split_body(value_ref, *refs):
    chunk_refs, sems = refs[:CHUNKS], refs[CHUNKS]
    copies = []
    for chunk, ref in enumerate(chunk_refs):
        copies.append(
            pltpu.make_async_copy(
                value_ref.at[pl.ds(own_row(chunk), TILE), :], ref, sems.at[chunk]
            )
        )
        copies[-1].start()
    for copy in copies:
        copy.wait()


def split(value):
    rows, width = value.shape
    return pl.pallas_call(
        split_body,
        in_specs=[pl.BlockSpec(memory_space=pltpu.HBM)],
        out_specs=[VMEM] * CHUNKS,
        out_shape=[pltpu.VMEM((TILE, width), value.dtype)] * CHUNKS,
        scratch_shapes=[pltpu.SemaphoreType.DMA((CHUNKS,))],
        compiler_params=pltpu.CompilerParams(vmem_limit_bytes=2 * MIB),
        cost_estimate=cost(0, 4 * rows * width),
        name="split",
    )(pltpu.with_memory_space_constraint(value, pltpu.HBM))


def product_flops(rows, width, lag):
    return 2 * (width // HEAD) * TILE * (TILE + 2 * lag) * rows // TILE * HEAD


def token_sums(square_ref, inner_ref, sums_ref, start):
    for at in range(0, square_ref.shape[0], LANES):
        rows = slice(at, at + LANES)
        cols = pl.ds(pl.multiple_of(start + at, LANES), LANES)
        sums_ref[0:1, cols] = jnp.sum(square_ref[rows, :].T, axis=0, keepdims=True)
        sums_ref[1:2, cols] = jnp.sum(inner_ref[rows, :].T, axis=0, keepdims=True)


def add_sums(mixed, gate, grad, gain, square_ref, inner_ref, at):
    hidden = gate.astype(jnp.float32) * mixed
    square_ref[at, :] += hidden * hidden
    inner_ref[at, :] += gain * grad.astype(jnp.float32) * hidden


def forward_body(slots, band_ref, own_ref, gate_ref, grad_ref, gain_ref, *refs):
    near_refs, far_refs, refs = refs[:CHUNKS], refs[CHUNKS : 2 * CHUNKS - 1], refs[2 * CHUNKS - 1 :]
    mixed_ref, sums_ref, even_ref, odd_ref, square_ref, inner_ref = refs
    pair = pl.program_id(0)

    @pl.when(pair == 0)
    def _():
        square_ref[...] = jnp.zeros_like(square_ref)
        inner_ref[...] = jnp.zeros_like(inner_ref)

    blocks = extended(rows_of(own_ref, pair), at_pair(near_refs, pair), at_pair(far_refs, pair))
    lay_out(blocks, even_ref, odd_ref)
    width = mixed_ref.shape[0] // TILE * HEAD
    results = [
        band_product(band_ref, 2 * pair + half, even_ref, odd_ref, half, slots, width)
        for half in range(2)
    ]
    lanes = slab(pair)
    for index, mixed in enumerate(token_blocks(*results)):
        at = slice(index * TILE, (index + 1) * TILE)
        mixed_ref[at, lanes] = mixed
        add_sums(
            mixed, gate_ref[at, lanes], grad_ref[at, lanes], gain_ref[:, lanes], square_ref, inner_ref, at
        )

    @pl.when(pair == pl.num_programs(0) - 1)
    def _():
        token_sums(square_ref, inner_ref, sums_ref, 0)


def forward(band, own, near, far, gate, grad, gain, lag):
    rows, width = gate.shape
    slots = 1 + 2 * lag // TILE
    operands = held(band, own, gate, grad, gain, *near, *far)
    return pl.pallas_call(
        functools.partial(forward_body, slots),
        grid=(width // LANES,),
        in_specs=[VMEM] * len(operands),
        out_specs=[VMEM] * 2,
        out_shape=[
            pltpu.VMEM((rows, width), jnp.float32),
            pltpu.VMEM((2, rows), jnp.float32),
        ],
        scratch_shapes=layout_scratch(rows, lag)
        + [pltpu.VMEM((rows, LANES), jnp.float32)] * 2,
        compiler_params=params(10),
        cost_estimate=cost(product_flops(rows, width, lag), 16 * rows * width),
        name="forward",
    )(*operands)


def forward_last_body(band_ref, last_ref, gate_ref, grad_ref, gain_ref, mixed_ref, sums_ref, *refs):
    first_ref, out_ref, square_ref, inner_ref = refs
    pair = pl.program_id(0)

    @pl.when(pair == 0)
    def _():
        square_ref[...] = jnp.zeros_like(square_ref)
        inner_ref[...] = jnp.zeros_like(inner_ref)
        out_ref[...] = sums_ref[...]

    lanes, rows = slab(pair), pl.ds(own_row(0), TILE)
    mixed = mixed_ref[rows, lanes] + last_term(band_ref, pair, last_ref[:, lanes])
    first_ref[:, lanes] = mixed
    add_sums(
        mixed,
        gate_ref[rows, lanes],
        grad_ref[rows, lanes],
        gain_ref[:, lanes],
        square_ref,
        inner_ref,
        slice(None),
    )

    @pl.when(pair == pl.num_programs(0) - 1)
    def _():
        token_sums(square_ref, inner_ref, out_ref, own_row(0))


def forward_last(band, last, gate, grad, gain, mixed, sums):
    rows, width = gate.shape
    operands = held(band, last, gate, grad, gain, mixed, sums)
    return pl.pallas_call(
        forward_last_body,
        grid=(width // LANES,),
        in_specs=[VMEM] * len(operands),
        out_specs=[VMEM] * 2,
        out_shape=[
            pltpu.VMEM((TILE, width), jnp.float32),
            pltpu.VMEM((2, rows), jnp.float32),
        ],
        scratch_shapes=[pltpu.VMEM((TILE, LANES), jnp.float32)] * 2,
        compiler_params=params(6),
        cost_estimate=cost(8 * TILE * TILE * width, 6 * TILE * width),
        name="forward_last",
    )(*operands)


def token_columns(full_width, sums_ref, tokens):
    scale = lax.rsqrt(sums_ref[0:1, tokens] / full_width + norm_eps)
    pull = scale * scale * sums_ref[1:2, tokens] / full_width
    return (
        jnp.broadcast_to(scale, (LANES, LANES)).T,
        jnp.broadcast_to(pull, (LANES, LANES)).T,
    )


def mix_grad_body(full_width, sums_ref, mixed_ref, first_ref, gate_ref, grad_ref, gain_ref, *refs):
    out_refs, gain_grad_ref, total_ref = refs[:-2], refs[-2], refs[-1]
    total_ref[...] = jnp.zeros_like(total_ref)
    for chunk, out_ref in enumerate(out_refs):
        for at in range(0, TILE, LANES):
            tokens = pl.ds(pl.multiple_of(own_row(chunk) + at, LANES), LANES)
            rows = slice(at, at + LANES)
            scale, pull = token_columns(full_width, sums_ref, tokens)
            for lane in range(0, mixed_ref.shape[1], LANES):
                cols = slice(lane, lane + LANES)
                gate = gate_ref[tokens, cols].astype(jnp.float32)
                grad = grad_ref[tokens, cols].astype(jnp.float32)
                mixed = mixed_ref[tokens, cols] if chunk else first_ref[rows, cols]
                hidden = gate * mixed
                hidden_grad = scale * (gain_ref[:, cols] * grad - hidden * pull)
                out_ref[rows, cols] = (hidden_grad * gate).astype(out_ref.dtype)
                total_ref[:, cols] += jnp.sum(
                    (grad * (hidden * scale)).reshape(LANES // 8, 8, LANES), axis=0
                )
    gain_grad_ref[...] = jnp.sum(total_ref[...], axis=0, keepdims=True)


def mix_grad_of(full_width, *operands):
    rows, width = operands[1].shape
    operands = held(*operands)
    *chunks, gain_sums = pl.pallas_call(
        functools.partial(mix_grad_body, full_width),
        in_specs=[VMEM] * len(operands),
        out_specs=[VMEM] * (CHUNKS + 1),
        out_shape=[pltpu.VMEM((TILE, width), jnp.bfloat16)] * CHUNKS
        + [pltpu.VMEM((1, width), jnp.float32)],
        scratch_shapes=[pltpu.VMEM((8, width), jnp.float32)],
        compiler_params=pltpu.CompilerParams(vmem_limit_bytes=4 * MIB),
        cost_estimate=cost(14 * rows * width, 10 * rows * width),
        name="mix_grad",
    )(*operands)
    return chunks, gain_sums


def norm_body(full_width, sums_ref, mixed_ref, first_ref, gate_ref, grad_ref, gain_ref, *refs):
    normed_ref, gate_grad_ref = refs
    start = pl.program_id(0) * LANES
    tokens = pl.ds(pl.multiple_of(start, LANES), LANES)
    within = pl.ds(pl.multiple_of(lax.rem(start, TILE), LANES), LANES)
    first = start // TILE == own_row(0) // TILE
    scale, pull = token_columns(full_width, sums_ref, tokens)
    for lane in range(0, mixed_ref.shape[1], LANES):
        cols = slice(lane, lane + LANES)
        gain = gain_ref[:, cols]
        gate = gate_ref[tokens, cols].astype(jnp.float32)
        mixed = jnp.where(first, first_ref[within, cols], mixed_ref[tokens, cols])
        grad = grad_ref[tokens, cols].astype(jnp.float32)
        hidden = gate * mixed
        normed_ref[:, cols] = (hidden * scale * gain).astype(normed_ref.dtype)
        hidden_grad = scale * (gain * grad - hidden * pull)
        gate_grad_ref[:, cols] = (hidden_grad * mixed).astype(gate_grad_ref.dtype)


def norm(full_width, *operands):
    rows, width = operands[1].shape
    operands = held(*operands)
    big = jax.ShapeDtypeStruct((rows, width), jnp.bfloat16)
    return pl.pallas_call(
        functools.partial(norm_body, full_width),
        grid=(rows // LANES,),
        in_specs=[VMEM] * len(operands),
        out_specs=[pl.BlockSpec((LANES, width), lambda g: (g, 0))] * 2,
        out_shape=[big, big],
        compiler_params=params(6),
        cost_estimate=cost(14 * rows * width, 12 * rows * width),
        name="norm",
    )(*operands)


def kernel_grad_body(slots, gain_ref, own_ref, *refs):
    near_refs, far_refs, refs = refs[:CHUNKS], refs[CHUNKS : 2 * CHUNKS], refs[2 * CHUNKS :]
    mix_refs, (out_ref, even_ref, odd_ref, mix_even_ref, cells_ref) = refs[:CHUNKS], refs[CHUNKS:]
    pair = pl.program_id(0)
    blocks = extended(rows_of(own_ref, pair), at_pair(near_refs, pair), at_pair(far_refs, pair))
    lay_out(blocks, even_ref, odd_ref)
    blocks = natural(at_pair(mix_refs, pair))
    lay_out(blocks, mix_even_ref, None)
    width = len(blocks) * HEAD
    span = cells_ref.shape[1]
    lags = span - LANES
    gains = gain_ref[:, slab(pair)]
    for half in range(2):
        mix = mix_even_ref[half]
        carry = None
        for lag_slot in range(slots):
            cross = lax.dot_general(
                window(even_ref, odd_ref, half, slots - 1 - lag_slot, width),
                mix,
                (((1,), (1,)), ((), ())),
                preferred_element_type=jnp.float32,
            )
            at = 2 * lag_slot * LANES
            upper, lower = cross[:LANES], cross[LANES:]
            if carry is not None:
                cells_ref[:, at - LANES : at] = carry + lower[:, :LANES]
            cells_ref[:, at : at + LANES] = upper[:, :LANES] + lower[:, LANES:]
            carry = upper[:, LANES:]
        total = cells_ref[0:8, :]
        for group in range(1, LANES // 8):
            total += pltpu.roll(cells_ref[8 * group : 8 * group + 8, :], span - 8 * group, 1)
        row = lax.broadcasted_iota(jnp.int32, (8, span), 0)
        for bit in (1, 2, 4):
            total = jnp.where((row & bit) != 0, pltpu.roll(total, span - bit, 1), total)
        sums = jnp.concatenate(
            [
                jnp.sum(total, axis=0, keepdims=True)[:, :lags],
                gains if half == 0 else pltpu.roll(gains, HEAD, 1),
            ],
            axis=1,
        )
        tall = min(8, out_ref.shape[0])
        row = 2 * pair + half
        group = pl.ds(pl.multiple_of(row // tall * tall, tall), tall)
        here = lax.broadcasted_iota(jnp.int32, (tall, out_ref.shape[1]), 0) == lax.rem(row, tall)
        out_ref[group, :] = jnp.where(here, sums, out_ref[group, :])


def kernel_grad_local(gain_sums, own, near, far, mix_grad, lag):
    rows, width = own.shape
    pairs = width // LANES
    slots = 1 + 2 * lag // TILE
    operands = held(gain_sums, own, *near, *far, *mix_grad)
    return pl.pallas_call(
        functools.partial(kernel_grad_body, slots),
        grid=(pairs,),
        in_specs=[VMEM] * len(operands),
        out_specs=VMEM,
        out_shape=pltpu.VMEM((2 * pairs, 2 * lag + LANES), jnp.float32),
        scratch_shapes=layout_scratch(rows, lag)
        + [
            pltpu.VMEM((2, TILE, rows // TILE * HEAD), jnp.bfloat16),
            pltpu.VMEM((LANES, 2 * lag + LANES), jnp.float32),
        ],
        compiler_params=params(10),
        cost_estimate=cost(product_flops(rows, width, lag), 8 * rows * width),
        name="kernel_grad",
    )(*operands)


def value_grad_body(slots, band_ref, *refs):
    own_refs, near_refs, refs = refs[:CHUNKS], refs[CHUNKS : 2 * CHUNKS], refs[2 * CHUNKS :]
    far_refs, (out_ref, first_ref, even_ref, odd_ref) = refs[: CHUNKS - 1], refs[CHUNKS - 1 :]
    pair = pl.program_id(0)
    own = natural(at_pair(own_refs, pair))
    blocks = extended(own, at_pair(near_refs, pair), at_pair(far_refs, pair))
    lay_out(blocks, even_ref, odd_ref)
    width = len(own) * HEAD
    results = [
        band_product(band_ref, 2 * pair + half, even_ref, odd_ref, half, slots, width)
        for half in range(2)
    ]
    blocks = token_blocks(*results)
    first_ref[:, slab(pair)] = jnp.where(odd_device(), blocks[-1], blocks[0])
    for index, block in enumerate(blocks):
        out_ref[index * TILE : (index + 1) * TILE, :] = block.astype(out_ref.dtype)


def value_grad_of(band, own, near, far, lag):
    rows, width = len(own) * TILE, own[0].shape[1]
    slots = 1 + 2 * lag // TILE
    operands = held(band, *own, *near, *far)
    return pl.pallas_call(
        functools.partial(value_grad_body, slots),
        grid=(width // LANES,),
        in_specs=[VMEM] * len(operands),
        out_specs=[pl.BlockSpec((rows, LANES), lambda g: (0, g)), VMEM],
        out_shape=[
            jax.ShapeDtypeStruct((rows, width), jnp.bfloat16),
            pltpu.VMEM((TILE, width), jnp.float32),
        ],
        scratch_shapes=layout_scratch(rows, lag),
        compiler_params=params(10),
        cost_estimate=cost(product_flops(rows, width, lag), 12 * rows * width),
        name="value_grad",
    )(*operands)


def value_grad_last_body(band_ref, last_ref, first_ref, rest_ref, out_ref, block_ref, sem):
    pair = pl.program_id(0)
    lanes = slab(pair)
    block = first_ref[:, lanes] + last_term(band_ref, pair, last_ref[:, lanes])
    block_ref[:, lanes] = block.astype(block_ref.dtype)

    @pl.when(pair == pl.num_programs(0) - 1)
    def _():
        copy = pltpu.make_async_copy(block_ref, out_ref.at[pl.ds(own_row(0), TILE), :], sem)
        copy.start()
        copy.wait()


def value_grad_last(band, last, first, rest):
    width = first.shape[1]
    operands = held(band, last, first)
    return pl.pallas_call(
        value_grad_last_body,
        grid=(width // LANES,),
        in_specs=[VMEM] * len(operands) + [pl.BlockSpec(memory_space=pl.ANY)],
        out_specs=pl.BlockSpec(memory_space=pl.ANY),
        out_shape=jax.ShapeDtypeStruct(rest.shape, rest.dtype),
        input_output_aliases={len(operands): 0},
        scratch_shapes=[pltpu.VMEM((TILE, width), jnp.bfloat16), pltpu.SemaphoreType.DMA(())],
        compiler_params=params(6),
        cost_estimate=cost(8 * TILE * TILE * width, 6 * TILE * width),
        name="value_grad_last",
    )(*operands, rest)


def swapped(chunk):
    count = lax.axis_size("seq")
    return lax.ppermute(chunk, "seq", [(i, i ^ 1) for i in range(count)])


def relayed(chunk):
    count = lax.axis_size("seq")
    pairs = [(i, i + 2) if i % 2 == 0 else (i, i - 2) for i in range(count)]
    return lax.ppermute(chunk, "seq", [(i, j) for i, j in pairs if 0 <= j < count])


def terms_over_bits(value, bits):
    count = lax.axis_size("seq")
    terms = []
    for mask in range(1, 1 << len(bits)):
        flip = sum(1 << bit for at, bit in enumerate(bits) if mask >> at & 1)
        terms.append(lax.ppermute(value, "seq", [(i, i ^ flip) for i in range(count)]))
    return terms


def sum_over(value, axis):
    count = lax.axis_size(axis)
    if count & (count - 1):
        return lax.psum(value, axis)
    for bit in range(count.bit_length() - 1):
        value += lax.ppermute(value, axis, [(i, i ^ (1 << bit)) for i in range(count)])
    return value


def on_device(gate_acts, value_acts, kernel, norm_gain, out_grad):
    rows, width = value_acts.shape
    heads = kernel.shape[0]
    lag = kernel.shape[1] // 2
    count = lax.axis_size("seq")
    assert width == heads * HEAD and rows == lag == CHUNKS * TILE
    assert count & (count - 1) == 0
    full_width = width * lax.axis_size("chan")
    gain = norm_gain.reshape(1, width)
    taps = kernel.astype(jnp.float32)

    ahead, behind = lax.optimization_barrier(
        (band_rows(taps[:, ::-1], 1, TILE - 1), band_rows(taps, 0, TILE))
    )
    band = bands(ahead)
    *chunks, last = split(value_acts)
    near = [swapped(chunk) for chunk in [*chunks, after(last, band)]]
    far = [relayed(chunk) for chunk in near]
    mixed, sums = forward(band, value_acts, near, far[:-1], gate_acts, out_grad, gain, lag)
    first, sums = forward_last(band, far[-1], gate_acts, out_grad, gain, mixed, sums)
    sums = sum_over(sums, "chan")
    args = (mixed, first, gate_acts, out_grad, gain)
    mix_grad, gain_sums = mix_grad_of(full_width, sums, *args)

    grad_near = [swapped(part) for part in mix_grad]
    totals = kernel_grad_local(gain_sums, value_acts, near, far, mix_grad, lag)
    normed, gate_grad = norm(full_width, after(sums, grad_near[0]), *args)
    back_band = bands(after(behind, grad_near[1]))
    grad_near[0], totals = lax.optimization_barrier((grad_near[0], totals))
    grad_near[3], normed, gate_grad, back_band = lax.optimization_barrier(
        (grad_near[3], normed, gate_grad, back_band)
    )
    bits = list(range(count.bit_length() - 1))
    for bit in bits[2:]:
        totals += terms_over_bits(totals, [bit])[0]
        if bit == 2:
            grad_near[1], totals = lax.optimization_barrier((grad_near[1], totals))
    grad_far = [relayed(chunk) for chunk in grad_near]
    totals, *grad_far[:2] = lax.optimization_barrier((totals, *grad_far[:2]))
    terms = [totals] + terms_over_bits(totals, bits[:2])
    value_grad, first = value_grad_of(back_band, mix_grad, grad_near, grad_far[:-1], lag)
    value_grad = value_grad_last(back_band, grad_far[-1], first, value_grad)
    value_grad, *terms = lax.optimization_barrier((value_grad, *terms))
    totals = sum(terms[1:], terms[0])
    tokens = rows * count
    kernel_grad = totals[:, : 2 * lag] / math.sqrt(tokens * HEAD)
    gain_grad = totals[:, 2 * lag : 2 * lag + HEAD].reshape(width) / math.sqrt(tokens)
    return (normed, gate_grad, value_grad, kernel_grad, gain_grad)


def solution(mesh):
    placed = (P("seq", "chan"), P("seq", "chan"), P("chan", None), P("chan"), P("seq", "chan"))
    return jax.shard_map(
        on_device,
        mesh=mesh,
        in_specs=placed,
        out_specs=(
            P("seq", "chan"),
            P("seq", "chan"),
            P("seq", "chan"),
            P("chan", None),
            P("chan"),
        ),
        check_vma=False,
    )
```

```python
import functools
import math

import jax
import jax.numpy as jnp
from jax import lax
from jax.experimental import pallas as pl
from jax.experimental.pallas import tpu as pltpu
from jax.sharding import PartitionSpec as P

norm_eps = 1e-06
TILE = 256
LANES = 128
HEAD = 64
CHUNKS = 4
MIB = 1 << 20


def params(mib):
    return pltpu.CompilerParams(
        vmem_limit_bytes=mib * MIB, dimension_semantics=("arbitrary",)
    )


def cost(flops, moved):
    return pl.CostEstimate(flops=flops, bytes_accessed=moved, transcendentals=0)


def lane_iota(rows):
    return lax.broadcasted_iota(jnp.int32, (rows, LANES), 1)


def slab(pair):
    return pl.ds(pl.multiple_of(pair * LANES, LANES), LANES)


def odd_device():
    return lax.axis_index("seq") % 2 == 1


def own_row(chunk):
    row = jnp.where(odd_device(), (CHUNKS - 1 - chunk) * TILE, chunk * TILE)
    return pl.multiple_of(row, TILE)


VMEM = pl.BlockSpec(memory_space=pltpu.VMEM)


def held(*arrays):
    return [pltpu.with_memory_space_constraint(array, pltpu.VMEM) for array in arrays]


def after(value, *others):
    return lax.optimization_barrier((value, *others))[0]


def band_body(row_ref, band_ref):
    tiles = row_ref.shape[2] // LANES
    step = pl.program_id(0)
    upper = lane_iota(LANES) >= lax.broadcasted_iota(jnp.int32, (LANES, LANES), 0)
    for half in range(2):
        head = 2 * step + half
        before = jnp.zeros((LANES, LANES), jnp.float32)
        band_ref[head, :, :LANES] = before.astype(band_ref.dtype)
        for tile in range(tiles):
            segment = row_ref[step, half : half + 1, tile * LANES : (tile + 1) * LANES]
            turned = pltpu.roll(
                jnp.broadcast_to(segment, (LANES, LANES)), 0, 1, stride=1, stride_axis=0
            )
            cell = jnp.where(upper, turned, before)
            band_ref[head, :, (tile + 1) * LANES : (tile + 2) * LANES] = cell.astype(
                band_ref.dtype
            )
            before = turned


def band_rows(taps, low, high):
    heads = taps.shape[0]
    return jnp.pad(taps, ((0, 0), (low, high))).reshape(heads // 2, 2, -1)


def bands(rows):
    heads, length = 2 * rows.shape[0], rows.shape[2]
    return pl.pallas_call(
        band_body,
        grid=(heads // 2,),
        in_specs=[VMEM],
        out_specs=VMEM,
        out_shape=pltpu.VMEM((heads, LANES, length + LANES), jnp.bfloat16),
        compiler_params=params(4),
        cost_estimate=cost(heads * LANES * length, 2 * heads * LANES * length),
        name="bands",
    )(*held(rows))


def natural(chunks):
    return [jnp.where(odd_device(), *pair) for pair in zip(chunks[::-1], chunks)]


def extended(own, near, far):
    if len(far) < CHUNKS:
        far = [*far, jnp.zeros_like(near[0])]
    odd = odd_device()
    left = [jnp.where(odd, n, f) for n, f in zip(near, far[::-1])]
    right = [jnp.where(odd, f, n) for n, f in zip(near[::-1], far)]
    return left + own + right


def at_pair(refs, pair):
    return [ref[:, slab(pair)] for ref in refs]


def rows_of(ref, pair):
    return [ref[at : at + TILE, slab(pair)] for at in range(0, ref.shape[0], TILE)]


def layout_scratch(rows, lag):
    wide = (rows + 2 * lag) // TILE * HEAD
    return [
        pltpu.VMEM((2, TILE, wide), jnp.bfloat16),
        pltpu.VMEM((2, TILE, wide - LANES), jnp.bfloat16),
    ]


def lay_out(blocks, even_ref, odd_ref):
    low = lane_iota(TILE) < HEAD
    turned = [pltpu.roll(block, HEAD, 1) for block in blocks]
    for tile in range(len(blocks) // 2):
        cols = slice(tile * LANES, (tile + 1) * LANES)
        first, second = 2 * tile, 2 * tile + 1
        even_ref[0, :, cols] = jnp.where(low, blocks[first], turned[second])
        even_ref[1, :, cols] = jnp.where(low, turned[first], blocks[second])
        if odd_ref is not None and second + 1 < len(blocks):
            odd_ref[0, :, cols] = jnp.where(low, blocks[second], turned[second + 1])
            odd_ref[1, :, cols] = jnp.where(low, turned[second], blocks[second + 1])


def window(even_ref, odd_ref, head, start, width):
    if start % 2 == 0:
        return even_ref[head, :, start * HEAD : start * HEAD + width]
    return odd_ref[head, :, (start - 1) * HEAD : (start - 1) * HEAD + width]


def band_product(band_ref, band_head, even_ref, odd_ref, head, slots, width):
    span = slots * TILE
    tile = jnp.concatenate(
        [band_ref[band_head, :, LANES : LANES + span], band_ref[band_head, :, :span]], axis=0
    )
    data = jnp.concatenate(
        [window(even_ref, odd_ref, head, slot, width) for slot in range(slots)], axis=0
    )
    return jnp.dot(tile, data, preferred_element_type=jnp.float32)


def token_blocks(first, second):
    low = lane_iota(TILE) < HEAD
    blocks = []
    for tile in range(first.shape[1] // LANES):
        cols = slice(tile * LANES, (tile + 1) * LANES)
        one, two = first[:, cols], second[:, cols]
        blocks.append(jnp.where(low, one, pltpu.roll(two, HEAD, 1)))
        blocks.append(jnp.where(low, pltpu.roll(one, HEAD, 1), two))
    return blocks


def last_term(band_ref, pair, last):
    low = lane_iota(TILE) < HEAD
    at = jnp.where(odd_device(), band_ref.shape[2] - LANES - TILE, 0)
    parts = []
    for half in range(2):
        head = 2 * pair + half
        tile = jnp.concatenate(
            [
                band_ref[head, :, pl.ds(pl.multiple_of(at + LANES, LANES), TILE)],
                band_ref[head, :, pl.ds(pl.multiple_of(at, LANES), TILE)],
            ],
            axis=0,
        )
        parts.append(jnp.dot(tile, last, preferred_element_type=jnp.float32))
    return jnp.where(low, *parts)


def split_body(value_ref, *refs):
    chunk_refs, sems = refs[:CHUNKS], refs[CHUNKS]
    copies = []
    for chunk, ref in enumerate(chunk_refs):
        copies.append(
            pltpu.make_async_copy(
                value_ref.at[pl.ds(own_row(chunk), TILE), :], ref, sems.at[chunk]
            )
        )
        copies[-1].start()
    for copy in copies:
        copy.wait()


def split(value):
    rows, width = value.shape
    return pl.pallas_call(
        split_body,
        in_specs=[pl.BlockSpec(memory_space=pltpu.HBM)],
        out_specs=[VMEM] * CHUNKS,
        out_shape=[pltpu.VMEM((TILE, width), value.dtype)] * CHUNKS,
        scratch_shapes=[pltpu.SemaphoreType.DMA((CHUNKS,))],
        compiler_params=pltpu.CompilerParams(vmem_limit_bytes=2 * MIB),
        cost_estimate=cost(0, 4 * rows * width),
        name="split",
    )(pltpu.with_memory_space_constraint(value, pltpu.HBM))


def product_flops(rows, width, lag):
    return 2 * (width // HEAD) * TILE * (TILE + 2 * lag) * rows // TILE * HEAD


def token_sums(square_ref, inner_ref, sums_ref, start):
    for at in range(0, square_ref.shape[0], LANES):
        rows = slice(at, at + LANES)
        cols = pl.ds(pl.multiple_of(start + at, LANES), LANES)
        sums_ref[0:1, cols] = jnp.sum(square_ref[rows, :].T, axis=0, keepdims=True)
        sums_ref[1:2, cols] = jnp.sum(inner_ref[rows, :].T, axis=0, keepdims=True)


def add_sums(mixed, gate, grad, gain, square_ref, inner_ref, at):
    hidden = gate.astype(jnp.float32) * mixed
    square_ref[at, :] += hidden * hidden
    inner_ref[at, :] += gain * grad.astype(jnp.float32) * hidden


def forward_body(slots, band_ref, own_ref, gate_ref, grad_ref, gain_ref, *refs):
    near_refs, far_refs, refs = refs[:CHUNKS], refs[CHUNKS : 2 * CHUNKS - 1], refs[2 * CHUNKS - 1 :]
    mixed_ref, sums_ref, even_ref, odd_ref, square_ref, inner_ref = refs
    pair = pl.program_id(0)

    @pl.when(pair == 0)
    def _():
        square_ref[...] = jnp.zeros_like(square_ref)
        inner_ref[...] = jnp.zeros_like(inner_ref)

    blocks = extended(rows_of(own_ref, pair), at_pair(near_refs, pair), at_pair(far_refs, pair))
    lay_out(blocks, even_ref, odd_ref)
    width = mixed_ref.shape[0] // TILE * HEAD
    results = [
        band_product(band_ref, 2 * pair + half, even_ref, odd_ref, half, slots, width)
        for half in range(2)
    ]
    lanes = slab(pair)
    for index, mixed in enumerate(token_blocks(*results)):
        at = slice(index * TILE, (index + 1) * TILE)
        mixed_ref[at, lanes] = mixed
        add_sums(
            mixed, gate_ref[at, lanes], grad_ref[at, lanes], gain_ref[:, lanes], square_ref, inner_ref, at
        )

    @pl.when(pair == pl.num_programs(0) - 1)
    def _():
        token_sums(square_ref, inner_ref, sums_ref, 0)


def forward(band, own, near, far, gate, grad, gain, lag):
    rows, width = gate.shape
    slots = 1 + 2 * lag // TILE
    operands = held(band, own, gate, grad, gain, *near, *far)
    return pl.pallas_call(
        functools.partial(forward_body, slots),
        grid=(width // LANES,),
        in_specs=[VMEM] * len(operands),
        out_specs=[VMEM] * 2,
        out_shape=[
            pltpu.VMEM((rows, width), jnp.float32),
            pltpu.VMEM((2, rows), jnp.float32),
        ],
        scratch_shapes=layout_scratch(rows, lag)
        + [pltpu.VMEM((rows, LANES), jnp.float32)] * 2,
        compiler_params=params(10),
        cost_estimate=cost(product_flops(rows, width, lag), 16 * rows * width),
        name="forward",
    )(*operands)


def forward_last_body(band_ref, last_ref, gate_ref, grad_ref, gain_ref, mixed_ref, sums_ref, *refs):
    first_ref, out_ref, square_ref, inner_ref = refs
    pair = pl.program_id(0)

    @pl.when(pair == 0)
    def _():
        square_ref[...] = jnp.zeros_like(square_ref)
        inner_ref[...] = jnp.zeros_like(inner_ref)
        out_ref[...] = sums_ref[...]

    lanes, rows = slab(pair), pl.ds(own_row(0), TILE)
    mixed = mixed_ref[rows, lanes] + last_term(band_ref, pair, last_ref[:, lanes])
    first_ref[:, lanes] = mixed
    add_sums(
        mixed,
        gate_ref[rows, lanes],
        grad_ref[rows, lanes],
        gain_ref[:, lanes],
        square_ref,
        inner_ref,
        slice(None),
    )

    @pl.when(pair == pl.num_programs(0) - 1)
    def _():
        token_sums(square_ref, inner_ref, out_ref, own_row(0))


def forward_last(band, last, gate, grad, gain, mixed, sums):
    rows, width = gate.shape
    operands = held(band, last, gate, grad, gain, mixed, sums)
    return pl.pallas_call(
        forward_last_body,
        grid=(width // LANES,),
        in_specs=[VMEM] * len(operands),
        out_specs=[VMEM] * 2,
        out_shape=[
            pltpu.VMEM((TILE, width), jnp.float32),
            pltpu.VMEM((2, rows), jnp.float32),
        ],
        scratch_shapes=[pltpu.VMEM((TILE, LANES), jnp.float32)] * 2,
        compiler_params=params(6),
        cost_estimate=cost(8 * TILE * TILE * width, 6 * TILE * width),
        name="forward_last",
    )(*operands)


def token_columns(full_width, sums_ref, tokens):
    scale = lax.rsqrt(sums_ref[0:1, tokens] / full_width + norm_eps)
    pull = scale * scale * sums_ref[1:2, tokens] / full_width
    return (
        jnp.broadcast_to(scale, (LANES, LANES)).T,
        jnp.broadcast_to(pull, (LANES, LANES)).T,
    )


def mix_grad_body(full_width, sums_ref, mixed_ref, first_ref, gate_ref, grad_ref, gain_ref, *refs):
    out_refs, gain_grad_ref, total_ref = refs[:-2], refs[-2], refs[-1]
    total_ref[...] = jnp.zeros_like(total_ref)
    for chunk, out_ref in enumerate(out_refs):
        for at in range(0, TILE, LANES):
            tokens = pl.ds(pl.multiple_of(own_row(chunk) + at, LANES), LANES)
            rows = slice(at, at + LANES)
            scale, pull = token_columns(full_width, sums_ref, tokens)
            for lane in range(0, mixed_ref.shape[1], LANES):
                cols = slice(lane, lane + LANES)
                gate = gate_ref[tokens, cols].astype(jnp.float32)
                grad = grad_ref[tokens, cols].astype(jnp.float32)
                mixed = mixed_ref[tokens, cols] if chunk else first_ref[rows, cols]
                hidden = gate * mixed
                hidden_grad = scale * (gain_ref[:, cols] * grad - hidden * pull)
                out_ref[rows, cols] = (hidden_grad * gate).astype(out_ref.dtype)
                total_ref[:, cols] += jnp.sum(
                    (grad * (hidden * scale)).reshape(LANES // 8, 8, LANES), axis=0
                )
    gain_grad_ref[...] = jnp.sum(total_ref[...], axis=0, keepdims=True)


def mix_grad_of(full_width, *operands):
    rows, width = operands[1].shape
    operands = held(*operands)
    *chunks, gain_sums = pl.pallas_call(
        functools.partial(mix_grad_body, full_width),
        in_specs=[VMEM] * len(operands),
        out_specs=[VMEM] * (CHUNKS + 1),
        out_shape=[pltpu.VMEM((TILE, width), jnp.bfloat16)] * CHUNKS
        + [pltpu.VMEM((1, width), jnp.float32)],
        scratch_shapes=[pltpu.VMEM((8, width), jnp.float32)],
        compiler_params=pltpu.CompilerParams(vmem_limit_bytes=4 * MIB),
        cost_estimate=cost(14 * rows * width, 10 * rows * width),
        name="mix_grad",
    )(*operands)
    return chunks, gain_sums


def norm_body(full_width, sums_ref, mixed_ref, first_ref, gate_ref, grad_ref, gain_ref, *refs):
    normed_ref, gate_grad_ref = refs
    start = pl.program_id(0) * LANES
    tokens = pl.ds(pl.multiple_of(start, LANES), LANES)
    within = pl.ds(pl.multiple_of(lax.rem(start, TILE), LANES), LANES)
    first = start // TILE == own_row(0) // TILE
    scale, pull = token_columns(full_width, sums_ref, tokens)
    for lane in range(0, mixed_ref.shape[1], LANES):
        cols = slice(lane, lane + LANES)
        gain = gain_ref[:, cols]
        gate = gate_ref[tokens, cols].astype(jnp.float32)
        mixed = jnp.where(first, first_ref[within, cols], mixed_ref[tokens, cols])
        grad = grad_ref[tokens, cols].astype(jnp.float32)
        hidden = gate * mixed
        normed_ref[:, cols] = (hidden * scale * gain).astype(normed_ref.dtype)
        hidden_grad = scale * (gain * grad - hidden * pull)
        gate_grad_ref[:, cols] = (hidden_grad * mixed).astype(gate_grad_ref.dtype)


def norm(full_width, *operands):
    rows, width = operands[1].shape
    operands = held(*operands)
    big = jax.ShapeDtypeStruct((rows, width), jnp.bfloat16)
    return pl.pallas_call(
        functools.partial(norm_body, full_width),
        grid=(rows // LANES,),
        in_specs=[VMEM] * len(operands),
        out_specs=[pl.BlockSpec((LANES, width), lambda g: (g, 0))] * 2,
        out_shape=[big, big],
        compiler_params=params(6),
        cost_estimate=cost(14 * rows * width, 12 * rows * width),
        name="norm",
    )(*operands)


def kernel_grad_body(slots, gain_ref, own_ref, *refs):
    near_refs, far_refs, refs = refs[:CHUNKS], refs[CHUNKS : 2 * CHUNKS], refs[2 * CHUNKS :]
    mix_refs, (out_ref, even_ref, odd_ref, mix_even_ref, cells_ref) = refs[:CHUNKS], refs[CHUNKS:]
    pair = pl.program_id(0)
    blocks = extended(rows_of(own_ref, pair), at_pair(near_refs, pair), at_pair(far_refs, pair))
    lay_out(blocks, even_ref, odd_ref)
    blocks = natural(at_pair(mix_refs, pair))
    lay_out(blocks, mix_even_ref, None)
    width = len(blocks) * HEAD
    span = cells_ref.shape[1]
    lags = span - LANES
    gains = gain_ref[:, slab(pair)]
    for half in range(2):
        mix = mix_even_ref[half]
        carry = None
        for lag_slot in range(slots):
            cross = lax.dot_general(
                window(even_ref, odd_ref, half, slots - 1 - lag_slot, width),
                mix,
                (((1,), (1,)), ((), ())),
                preferred_element_type=jnp.float32,
            )
            at = 2 * lag_slot * LANES
            upper, lower = cross[:LANES], cross[LANES:]
            if carry is not None:
                cells_ref[:, at - LANES : at] = carry + lower[:, :LANES]
            cells_ref[:, at : at + LANES] = upper[:, :LANES] + lower[:, LANES:]
            carry = upper[:, LANES:]
        total = cells_ref[0:8, :]
        for group in range(1, LANES // 8):
            total += pltpu.roll(cells_ref[8 * group : 8 * group + 8, :], span - 8 * group, 1)
        row = lax.broadcasted_iota(jnp.int32, (8, span), 0)
        for bit in (1, 2, 4):
            total = jnp.where((row & bit) != 0, pltpu.roll(total, span - bit, 1), total)
        sums = jnp.concatenate(
            [
                jnp.sum(total, axis=0, keepdims=True)[:, :lags],
                gains if half == 0 else pltpu.roll(gains, HEAD, 1),
            ],
            axis=1,
        )
        tall = min(8, out_ref.shape[0])
        row = 2 * pair + half
        group = pl.ds(pl.multiple_of(row // tall * tall, tall), tall)
        here = lax.broadcasted_iota(jnp.int32, (tall, out_ref.shape[1]), 0) == lax.rem(row, tall)
        out_ref[group, :] = jnp.where(here, sums, out_ref[group, :])


def kernel_grad_local(gain_sums, own, near, far, mix_grad, lag):
    rows, width = own.shape
    pairs = width // LANES
    slots = 1 + 2 * lag // TILE
    operands = held(gain_sums, own, *near, *far, *mix_grad)
    return pl.pallas_call(
        functools.partial(kernel_grad_body, slots),
        grid=(pairs,),
        in_specs=[VMEM] * len(operands),
        out_specs=VMEM,
        out_shape=pltpu.VMEM((2 * pairs, 2 * lag + LANES), jnp.float32),
        scratch_shapes=layout_scratch(rows, lag)
        + [
            pltpu.VMEM((2, TILE, rows // TILE * HEAD), jnp.bfloat16),
            pltpu.VMEM((LANES, 2 * lag + LANES), jnp.float32),
        ],
        compiler_params=params(10),
        cost_estimate=cost(product_flops(rows, width, lag), 8 * rows * width),
        name="kernel_grad",
    )(*operands)


def value_grad_body(slots, band_ref, *refs):
    own_refs, near_refs, refs = refs[:CHUNKS], refs[CHUNKS : 2 * CHUNKS], refs[2 * CHUNKS :]
    far_refs, (out_ref, first_ref, even_ref, odd_ref) = refs[: CHUNKS - 1], refs[CHUNKS - 1 :]
    pair = pl.program_id(0)
    own = natural(at_pair(own_refs, pair))
    blocks = extended(own, at_pair(near_refs, pair), at_pair(far_refs, pair))
    lay_out(blocks, even_ref, odd_ref)
    width = len(own) * HEAD
    results = [
        band_product(band_ref, 2 * pair + half, even_ref, odd_ref, half, slots, width)
        for half in range(2)
    ]
    blocks = token_blocks(*results)
    first_ref[:, slab(pair)] = jnp.where(odd_device(), blocks[-1], blocks[0])
    for index, block in enumerate(blocks):
        out_ref[index * TILE : (index + 1) * TILE, :] = block.astype(out_ref.dtype)


def value_grad_of(band, own, near, far, lag):
    rows, width = len(own) * TILE, own[0].shape[1]
    slots = 1 + 2 * lag // TILE
    operands = held(band, *own, *near, *far)
    return pl.pallas_call(
        functools.partial(value_grad_body, slots),
        grid=(width // LANES,),
        in_specs=[VMEM] * len(operands),
        out_specs=[pl.BlockSpec((rows, LANES), lambda g: (0, g)), VMEM],
        out_shape=[
            jax.ShapeDtypeStruct((rows, width), jnp.bfloat16),
            pltpu.VMEM((TILE, width), jnp.float32),
        ],
        scratch_shapes=layout_scratch(rows, lag),
        compiler_params=params(10),
        cost_estimate=cost(product_flops(rows, width, lag), 12 * rows * width),
        name="value_grad",
    )(*operands)


def value_grad_last_body(band_ref, last_ref, first_ref, rest_ref, out_ref, block_ref, sem):
    pair = pl.program_id(0)
    lanes = slab(pair)
    block = first_ref[:, lanes] + last_term(band_ref, pair, last_ref[:, lanes])
    block_ref[:, lanes] = block.astype(block_ref.dtype)

    @pl.when(pair == pl.num_programs(0) - 1)
    def _():
        copy = pltpu.make_async_copy(block_ref, out_ref.at[pl.ds(own_row(0), TILE), :], sem)
        copy.start()
        copy.wait()


def value_grad_last(band, last, first, rest):
    width = first.shape[1]
    operands = held(band, last, first)
    return pl.pallas_call(
        value_grad_last_body,
        grid=(width // LANES,),
        in_specs=[VMEM] * len(operands) + [pl.BlockSpec(memory_space=pl.ANY)],
        out_specs=pl.BlockSpec(memory_space=pl.ANY),
        out_shape=jax.ShapeDtypeStruct(rest.shape, rest.dtype),
        input_output_aliases={len(operands): 0},
        scratch_shapes=[pltpu.VMEM((TILE, width), jnp.bfloat16), pltpu.SemaphoreType.DMA(())],
        compiler_params=params(6),
        cost_estimate=cost(8 * TILE * TILE * width, 6 * TILE * width),
        name="value_grad_last",
    )(*operands, rest)


def swapped(chunk):
    count = lax.axis_size("seq")
    return lax.ppermute(chunk, "seq", [(i, i ^ 1) for i in range(count)])


def relayed(chunk):
    count = lax.axis_size("seq")
    pairs = [(i, i + 2) if i % 2 == 0 else (i, i - 2) for i in range(count)]
    return lax.ppermute(chunk, "seq", [(i, j) for i, j in pairs if 0 <= j < count])


def terms_over_bits(value, bits):
    count = lax.axis_size("seq")
    terms = []
    for mask in range(1, 1 << len(bits)):
        flip = sum(1 << bit for at, bit in enumerate(bits) if mask >> at & 1)
        terms.append(lax.ppermute(value, "seq", [(i, i ^ flip) for i in range(count)]))
    return terms


def sum_over(value, axis):
    count = lax.axis_size(axis)
    if count & (count - 1):
        return lax.psum(value, axis)
    for bit in range(count.bit_length() - 1):
        value += lax.ppermute(value, axis, [(i, i ^ (1 << bit)) for i in range(count)])
    return value


def on_device(gate_acts, value_acts, kernel, norm_gain, out_grad):
    rows, width = value_acts.shape
    heads = kernel.shape[0]
    lag = kernel.shape[1] // 2
    count = lax.axis_size("seq")
    assert width == heads * HEAD and rows == lag == CHUNKS * TILE
    assert count & (count - 1) == 0
    full_width = width * lax.axis_size("chan")
    gain = norm_gain.reshape(1, width)
    taps = kernel.astype(jnp.float32)

    ahead, behind = lax.optimization_barrier(
        (band_rows(taps[:, ::-1], 1, TILE - 1), band_rows(taps, 0, TILE))
    )
    band = bands(ahead)
    *chunks, last = split(value_acts)
    near = [swapped(chunk) for chunk in [*chunks, after(last, band)]]
    far = [relayed(chunk) for chunk in near]
    mixed, sums = forward(band, value_acts, near, far[:-1], gate_acts, out_grad, gain, lag)
    first, sums = forward_last(band, far[-1], gate_acts, out_grad, gain, mixed, sums)
    sums = sum_over(sums, "chan")
    args = (mixed, first, gate_acts, out_grad, gain)
    mix_grad, gain_sums = mix_grad_of(full_width, sums, *args)

    grad_near = [swapped(part) for part in mix_grad]
    totals = kernel_grad_local(gain_sums, value_acts, near, far, mix_grad, lag)
    normed, gate_grad = norm(full_width, after(sums, grad_near[0]), *args)
    back_band = bands(after(behind, grad_near[1]))
    grad_near[0], totals = lax.optimization_barrier((grad_near[0], totals))
    grad_near[3], normed, gate_grad, back_band = lax.optimization_barrier(
        (grad_near[3], normed, gate_grad, back_band)
    )
    bits = list(range(count.bit_length() - 1))
    term = jnp.zeros_like(totals)
    for bit in bits[2:]:
        totals += term
        term = terms_over_bits(totals, [bit])[0]
        if bit == 2:
            totals += term
            term = jnp.zeros_like(totals)
            grad_near[1], totals = lax.optimization_barrier((grad_near[1], totals))
            grad_near[2], totals = lax.optimization_barrier((grad_near[2], totals))
    grad_far = [relayed(chunk) for chunk in grad_near]
    value_grad, first = value_grad_of(back_band, mix_grad, grad_near, grad_far[:-1], lag)
    totals, term, first = lax.optimization_barrier((totals, term, first))
    totals += term
    terms = [totals] + terms_over_bits(totals, bits[:2])
    value_grad = value_grad_last(back_band, grad_far[-1], first, value_grad)
    value_grad, *terms = lax.optimization_barrier((value_grad, *terms))
    totals = sum(terms[1:], terms[0])
    tokens = rows * count
    kernel_grad = totals[:, : 2 * lag] / math.sqrt(tokens * HEAD)
    gain_grad = totals[:, 2 * lag : 2 * lag + HEAD].reshape(width) / math.sqrt(tokens)
    return (normed, gate_grad, value_grad, kernel_grad, gain_grad)


def solution(mesh):
    placed = (P("seq", "chan"), P("seq", "chan"), P("chan", None), P("chan"), P("seq", "chan"))
    return jax.shard_map(
        on_device,
        mesh=mesh,
        in_specs=placed,
        out_specs=(
            P("seq", "chan"),
            P("seq", "chan"),
            P("seq", "chan"),
            P("chan", None),
            P("chan"),
        ),
        check_vma=False,
    )
```

```python
import functools
import math

import jax
import jax.numpy as jnp
from jax import lax
from jax.experimental import pallas as pl
from jax.experimental.pallas import tpu as pltpu
from jax.sharding import PartitionSpec as P

norm_eps = 1e-06
TILE = 256
LANES = 128
HEAD = 64
CHUNKS = 4
MIB = 1 << 20


def params(mib):
    return pltpu.CompilerParams(
        vmem_limit_bytes=mib * MIB, dimension_semantics=("arbitrary",)
    )


def cost(flops, moved):
    return pl.CostEstimate(flops=flops, bytes_accessed=moved, transcendentals=0)


def lane_iota(rows):
    return lax.broadcasted_iota(jnp.int32, (rows, LANES), 1)


def slab(pair):
    return pl.ds(pl.multiple_of(pair * LANES, LANES), LANES)


def odd_device():
    return lax.axis_index("seq") % 2 == 1


def own_row(chunk):
    row = jnp.where(odd_device(), (CHUNKS - 1 - chunk) * TILE, chunk * TILE)
    return pl.multiple_of(row, TILE)


VMEM = pl.BlockSpec(memory_space=pltpu.VMEM)


def held(*arrays):
    return [pltpu.with_memory_space_constraint(array, pltpu.VMEM) for array in arrays]


def after(value, *others):
    return lax.optimization_barrier((value, *others))[0]


def band_body(row_ref, band_ref):
    tiles = row_ref.shape[2] // LANES
    step = pl.program_id(0)
    upper = lane_iota(LANES) >= lax.broadcasted_iota(jnp.int32, (LANES, LANES), 0)
    for half in range(2):
        head = 2 * step + half
        before = jnp.zeros((LANES, LANES), jnp.float32)
        band_ref[head, :, :LANES] = before.astype(band_ref.dtype)
        for tile in range(tiles):
            segment = row_ref[step, half : half + 1, tile * LANES : (tile + 1) * LANES]
            turned = pltpu.roll(
                jnp.broadcast_to(segment, (LANES, LANES)), 0, 1, stride=1, stride_axis=0
            )
            cell = jnp.where(upper, turned, before)
            band_ref[head, :, (tile + 1) * LANES : (tile + 2) * LANES] = cell.astype(
                band_ref.dtype
            )
            before = turned


def band_rows(taps, low, high):
    heads = taps.shape[0]
    return jnp.pad(taps, ((0, 0), (low, high))).reshape(heads // 2, 2, -1)


def bands(rows):
    heads, length = 2 * rows.shape[0], rows.shape[2]
    return pl.pallas_call(
        band_body,
        grid=(heads // 2,),
        in_specs=[VMEM],
        out_specs=VMEM,
        out_shape=pltpu.VMEM((heads, LANES, length + LANES), jnp.bfloat16),
        compiler_params=params(4),
        cost_estimate=cost(heads * LANES * length, 2 * heads * LANES * length),
        name="bands",
    )(*held(rows))


def natural(chunks):
    return [jnp.where(odd_device(), *pair) for pair in zip(chunks[::-1], chunks)]


def extended(own, near, far):
    if len(far) < CHUNKS:
        far = [*far, jnp.zeros_like(near[0])]
    odd = odd_device()
    left = [jnp.where(odd, n, f) for n, f in zip(near, far[::-1])]
    right = [jnp.where(odd, f, n) for n, f in zip(near[::-1], far)]
    return left + own + right


def at_pair(refs, pair):
    return [ref[:, slab(pair)] for ref in refs]


def rows_of(ref, pair):
    return [ref[at : at + TILE, slab(pair)] for at in range(0, ref.shape[0], TILE)]


def layout_scratch(rows, lag):
    wide = (rows + 2 * lag) // TILE * HEAD
    return [
        pltpu.VMEM((2, TILE, wide), jnp.bfloat16),
        pltpu.VMEM((2, TILE, wide - LANES), jnp.bfloat16),
    ]


def lay_out(blocks, even_ref, odd_ref):
    low = lane_iota(TILE) < HEAD
    turned = [pltpu.roll(block, HEAD, 1) for block in blocks]
    for tile in range(len(blocks) // 2):
        cols = slice(tile * LANES, (tile + 1) * LANES)
        first, second = 2 * tile, 2 * tile + 1
        even_ref[0, :, cols] = jnp.where(low, blocks[first], turned[second])
        even_ref[1, :, cols] = jnp.where(low, turned[first], blocks[second])
        if odd_ref is not None and second + 1 < len(blocks):
            odd_ref[0, :, cols] = jnp.where(low, blocks[second], turned[second + 1])
            odd_ref[1, :, cols] = jnp.where(low, turned[second], blocks[second + 1])


def window(even_ref, odd_ref, head, start, width):
    if start % 2 == 0:
        return even_ref[head, :, start * HEAD : start * HEAD + width]
    return odd_ref[head, :, (start - 1) * HEAD : (start - 1) * HEAD + width]


def band_product(band_ref, band_head, even_ref, odd_ref, head, slots, width):
    span = slots * TILE
    tile = jnp.concatenate(
        [band_ref[band_head, :, LANES : LANES + span], band_ref[band_head, :, :span]], axis=0
    )
    data = jnp.concatenate(
        [window(even_ref, odd_ref, head, slot, width) for slot in range(slots)], axis=0
    )
    return jnp.dot(tile, data, preferred_element_type=jnp.float32)


def token_blocks(first, second):
    low = lane_iota(TILE) < HEAD
    blocks = []
    for tile in range(first.shape[1] // LANES):
        cols = slice(tile * LANES, (tile + 1) * LANES)
        one, two = first[:, cols], second[:, cols]
        blocks.append(jnp.where(low, one, pltpu.roll(two, HEAD, 1)))
        blocks.append(jnp.where(low, pltpu.roll(one, HEAD, 1), two))
    return blocks


def last_term(band_ref, pair, last):
    low = lane_iota(TILE) < HEAD
    at = jnp.where(odd_device(), band_ref.shape[2] - LANES - TILE, 0)
    parts = []
    for half in range(2):
        head = 2 * pair + half
        tile = jnp.concatenate(
            [
                band_ref[head, :, pl.ds(pl.multiple_of(at + LANES, LANES), TILE)],
                band_ref[head, :, pl.ds(pl.multiple_of(at, LANES), TILE)],
            ],
            axis=0,
        )
        parts.append(jnp.dot(tile, last, preferred_element_type=jnp.float32))
    return jnp.where(low, *parts)


def split_body(value_ref, *refs):
    chunk_refs, sems = refs[:CHUNKS], refs[CHUNKS]
    copies = []
    for chunk, ref in enumerate(chunk_refs):
        copies.append(
            pltpu.make_async_copy(
                value_ref.at[pl.ds(own_row(chunk), TILE), :], ref, sems.at[chunk]
            )
        )
        copies[-1].start()
    for copy in copies:
        copy.wait()


def split(value):
    rows, width = value.shape
    return pl.pallas_call(
        split_body,
        in_specs=[pl.BlockSpec(memory_space=pltpu.HBM)],
        out_specs=[VMEM] * CHUNKS,
        out_shape=[pltpu.VMEM((TILE, width), value.dtype)] * CHUNKS,
        scratch_shapes=[pltpu.SemaphoreType.DMA((CHUNKS,))],
        compiler_params=pltpu.CompilerParams(vmem_limit_bytes=2 * MIB),
        cost_estimate=cost(0, 4 * rows * width),
        name="split",
    )(pltpu.with_memory_space_constraint(value, pltpu.HBM))


def product_flops(rows, width, lag):
    return 2 * (width // HEAD) * TILE * (TILE + 2 * lag) * rows // TILE * HEAD


def token_sums(square_ref, inner_ref, sums_ref, start):
    for at in range(0, square_ref.shape[0], LANES):
        rows = slice(at, at + LANES)
        cols = pl.ds(pl.multiple_of(start + at, LANES), LANES)
        sums_ref[0:1, cols] = jnp.sum(square_ref[rows, :].T, axis=0, keepdims=True)
        sums_ref[1:2, cols] = jnp.sum(inner_ref[rows, :].T, axis=0, keepdims=True)


def add_sums(mixed, gate, grad, gain, square_ref, inner_ref, at):
    hidden = gate.astype(jnp.float32) * mixed
    square_ref[at, :] += hidden * hidden
    inner_ref[at, :] += gain * grad.astype(jnp.float32) * hidden


def forward_body(slots, band_ref, own_ref, gate_ref, grad_ref, gain_ref, *refs):
    near_refs, far_refs, refs = refs[:CHUNKS], refs[CHUNKS : 2 * CHUNKS - 1], refs[2 * CHUNKS - 1 :]
    mixed_ref, sums_ref, even_ref, odd_ref, square_ref, inner_ref = refs
    pair = pl.program_id(0)

    @pl.when(pair == 0)
    def _():
        square_ref[...] = jnp.zeros_like(square_ref)
        inner_ref[...] = jnp.zeros_like(inner_ref)

    blocks = extended(rows_of(own_ref, pair), at_pair(near_refs, pair), at_pair(far_refs, pair))
    lay_out(blocks, even_ref, odd_ref)
    width = mixed_ref.shape[0] // TILE * HEAD
    results = [
        band_product(band_ref, 2 * pair + half, even_ref, odd_ref, half, slots, width)
        for half in range(2)
    ]
    lanes = slab(pair)
    for index, mixed in enumerate(token_blocks(*results)):
        at = slice(index * TILE, (index + 1) * TILE)
        mixed_ref[at, lanes] = mixed
        add_sums(
            mixed, gate_ref[at, lanes], grad_ref[at, lanes], gain_ref[:, lanes], square_ref, inner_ref, at
        )

    @pl.when(pair == pl.num_programs(0) - 1)
    def _():
        token_sums(square_ref, inner_ref, sums_ref, 0)


def forward(band, own, near, far, gate, grad, gain, lag):
    rows, width = gate.shape
    slots = 1 + 2 * lag // TILE
    operands = held(band, own, gate, grad, gain, *near, *far)
    return pl.pallas_call(
        functools.partial(forward_body, slots),
        grid=(width // LANES,),
        in_specs=[VMEM] * len(operands),
        out_specs=[VMEM] * 2,
        out_shape=[
            pltpu.VMEM((rows, width), jnp.float32),
            pltpu.VMEM((2, rows), jnp.float32),
        ],
        scratch_shapes=layout_scratch(rows, lag)
        + [pltpu.VMEM((rows, LANES), jnp.float32)] * 2,
        compiler_params=params(10),
        cost_estimate=cost(product_flops(rows, width, lag), 16 * rows * width),
        name="forward",
    )(*operands)


def forward_last_body(band_ref, last_ref, gate_ref, grad_ref, gain_ref, mixed_ref, sums_ref, *refs):
    first_ref, out_ref, square_ref, inner_ref = refs
    pair = pl.program_id(0)

    @pl.when(pair == 0)
    def _():
        square_ref[...] = jnp.zeros_like(square_ref)
        inner_ref[...] = jnp.zeros_like(inner_ref)
        out_ref[...] = sums_ref[...]

    lanes, rows = slab(pair), pl.ds(own_row(0), TILE)
    mixed = mixed_ref[rows, lanes] + last_term(band_ref, pair, last_ref[:, lanes])
    first_ref[:, lanes] = mixed
    add_sums(
        mixed,
        gate_ref[rows, lanes],
        grad_ref[rows, lanes],
        gain_ref[:, lanes],
        square_ref,
        inner_ref,
        slice(None),
    )

    @pl.when(pair == pl.num_programs(0) - 1)
    def _():
        token_sums(square_ref, inner_ref, out_ref, own_row(0))


def forward_last(band, last, gate, grad, gain, mixed, sums):
    rows, width = gate.shape
    operands = held(band, last, gate, grad, gain, mixed, sums)
    return pl.pallas_call(
        forward_last_body,
        grid=(width // LANES,),
        in_specs=[VMEM] * len(operands),
        out_specs=[VMEM] * 2,
        out_shape=[
            pltpu.VMEM((TILE, width), jnp.float32),
            pltpu.VMEM((2, rows), jnp.float32),
        ],
        scratch_shapes=[pltpu.VMEM((TILE, LANES), jnp.float32)] * 2,
        compiler_params=params(6),
        cost_estimate=cost(8 * TILE * TILE * width, 6 * TILE * width),
        name="forward_last",
    )(*operands)


def token_columns(full_width, sums_ref, tokens):
    scale = lax.rsqrt(sums_ref[0:1, tokens] / full_width + norm_eps)
    pull = scale * scale * sums_ref[1:2, tokens] / full_width
    return (
        jnp.broadcast_to(scale, (LANES, LANES)).T,
        jnp.broadcast_to(pull, (LANES, LANES)).T,
    )


def mix_grad_body(full_width, sums_ref, mixed_ref, first_ref, gate_ref, grad_ref, gain_ref, *refs):
    out_refs, gain_grad_ref, total_ref = refs[:-2], refs[-2], refs[-1]
    total_ref[...] = jnp.zeros_like(total_ref)
    for chunk, out_ref in enumerate(out_refs):
        for at in range(0, TILE, LANES):
            tokens = pl.ds(pl.multiple_of(own_row(chunk) + at, LANES), LANES)
            rows = slice(at, at + LANES)
            scale, pull = token_columns(full_width, sums_ref, tokens)
            for lane in range(0, mixed_ref.shape[1], LANES):
                cols = slice(lane, lane + LANES)
                gate = gate_ref[tokens, cols].astype(jnp.float32)
                grad = grad_ref[tokens, cols].astype(jnp.float32)
                mixed = mixed_ref[tokens, cols] if chunk else first_ref[rows, cols]
                hidden = gate * mixed
                hidden_grad = scale * (gain_ref[:, cols] * grad - hidden * pull)
                out_ref[rows, cols] = (hidden_grad * gate).astype(out_ref.dtype)
                total_ref[:, cols] += jnp.sum(
                    (grad * (hidden * scale)).reshape(LANES // 8, 8, LANES), axis=0
                )
    gain_grad_ref[...] = jnp.sum(total_ref[...], axis=0, keepdims=True)


def mix_grad_of(full_width, *operands):
    rows, width = operands[1].shape
    operands = held(*operands)
    *chunks, gain_sums = pl.pallas_call(
        functools.partial(mix_grad_body, full_width),
        in_specs=[VMEM] * len(operands),
        out_specs=[VMEM] * (CHUNKS + 1),
        out_shape=[pltpu.VMEM((TILE, width), jnp.bfloat16)] * CHUNKS
        + [pltpu.VMEM((1, width), jnp.float32)],
        scratch_shapes=[pltpu.VMEM((8, width), jnp.float32)],
        compiler_params=pltpu.CompilerParams(vmem_limit_bytes=4 * MIB),
        cost_estimate=cost(14 * rows * width, 10 * rows * width),
        name="mix_grad",
    )(*operands)
    return chunks, gain_sums


def norm_body(full_width, sums_ref, mixed_ref, first_ref, gate_ref, grad_ref, gain_ref, *refs):
    normed_ref, gate_grad_ref = refs
    start = pl.program_id(0) * LANES
    tokens = pl.ds(pl.multiple_of(start, LANES), LANES)
    within = pl.ds(pl.multiple_of(lax.rem(start, TILE), LANES), LANES)
    first = start // TILE == own_row(0) // TILE
    scale, pull = token_columns(full_width, sums_ref, tokens)
    for lane in range(0, mixed_ref.shape[1], LANES):
        cols = slice(lane, lane + LANES)
        gain = gain_ref[:, cols]
        gate = gate_ref[tokens, cols].astype(jnp.float32)
        mixed = jnp.where(first, first_ref[within, cols], mixed_ref[tokens, cols])
        grad = grad_ref[tokens, cols].astype(jnp.float32)
        hidden = gate * mixed
        normed_ref[:, cols] = (hidden * scale * gain).astype(normed_ref.dtype)
        hidden_grad = scale * (gain * grad - hidden * pull)
        gate_grad_ref[:, cols] = (hidden_grad * mixed).astype(gate_grad_ref.dtype)


def norm(full_width, *operands):
    rows, width = operands[1].shape
    operands = held(*operands)
    big = jax.ShapeDtypeStruct((rows, width), jnp.bfloat16)
    return pl.pallas_call(
        functools.partial(norm_body, full_width),
        grid=(rows // LANES,),
        in_specs=[VMEM] * len(operands),
        out_specs=[pl.BlockSpec((LANES, width), lambda g: (g, 0))] * 2,
        out_shape=[big, big],
        compiler_params=params(6),
        cost_estimate=cost(14 * rows * width, 12 * rows * width),
        name="norm",
    )(*operands)


def kernel_grad_body(slots, gain_ref, own_ref, *refs):
    near_refs, far_refs, refs = refs[:CHUNKS], refs[CHUNKS : 2 * CHUNKS], refs[2 * CHUNKS :]
    mix_refs, (out_ref, even_ref, odd_ref, mix_even_ref, cells_ref) = refs[:CHUNKS], refs[CHUNKS:]
    pair = pl.program_id(0)
    blocks = extended(rows_of(own_ref, pair), at_pair(near_refs, pair), at_pair(far_refs, pair))
    lay_out(blocks, even_ref, odd_ref)
    blocks = natural(at_pair(mix_refs, pair))
    lay_out(blocks, mix_even_ref, None)
    width = len(blocks) * HEAD
    span = cells_ref.shape[1]
    lags = span - LANES
    gains = gain_ref[:, slab(pair)]
    for half in range(2):
        mix = mix_even_ref[half].T
        carry = None
        for lag_slot in range(slots):
            cross = jnp.dot(
                window(even_ref, odd_ref, half, slots - 1 - lag_slot, width),
                mix,
                preferred_element_type=jnp.float32,
            )
            at = 2 * lag_slot * LANES
            upper, lower = cross[:LANES], cross[LANES:]
            if carry is not None:
                cells_ref[:, at - LANES : at] = carry + lower[:, :LANES]
            cells_ref[:, at : at + LANES] = upper[:, :LANES] + lower[:, LANES:]
            carry = upper[:, LANES:]
        total = cells_ref[0:8, :]
        for group in range(1, LANES // 8):
            total += pltpu.roll(cells_ref[8 * group : 8 * group + 8, :], span - 8 * group, 1)
        row = lax.broadcasted_iota(jnp.int32, (8, span), 0)
        for bit in (1, 2, 4):
            total = jnp.where((row & bit) != 0, pltpu.roll(total, span - bit, 1), total)
        sums = jnp.concatenate(
            [
                jnp.sum(total, axis=0, keepdims=True)[:, :lags],
                gains if half == 0 else pltpu.roll(gains, HEAD, 1),
            ],
            axis=1,
        )
        tall = min(8, out_ref.shape[0])
        row = 2 * pair + half
        group = pl.ds(pl.multiple_of(row // tall * tall, tall), tall)
        here = lax.broadcasted_iota(jnp.int32, (tall, out_ref.shape[1]), 0) == lax.rem(row, tall)
        out_ref[group, :] = jnp.where(here, sums, out_ref[group, :])


def kernel_grad_local(gain_sums, own, near, far, mix_grad, lag):
    rows, width = own.shape
    pairs = width // LANES
    slots = 1 + 2 * lag // TILE
    operands = held(gain_sums, own, *near, *far, *mix_grad)
    return pl.pallas_call(
        functools.partial(kernel_grad_body, slots),
        grid=(pairs,),
        in_specs=[VMEM] * len(operands),
        out_specs=VMEM,
        out_shape=pltpu.VMEM((2 * pairs, 2 * lag + LANES), jnp.float32),
        scratch_shapes=layout_scratch(rows, lag)
        + [
            pltpu.VMEM((2, TILE, rows // TILE * HEAD), jnp.bfloat16),
            pltpu.VMEM((LANES, 2 * lag + LANES), jnp.float32),
        ],
        compiler_params=params(10),
        cost_estimate=cost(product_flops(rows, width, lag), 8 * rows * width),
        name="kernel_grad",
    )(*operands)


def value_grad_body(slots, band_ref, *refs):
    own_refs, near_refs, refs = refs[:CHUNKS], refs[CHUNKS : 2 * CHUNKS], refs[2 * CHUNKS :]
    far_refs, (out_ref, first_ref, even_ref, odd_ref) = refs[: CHUNKS - 1], refs[CHUNKS - 1 :]
    pair = pl.program_id(0)
    own = natural(at_pair(own_refs, pair))
    blocks = extended(own, at_pair(near_refs, pair), at_pair(far_refs, pair))
    lay_out(blocks, even_ref, odd_ref)
    width = len(own) * HEAD
    results = [
        band_product(band_ref, 2 * pair + half, even_ref, odd_ref, half, slots, width)
        for half in range(2)
    ]
    blocks = token_blocks(*results)
    first_ref[:, slab(pair)] = jnp.where(odd_device(), blocks[-1], blocks[0])
    for index, block in enumerate(blocks):
        out_ref[index * TILE : (index + 1) * TILE, :] = block.astype(out_ref.dtype)


def value_grad_of(band, own, near, far, lag):
    rows, width = len(own) * TILE, own[0].shape[1]
    slots = 1 + 2 * lag // TILE
    operands = held(band, *own, *near, *far)
    return pl.pallas_call(
        functools.partial(value_grad_body, slots),
        grid=(width // LANES,),
        in_specs=[VMEM] * len(operands),
        out_specs=[pl.BlockSpec((rows, LANES), lambda g: (0, g)), VMEM],
        out_shape=[
            jax.ShapeDtypeStruct((rows, width), jnp.bfloat16),
            pltpu.VMEM((TILE, width), jnp.float32),
        ],
        scratch_shapes=layout_scratch(rows, lag),
        compiler_params=params(10),
        cost_estimate=cost(product_flops(rows, width, lag), 12 * rows * width),
        name="value_grad",
    )(*operands)


def value_grad_last_body(band_ref, last_ref, first_ref, rest_ref, out_ref, block_ref, sem):
    pair = pl.program_id(0)
    lanes = slab(pair)
    block = first_ref[:, lanes] + last_term(band_ref, pair, last_ref[:, lanes])
    block_ref[:, lanes] = block.astype(block_ref.dtype)

    @pl.when(pair == pl.num_programs(0) - 1)
    def _():
        copy = pltpu.make_async_copy(block_ref, out_ref.at[pl.ds(own_row(0), TILE), :], sem)
        copy.start()
        copy.wait()


def value_grad_last(band, last, first, rest):
    width = first.shape[1]
    operands = held(band, last, first)
    return pl.pallas_call(
        value_grad_last_body,
        grid=(width // LANES,),
        in_specs=[VMEM] * len(operands) + [pl.BlockSpec(memory_space=pl.ANY)],
        out_specs=pl.BlockSpec(memory_space=pl.ANY),
        out_shape=jax.ShapeDtypeStruct(rest.shape, rest.dtype),
        input_output_aliases={len(operands): 0},
        scratch_shapes=[pltpu.VMEM((TILE, width), jnp.bfloat16), pltpu.SemaphoreType.DMA(())],
        compiler_params=params(6),
        cost_estimate=cost(8 * TILE * TILE * width, 6 * TILE * width),
        name="value_grad_last",
    )(*operands, rest)


def swapped(chunk):
    count = lax.axis_size("seq")
    return lax.ppermute(chunk, "seq", [(i, i ^ 1) for i in range(count)])


def relayed(chunk):
    count = lax.axis_size("seq")
    pairs = [(i, i + 2) if i % 2 == 0 else (i, i - 2) for i in range(count)]
    return lax.ppermute(chunk, "seq", [(i, j) for i, j in pairs if 0 <= j < count])


def terms_over_bits(value, bits):
    count = lax.axis_size("seq")
    terms = []
    for mask in range(1, 1 << len(bits)):
        flip = sum(1 << bit for at, bit in enumerate(bits) if mask >> at & 1)
        terms.append(lax.ppermute(value, "seq", [(i, i ^ flip) for i in range(count)]))
    return terms


def sum_over(value, axis):
    count = lax.axis_size(axis)
    if count & (count - 1):
        return lax.psum(value, axis)
    for bit in range(count.bit_length() - 1):
        value += lax.ppermute(value, axis, [(i, i ^ (1 << bit)) for i in range(count)])
    return value


def on_device(gate_acts, value_acts, kernel, norm_gain, out_grad):
    rows, width = value_acts.shape
    heads = kernel.shape[0]
    lag = kernel.shape[1] // 2
    count = lax.axis_size("seq")
    assert width == heads * HEAD and rows == lag == CHUNKS * TILE
    assert count & (count - 1) == 0
    full_width = width * lax.axis_size("chan")
    gain = norm_gain.reshape(1, width)
    taps = kernel.astype(jnp.float32)

    ahead, behind = lax.optimization_barrier(
        (band_rows(taps[:, ::-1], 1, TILE - 1), band_rows(taps, 0, TILE))
    )
    band = bands(ahead)
    *chunks, last = split(value_acts)
    near = [swapped(chunk) for chunk in [*chunks, after(last, band)]]
    far = [relayed(chunk) for chunk in near]
    mixed, sums = forward(band, value_acts, near, far[:-1], gate_acts, out_grad, gain, lag)
    first, sums = forward_last(band, far[-1], gate_acts, out_grad, gain, mixed, sums)
    sums = sum_over(sums, "chan")
    args = (mixed, first, gate_acts, out_grad, gain)
    mix_grad, gain_sums = mix_grad_of(full_width, sums, *args)

    grad_near = [swapped(part) for part in mix_grad]
    totals = kernel_grad_local(gain_sums, value_acts, near, far, mix_grad, lag)
    normed, gate_grad = norm(full_width, after(sums, grad_near[0]), *args)
    back_band = bands(after(behind, grad_near[1]))
    grad_near[0], totals = lax.optimization_barrier((grad_near[0], totals))
    grad_near[3], normed, gate_grad, back_band = lax.optimization_barrier(
        (grad_near[3], normed, gate_grad, back_band)
    )
    bits = list(range(count.bit_length() - 1))
    for bit in bits[2:]:
        totals += terms_over_bits(totals, [bit])[0]
    grad_near[1], totals = lax.optimization_barrier((grad_near[1], totals))
    grad_far = [relayed(chunk) for chunk in grad_near]
    totals, *grad_far[:2] = lax.optimization_barrier((totals, *grad_far[:2]))
    terms = [totals] + terms_over_bits(totals, bits[:2])
    value_grad, first = value_grad_of(back_band, mix_grad, grad_near, grad_far[:-1], lag)
    value_grad = value_grad_last(back_band, grad_far[-1], first, value_grad)
    value_grad, *terms = lax.optimization_barrier((value_grad, *terms))
    totals = sum(terms[1:], terms[0])
    tokens = rows * count
    kernel_grad = totals[:, : 2 * lag] / math.sqrt(tokens * HEAD)
    gain_grad = totals[:, 2 * lag : 2 * lag + HEAD].reshape(width) / math.sqrt(tokens)
    return (normed, gate_grad, value_grad, kernel_grad, gain_grad)


def solution(mesh):
    placed = (P("seq", "chan"), P("seq", "chan"), P("chan", None), P("chan"), P("seq", "chan"))
    return jax.shard_map(
        on_device,
        mesh=mesh,
        in_specs=placed,
        out_specs=(
            P("seq", "chan"),
            P("seq", "chan"),
            P("seq", "chan"),
            P("chan", None),
            P("chan"),
        ),
        check_vma=False,
    )
```

```python
import functools
import math

import jax
import jax.numpy as jnp
from jax import lax
from jax.experimental import pallas as pl
from jax.experimental.pallas import tpu as pltpu
from jax.sharding import PartitionSpec as P

norm_eps = 1e-06
TILE = 256
LANES = 128
HEAD = 64
CHUNKS = 4
MIB = 1 << 20


def params(mib):
    return pltpu.CompilerParams(
        vmem_limit_bytes=mib * MIB, dimension_semantics=("arbitrary",)
    )


def cost(flops, moved):
    return pl.CostEstimate(flops=flops, bytes_accessed=moved, transcendentals=0)


def lane_iota(rows):
    return lax.broadcasted_iota(jnp.int32, (rows, LANES), 1)


def slab(pair):
    return pl.ds(pl.multiple_of(pair * LANES, LANES), LANES)


def odd_device():
    return lax.axis_index("seq") % 2 == 1


def own_row(chunk):
    row = jnp.where(odd_device(), (CHUNKS - 1 - chunk) * TILE, chunk * TILE)
    return pl.multiple_of(row, TILE)


VMEM = pl.BlockSpec(memory_space=pltpu.VMEM)


def held(*arrays):
    return [pltpu.with_memory_space_constraint(array, pltpu.VMEM) for array in arrays]


def after(value, *others):
    return lax.optimization_barrier((value, *others))[0]


def band_body(row_ref, band_ref):
    tiles = row_ref.shape[2] // LANES
    step = pl.program_id(0)
    upper = lane_iota(LANES) >= lax.broadcasted_iota(jnp.int32, (LANES, LANES), 0)
    for half in range(2):
        head = 2 * step + half
        before = jnp.zeros((LANES, LANES), jnp.float32)
        band_ref[head, :, :LANES] = before.astype(band_ref.dtype)
        for tile in range(tiles):
            segment = row_ref[step, half : half + 1, tile * LANES : (tile + 1) * LANES]
            turned = pltpu.roll(
                jnp.broadcast_to(segment, (LANES, LANES)), 0, 1, stride=1, stride_axis=0
            )
            cell = jnp.where(upper, turned, before)
            band_ref[head, :, (tile + 1) * LANES : (tile + 2) * LANES] = cell.astype(
                band_ref.dtype
            )
            before = turned


def band_rows(taps, low, high):
    heads = taps.shape[0]
    return jnp.pad(taps, ((0, 0), (low, high))).reshape(heads // 2, 2, -1)


def bands(rows):
    heads, length = 2 * rows.shape[0], rows.shape[2]
    return pl.pallas_call(
        band_body,
        grid=(heads // 2,),
        in_specs=[VMEM],
        out_specs=VMEM,
        out_shape=pltpu.VMEM((heads, LANES, length + LANES), jnp.bfloat16),
        compiler_params=params(4),
        cost_estimate=cost(heads * LANES * length, 2 * heads * LANES * length),
        name="bands",
    )(*held(rows))


def natural(chunks):
    return [jnp.where(odd_device(), *pair) for pair in zip(chunks[::-1], chunks)]


def extended(own, near, far):
    if len(far) < CHUNKS:
        far = [*far, jnp.zeros_like(near[0])]
    odd = odd_device()
    left = [jnp.where(odd, n, f) for n, f in zip(near, far[::-1])]
    right = [jnp.where(odd, f, n) for n, f in zip(near[::-1], far)]
    return left + own + right


def at_pair(refs, pair):
    return [ref[:, slab(pair)] for ref in refs]


def rows_of(ref, pair):
    return [ref[at : at + TILE, slab(pair)] for at in range(0, ref.shape[0], TILE)]


def layout_scratch(rows, lag, heads=2):
    wide = (rows + 2 * lag) // TILE * HEAD
    return [
        pltpu.VMEM((heads, TILE, wide), jnp.bfloat16),
        pltpu.VMEM((heads, TILE, wide - LANES), jnp.bfloat16),
    ]


def lay_out(blocks, even_ref, odd_ref, base=0):
    low = lane_iota(TILE) < HEAD
    turned = [pltpu.roll(block, HEAD, 1) for block in blocks]
    for tile in range(len(blocks) // 2):
        cols = slice(tile * LANES, (tile + 1) * LANES)
        first, second = 2 * tile, 2 * tile + 1
        even_ref[base, :, cols] = jnp.where(low, blocks[first], turned[second])
        even_ref[base + 1, :, cols] = jnp.where(low, turned[first], blocks[second])
        if odd_ref is not None and second + 1 < len(blocks):
            odd_ref[base, :, cols] = jnp.where(low, blocks[second], turned[second + 1])
            odd_ref[base + 1, :, cols] = jnp.where(low, turned[second], blocks[second + 1])


def window(even_ref, odd_ref, head, start, width):
    if start % 2 == 0:
        return even_ref[head, :, start * HEAD : start * HEAD + width]
    return odd_ref[head, :, (start - 1) * HEAD : (start - 1) * HEAD + width]


def band_product(band_ref, band_head, even_ref, odd_ref, head, slots, width):
    span = slots * TILE
    tile = jnp.concatenate(
        [band_ref[band_head, :, LANES : LANES + span], band_ref[band_head, :, :span]], axis=0
    )
    data = jnp.concatenate(
        [window(even_ref, odd_ref, head, slot, width) for slot in range(slots)], axis=0
    )
    return jnp.dot(tile, data, preferred_element_type=jnp.float32)


def token_blocks(first, second):
    low = lane_iota(TILE) < HEAD
    blocks = []
    for tile in range(first.shape[1] // LANES):
        cols = slice(tile * LANES, (tile + 1) * LANES)
        one, two = first[:, cols], second[:, cols]
        blocks.append(jnp.where(low, one, pltpu.roll(two, HEAD, 1)))
        blocks.append(jnp.where(low, pltpu.roll(one, HEAD, 1), two))
    return blocks


def last_term(band_ref, pair, last):
    low = lane_iota(TILE) < HEAD
    at = jnp.where(odd_device(), band_ref.shape[2] - LANES - TILE, 0)
    parts = []
    for half in range(2):
        head = 2 * pair + half
        tile = jnp.concatenate(
            [
                band_ref[head, :, pl.ds(pl.multiple_of(at + LANES, LANES), TILE)],
                band_ref[head, :, pl.ds(pl.multiple_of(at, LANES), TILE)],
            ],
            axis=0,
        )
        parts.append(jnp.dot(tile, last, preferred_element_type=jnp.float32))
    return jnp.where(low, *parts)


def split_body(value_ref, *refs):
    chunk_refs, sems = refs[:CHUNKS], refs[CHUNKS]
    copies = []
    for chunk, ref in enumerate(chunk_refs):
        copies.append(
            pltpu.make_async_copy(
                value_ref.at[pl.ds(own_row(chunk), TILE), :], ref, sems.at[chunk]
            )
        )
        copies[-1].start()
    for copy in copies:
        copy.wait()


def split(value):
    rows, width = value.shape
    return pl.pallas_call(
        split_body,
        in_specs=[pl.BlockSpec(memory_space=pltpu.HBM)],
        out_specs=[VMEM] * CHUNKS,
        out_shape=[pltpu.VMEM((TILE, width), value.dtype)] * CHUNKS,
        scratch_shapes=[pltpu.SemaphoreType.DMA((CHUNKS,))],
        compiler_params=pltpu.CompilerParams(vmem_limit_bytes=2 * MIB),
        cost_estimate=cost(0, 4 * rows * width),
        name="split",
    )(pltpu.with_memory_space_constraint(value, pltpu.HBM))


def product_flops(rows, width, lag):
    return 2 * (width // HEAD) * TILE * (TILE + 2 * lag) * rows // TILE * HEAD


def token_sums(square_ref, inner_ref, sums_ref, start):
    for at in range(0, square_ref.shape[0], LANES):
        rows = slice(at, at + LANES)
        cols = pl.ds(pl.multiple_of(start + at, LANES), LANES)
        sums_ref[0:1, cols] = jnp.sum(square_ref[rows, :].T, axis=0, keepdims=True)
        sums_ref[1:2, cols] = jnp.sum(inner_ref[rows, :].T, axis=0, keepdims=True)


def add_sums(mixed, gate, grad, gain, square_ref, inner_ref, at):
    hidden = gate.astype(jnp.float32) * mixed
    square_ref[at, :] += hidden * hidden
    inner_ref[at, :] += gain * grad.astype(jnp.float32) * hidden


def forward_body(slots, band_ref, own_ref, gate_ref, grad_ref, gain_ref, *refs):
    near_refs, far_refs, refs = refs[:CHUNKS], refs[CHUNKS : 2 * CHUNKS - 1], refs[2 * CHUNKS - 1 :]
    mixed_ref, sums_ref, even_ref, odd_ref, square_ref, inner_ref = refs
    pair = pl.program_id(0)
    heads = (2 * pair, 2 * pair + 1)

    @pl.when(pair == 0)
    def _():
        square_ref[...] = jnp.zeros_like(square_ref)
        inner_ref[...] = jnp.zeros_like(inner_ref)

    blocks = extended(rows_of(own_ref, pair), at_pair(near_refs, pair), at_pair(far_refs, pair))
    lay_out(blocks, even_ref, odd_ref, 2 * pair)
    width = mixed_ref.shape[0] // TILE * HEAD
    results = [band_product(band_ref, h, even_ref, odd_ref, h, slots, width) for h in heads]
    lanes = slab(pair)
    for index, mixed in enumerate(token_blocks(*results)):
        at = slice(index * TILE, (index + 1) * TILE)
        mixed_ref[at, lanes] = mixed
        add_sums(
            mixed, gate_ref[at, lanes], grad_ref[at, lanes], gain_ref[:, lanes], square_ref, inner_ref, at
        )

    @pl.when(pair == pl.num_programs(0) - 1)
    def _():
        token_sums(square_ref, inner_ref, sums_ref, 0)


def forward(band, own, near, far, gate, grad, gain, lag):
    rows, width = gate.shape
    slots = 1 + 2 * lag // TILE
    operands = held(band, own, gate, grad, gain, *near, *far)
    return pl.pallas_call(
        functools.partial(forward_body, slots),
        grid=(width // LANES,),
        in_specs=[VMEM] * len(operands),
        out_specs=[VMEM] * 4,
        out_shape=[
            pltpu.VMEM((rows, width), jnp.float32),
            pltpu.VMEM((2, rows), jnp.float32),
            *layout_scratch(rows, lag, width // HEAD),
        ],
        scratch_shapes=[pltpu.VMEM((rows, LANES), jnp.float32)] * 2,
        compiler_params=params(9),
        cost_estimate=cost(product_flops(rows, width, lag), 16 * rows * width),
        name="forward",
    )(*operands)


def forward_last_body(band_ref, last_ref, gate_ref, grad_ref, gain_ref, mixed_ref, sums_ref, *refs):
    first_ref, out_ref, square_ref, inner_ref = refs
    pair = pl.program_id(0)

    @pl.when(pair == 0)
    def _():
        square_ref[...] = jnp.zeros_like(square_ref)
        inner_ref[...] = jnp.zeros_like(inner_ref)
        out_ref[...] = sums_ref[...]

    lanes, rows = slab(pair), pl.ds(own_row(0), TILE)
    mixed = mixed_ref[rows, lanes] + last_term(band_ref, pair, last_ref[:, lanes])
    first_ref[:, lanes] = mixed
    add_sums(
        mixed,
        gate_ref[rows, lanes],
        grad_ref[rows, lanes],
        gain_ref[:, lanes],
        square_ref,
        inner_ref,
        slice(None),
    )

    @pl.when(pair == pl.num_programs(0) - 1)
    def _():
        token_sums(square_ref, inner_ref, out_ref, own_row(0))


def forward_last(band, last, gate, grad, gain, mixed, sums):
    rows, width = gate.shape
    operands = held(band, last, gate, grad, gain, mixed, sums)
    return pl.pallas_call(
        forward_last_body,
        grid=(width // LANES,),
        in_specs=[VMEM] * len(operands),
        out_specs=[VMEM] * 2,
        out_shape=[
            pltpu.VMEM((TILE, width), jnp.float32),
            pltpu.VMEM((2, rows), jnp.float32),
        ],
        scratch_shapes=[pltpu.VMEM((TILE, LANES), jnp.float32)] * 2,
        compiler_params=params(6),
        cost_estimate=cost(8 * TILE * TILE * width, 6 * TILE * width),
        name="forward_last",
    )(*operands)


def token_columns(full_width, sums_ref, tokens):
    scale = lax.rsqrt(sums_ref[0:1, tokens] / full_width + norm_eps)
    pull = scale * scale * sums_ref[1:2, tokens] / full_width
    return (
        jnp.broadcast_to(scale, (LANES, LANES)).T,
        jnp.broadcast_to(pull, (LANES, LANES)).T,
    )


def mix_grad_body(full_width, sums_ref, mixed_ref, first_ref, gate_ref, grad_ref, gain_ref, *refs):
    out_refs, gain_grad_ref, total_ref = refs[:-2], refs[-2], refs[-1]
    total_ref[...] = jnp.zeros_like(total_ref)
    for chunk, out_ref in enumerate(out_refs):
        for at in range(0, TILE, LANES):
            tokens = pl.ds(pl.multiple_of(own_row(chunk) + at, LANES), LANES)
            rows = slice(at, at + LANES)
            scale, pull = token_columns(full_width, sums_ref, tokens)
            for lane in range(0, mixed_ref.shape[1], LANES):
                cols = slice(lane, lane + LANES)
                gate = gate_ref[tokens, cols].astype(jnp.float32)
                grad = grad_ref[tokens, cols].astype(jnp.float32)
                mixed = mixed_ref[tokens, cols] if chunk else first_ref[rows, cols]
                hidden = gate * mixed
                hidden_grad = scale * (gain_ref[:, cols] * grad - hidden * pull)
                out_ref[rows, cols] = (hidden_grad * gate).astype(out_ref.dtype)
                total_ref[:, cols] += jnp.sum(
                    (grad * (hidden * scale)).reshape(LANES // 8, 8, LANES), axis=0
                )
    gain_grad_ref[...] = jnp.sum(total_ref[...], axis=0, keepdims=True)


def mix_grad_of(full_width, *operands):
    rows, width = operands[1].shape
    operands = held(*operands)
    *chunks, gain_sums = pl.pallas_call(
        functools.partial(mix_grad_body, full_width),
        in_specs=[VMEM] * len(operands),
        out_specs=[VMEM] * (CHUNKS + 1),
        out_shape=[pltpu.VMEM((TILE, width), jnp.bfloat16)] * CHUNKS
        + [pltpu.VMEM((1, width), jnp.float32)],
        scratch_shapes=[pltpu.VMEM((8, width), jnp.float32)],
        compiler_params=pltpu.CompilerParams(vmem_limit_bytes=4 * MIB),
        cost_estimate=cost(14 * rows * width, 10 * rows * width),
        name="mix_grad",
    )(*operands)
    return chunks, gain_sums


def norm_body(full_width, sums_ref, mixed_ref, first_ref, gate_ref, grad_ref, gain_ref, *refs):
    normed_ref, gate_grad_ref = refs
    start = pl.program_id(0) * LANES
    tokens = pl.ds(pl.multiple_of(start, LANES), LANES)
    within = pl.ds(pl.multiple_of(lax.rem(start, TILE), LANES), LANES)
    first = start // TILE == own_row(0) // TILE
    scale, pull = token_columns(full_width, sums_ref, tokens)
    for lane in range(0, mixed_ref.shape[1], LANES):
        cols = slice(lane, lane + LANES)
        gain = gain_ref[:, cols]
        gate = gate_ref[tokens, cols].astype(jnp.float32)
        mixed = jnp.where(first, first_ref[within, cols], mixed_ref[tokens, cols])
        grad = grad_ref[tokens, cols].astype(jnp.float32)
        hidden = gate * mixed
        normed_ref[:, cols] = (hidden * scale * gain).astype(normed_ref.dtype)
        hidden_grad = scale * (gain * grad - hidden * pull)
        gate_grad_ref[:, cols] = (hidden_grad * mixed).astype(gate_grad_ref.dtype)


def norm(full_width, *operands):
    rows, width = operands[1].shape
    operands = held(*operands)
    big = jax.ShapeDtypeStruct((rows, width), jnp.bfloat16)
    return pl.pallas_call(
        functools.partial(norm_body, full_width),
        grid=(rows // LANES,),
        in_specs=[VMEM] * len(operands),
        out_specs=[pl.BlockSpec((LANES, width), lambda g: (g, 0))] * 2,
        out_shape=[big, big],
        compiler_params=params(6),
        cost_estimate=cost(14 * rows * width, 12 * rows * width),
        name="norm",
    )(*operands)


def patched(even_ref, head, half, slot, slots, width, last):
    data = even_ref[head, :, slot * HEAD : slot * HEAD + width]
    low = lane_iota(TILE) < HEAD
    turned = pltpu.roll(last, HEAD, 1)
    if slot == 0:
        tile = data[:, :LANES]
        put = jnp.where(low, last if half == 0 else turned, tile)
        return jnp.concatenate([jnp.where(odd_device(), tile, put), data[:, LANES:]], axis=1)
    if slot == slots - 1:
        tile = data[:, width - LANES :]
        put = jnp.where(low, tile, turned if half == 0 else last)
        return jnp.concatenate([data[:, : width - LANES], jnp.where(odd_device(), put, tile)], axis=1)
    return data


def kernel_grad_body(slots, gain_ref, even_ref, odd_ref, last_ref, *refs):
    mix_refs, (out_ref, mix_even_ref, cells_ref) = refs[:CHUNKS], refs[CHUNKS:]
    pair = pl.program_id(0)
    last = last_ref[:, slab(pair)]
    blocks = natural(at_pair(mix_refs, pair))
    lay_out(blocks, mix_even_ref, None)
    width = len(blocks) * HEAD
    span = cells_ref.shape[1]
    lags = span - LANES
    gains = gain_ref[:, slab(pair)]
    for half in range(2):
        mix = mix_even_ref[half].T
        carry = None
        for lag_slot in range(slots):
            slot, head = slots - 1 - lag_slot, 2 * pair + half
            if slot % 2 == 0:
                data = patched(even_ref, head, half, slot, slots, width, last)
            else:
                data = window(even_ref, odd_ref, head, slot, width)
            cross = jnp.dot(data, mix, preferred_element_type=jnp.float32)
            at = 2 * lag_slot * LANES
            upper, lower = cross[:LANES], cross[LANES:]
            if carry is not None:
                cells_ref[:, at - LANES : at] = carry + lower[:, :LANES]
            cells_ref[:, at : at + LANES] = upper[:, :LANES] + lower[:, LANES:]
            carry = upper[:, LANES:]
        total = cells_ref[0:8, :]
        for group in range(1, LANES // 8):
            total += pltpu.roll(cells_ref[8 * group : 8 * group + 8, :], span - 8 * group, 1)
        row = lax.broadcasted_iota(jnp.int32, (8, span), 0)
        for bit in (1, 2, 4):
            total = jnp.where((row & bit) != 0, pltpu.roll(total, span - bit, 1), total)
        sums = jnp.concatenate(
            [
                jnp.sum(total, axis=0, keepdims=True)[:, :lags],
                gains if half == 0 else pltpu.roll(gains, HEAD, 1),
            ],
            axis=1,
        )
        tall = min(8, out_ref.shape[0])
        row = 2 * pair + half
        group = pl.ds(pl.multiple_of(row // tall * tall, tall), tall)
        here = lax.broadcasted_iota(jnp.int32, (tall, out_ref.shape[1]), 0) == lax.rem(row, tall)
        out_ref[group, :] = jnp.where(here, sums, out_ref[group, :])


def kernel_grad_local(gain_sums, even, odd, last, mix_grad, lag):
    rows, width = len(mix_grad) * TILE, last.shape[1]
    pairs = width // LANES
    slots = 1 + 2 * lag // TILE
    operands = held(gain_sums, even, odd, last, *mix_grad)
    return pl.pallas_call(
        functools.partial(kernel_grad_body, slots),
        grid=(pairs,),
        in_specs=[VMEM] * len(operands),
        out_specs=VMEM,
        out_shape=pltpu.VMEM((2 * pairs, 2 * lag + LANES), jnp.float32),
        scratch_shapes=[
            pltpu.VMEM((2, TILE, rows // TILE * HEAD), jnp.bfloat16),
            pltpu.VMEM((LANES, 2 * lag + LANES), jnp.float32),
        ],
        compiler_params=params(8),
        cost_estimate=cost(product_flops(rows, width, lag), 8 * rows * width),
        name="kernel_grad",
    )(*operands)


def value_grad_body(slots, band_ref, *refs):
    own_refs, near_refs, refs = refs[:CHUNKS], refs[CHUNKS : 2 * CHUNKS], refs[2 * CHUNKS :]
    far_refs, (out_ref, first_ref, even_ref, odd_ref) = refs[: CHUNKS - 1], refs[CHUNKS - 1 :]
    pair = pl.program_id(0)
    own = natural(at_pair(own_refs, pair))
    blocks = extended(own, at_pair(near_refs, pair), at_pair(far_refs, pair))
    lay_out(blocks, even_ref, odd_ref)
    width = len(own) * HEAD
    results = [
        band_product(band_ref, 2 * pair + half, even_ref, odd_ref, half, slots, width)
        for half in range(2)
    ]
    blocks = token_blocks(*results)
    first_ref[:, slab(pair)] = jnp.where(odd_device(), blocks[-1], blocks[0])
    for index, block in enumerate(blocks):
        out_ref[index * TILE : (index + 1) * TILE, :] = block.astype(out_ref.dtype)


def value_grad_of(band, own, near, far, lag):
    rows, width = len(own) * TILE, own[0].shape[1]
    slots = 1 + 2 * lag // TILE
    operands = held(band, *own, *near, *far)
    return pl.pallas_call(
        functools.partial(value_grad_body, slots),
        grid=(width // LANES,),
        in_specs=[VMEM] * len(operands),
        out_specs=[pl.BlockSpec((rows, LANES), lambda g: (0, g)), VMEM],
        out_shape=[
            jax.ShapeDtypeStruct((rows, width), jnp.bfloat16),
            pltpu.VMEM((TILE, width), jnp.float32),
        ],
        scratch_shapes=layout_scratch(rows, lag),
        compiler_params=params(10),
        cost_estimate=cost(product_flops(rows, width, lag), 12 * rows * width),
        name="value_grad",
    )(*operands)


def value_grad_last_body(band_ref, last_ref, first_ref, rest_ref, out_ref, block_ref, sem):
    pair = pl.program_id(0)
    lanes = slab(pair)
    block = first_ref[:, lanes] + last_term(band_ref, pair, last_ref[:, lanes])
    block_ref[:, lanes] = block.astype(block_ref.dtype)

    @pl.when(pair == pl.num_programs(0) - 1)
    def _():
        copy = pltpu.make_async_copy(block_ref, out_ref.at[pl.ds(own_row(0), TILE), :], sem)
        copy.start()
        copy.wait()


def value_grad_last(band, last, first, rest):
    width = first.shape[1]
    operands = held(band, last, first)
    return pl.pallas_call(
        value_grad_last_body,
        grid=(width // LANES,),
        in_specs=[VMEM] * len(operands) + [pl.BlockSpec(memory_space=pl.ANY)],
        out_specs=pl.BlockSpec(memory_space=pl.ANY),
        out_shape=jax.ShapeDtypeStruct(rest.shape, rest.dtype),
        input_output_aliases={len(operands): 0},
        scratch_shapes=[pltpu.VMEM((TILE, width), jnp.bfloat16), pltpu.SemaphoreType.DMA(())],
        compiler_params=params(6),
        cost_estimate=cost(8 * TILE * TILE * width, 6 * TILE * width),
        name="value_grad_last",
    )(*operands, rest)


def swapped(chunk):
    count = lax.axis_size("seq")
    return lax.ppermute(chunk, "seq", [(i, i ^ 1) for i in range(count)])


def relayed(chunk):
    count = lax.axis_size("seq")
    pairs = [(i, i + 2) if i % 2 == 0 else (i, i - 2) for i in range(count)]
    return lax.ppermute(chunk, "seq", [(i, j) for i, j in pairs if 0 <= j < count])


def terms_over_bits(value, bits):
    count = lax.axis_size("seq")
    terms = []
    for mask in range(1, 1 << len(bits)):
        flip = sum(1 << bit for at, bit in enumerate(bits) if mask >> at & 1)
        terms.append(lax.ppermute(value, "seq", [(i, i ^ flip) for i in range(count)]))
    return terms


def sum_over(value, axis):
    count = lax.axis_size(axis)
    if count & (count - 1):
        return lax.psum(value, axis)
    for bit in range(count.bit_length() - 1):
        value += lax.ppermute(value, axis, [(i, i ^ (1 << bit)) for i in range(count)])
    return value


def on_device(gate_acts, value_acts, kernel, norm_gain, out_grad):
    rows, width = value_acts.shape
    heads = kernel.shape[0]
    lag = kernel.shape[1] // 2
    count = lax.axis_size("seq")
    assert width == heads * HEAD and rows == lag == CHUNKS * TILE
    assert count & (count - 1) == 0
    full_width = width * lax.axis_size("chan")
    gain = norm_gain.reshape(1, width)
    taps = kernel.astype(jnp.float32)

    ahead, behind = lax.optimization_barrier(
        (band_rows(taps[:, ::-1], 1, TILE - 1), band_rows(taps, 0, TILE))
    )
    band = bands(ahead)
    *chunks, last = split(value_acts)
    near = [swapped(chunk) for chunk in [*chunks, after(last, band)]]
    far = [relayed(chunk) for chunk in near]
    mixed, sums, even, odd = forward(
        band, value_acts, near, far[:-1], gate_acts, out_grad, gain, lag
    )
    first, sums = forward_last(band, far[-1], gate_acts, out_grad, gain, mixed, sums)
    sums = sum_over(sums, "chan")
    args = (mixed, first, gate_acts, out_grad, gain)
    mix_grad, gain_sums = mix_grad_of(full_width, sums, *args)

    grad_near = [swapped(part) for part in mix_grad]
    totals = kernel_grad_local(gain_sums, even, odd, far[-1], mix_grad, lag)
    normed, gate_grad = norm(full_width, after(sums, grad_near[0]), *args)
    back_band = bands(after(behind, grad_near[1]))
    grad_near[0], totals = lax.optimization_barrier((grad_near[0], totals))
    grad_near[3], normed, gate_grad, back_band = lax.optimization_barrier(
        (grad_near[3], normed, gate_grad, back_band)
    )
    bits = list(range(count.bit_length() - 1))
    for bit in bits[2:]:
        totals += terms_over_bits(totals, [bit])[0]
    grad_near[1], totals = lax.optimization_barrier((grad_near[1], totals))
    grad_far = [relayed(chunk) for chunk in grad_near]
    totals, *grad_far[:2] = lax.optimization_barrier((totals, *grad_far[:2]))
    terms = [totals] + terms_over_bits(totals, bits[:2])
    value_grad, first = value_grad_of(back_band, mix_grad, grad_near, grad_far[:-1], lag)
    value_grad = value_grad_last(back_band, grad_far[-1], first, value_grad)
    value_grad, *terms = lax.optimization_barrier((value_grad, *terms))
    totals = sum(terms[1:], terms[0])
    tokens = rows * count
    kernel_grad = totals[:, : 2 * lag] / math.sqrt(tokens * HEAD)
    gain_grad = totals[:, 2 * lag : 2 * lag + HEAD].reshape(width) / math.sqrt(tokens)
    return (normed, gate_grad, value_grad, kernel_grad, gain_grad)


def solution(mesh):
    placed = (P("seq", "chan"), P("seq", "chan"), P("chan", None), P("chan"), P("seq", "chan"))
    return jax.shard_map(
        on_device,
        mesh=mesh,
        in_specs=placed,
        out_specs=(
            P("seq", "chan"),
            P("seq", "chan"),
            P("seq", "chan"),
            P("chan", None),
            P("chan"),
        ),
        check_vma=False,
    )
```

```python
import functools
import math

import jax
import jax.numpy as jnp
from jax import lax
from jax.experimental import pallas as pl
from jax.experimental.pallas import tpu as pltpu
from jax.sharding import PartitionSpec as P

norm_eps = 1e-06
TILE = 256
LANES = 128
HEAD = 64
CHUNKS = 4
MIB = 1 << 20


def params(mib):
    return pltpu.CompilerParams(
        vmem_limit_bytes=mib * MIB, dimension_semantics=("arbitrary",)
    )


def cost(flops, moved):
    return pl.CostEstimate(flops=flops, bytes_accessed=moved, transcendentals=0)


def lane_iota(rows):
    return lax.broadcasted_iota(jnp.int32, (rows, LANES), 1)


def slab(pair):
    return pl.ds(pl.multiple_of(pair * LANES, LANES), LANES)


def odd_device():
    return lax.axis_index("seq") % 2 == 1


def own_row(chunk):
    row = jnp.where(odd_device(), (CHUNKS - 1 - chunk) * TILE, chunk * TILE)
    return pl.multiple_of(row, TILE)


VMEM = pl.BlockSpec(memory_space=pltpu.VMEM)


def held(*arrays):
    return [pltpu.with_memory_space_constraint(array, pltpu.VMEM) for array in arrays]


def after(value, *others):
    return lax.optimization_barrier((value, *others))[0]


def band_body(row_ref, band_ref):
    tiles = row_ref.shape[2] // LANES
    step = pl.program_id(0)
    upper = lane_iota(LANES) >= lax.broadcasted_iota(jnp.int32, (LANES, LANES), 0)
    for half in range(2):
        head = 2 * step + half
        before = jnp.zeros((LANES, LANES), jnp.float32)
        band_ref[head, :, :LANES] = before.astype(band_ref.dtype)
        for tile in range(tiles):
            segment = row_ref[step, half : half + 1, tile * LANES : (tile + 1) * LANES]
            turned = pltpu.roll(
                jnp.broadcast_to(segment, (LANES, LANES)), 0, 1, stride=1, stride_axis=0
            )
            cell = jnp.where(upper, turned, before)
            band_ref[head, :, (tile + 1) * LANES : (tile + 2) * LANES] = cell.astype(
                band_ref.dtype
            )
            before = turned


def band_rows(taps, low, high):
    heads = taps.shape[0]
    return jnp.pad(taps, ((0, 0), (low, high))).reshape(heads // 2, 2, -1)


def bands(rows):
    heads, length = 2 * rows.shape[0], rows.shape[2]
    return pl.pallas_call(
        band_body,
        grid=(heads // 2,),
        in_specs=[VMEM],
        out_specs=VMEM,
        out_shape=pltpu.VMEM((heads, LANES, length + LANES), jnp.bfloat16),
        compiler_params=params(4),
        cost_estimate=cost(heads * LANES * length, 2 * heads * LANES * length),
        name="bands",
    )(*held(rows))


def natural(chunks):
    return [jnp.where(odd_device(), *pair) for pair in zip(chunks[::-1], chunks)]


def extended(own, near, far):
    if len(far) < CHUNKS:
        far = [*far, jnp.zeros_like(near[0])]
    odd = odd_device()
    left = [jnp.where(odd, n, f) for n, f in zip(near, far[::-1])]
    right = [jnp.where(odd, f, n) for n, f in zip(near[::-1], far)]
    return left + own + right


def at_pair(refs, pair):
    return [ref[:, slab(pair)] for ref in refs]


def rows_of(ref, pair):
    return [ref[at : at + TILE, slab(pair)] for at in range(0, ref.shape[0], TILE)]


def layout_scratch(rows, lag, heads=2):
    wide = (rows + 2 * lag) // TILE * HEAD
    return [
        pltpu.VMEM((heads, TILE, wide), jnp.bfloat16),
        pltpu.VMEM((heads, TILE, wide - LANES), jnp.bfloat16),
    ]


def lay_out(blocks, even_ref, odd_ref, base=0):
    low = lane_iota(TILE) < HEAD
    turned = [pltpu.roll(block, HEAD, 1) for block in blocks]
    for tile in range(len(blocks) // 2):
        cols = slice(tile * LANES, (tile + 1) * LANES)
        first, second = 2 * tile, 2 * tile + 1
        even_ref[base, :, cols] = jnp.where(low, blocks[first], turned[second])
        even_ref[base + 1, :, cols] = jnp.where(low, turned[first], blocks[second])
        if odd_ref is not None and second + 1 < len(blocks):
            odd_ref[base, :, cols] = jnp.where(low, blocks[second], turned[second + 1])
            odd_ref[base + 1, :, cols] = jnp.where(low, turned[second], blocks[second + 1])


def window(even_ref, odd_ref, head, start, width):
    if start % 2 == 0:
        return even_ref[head, :, start * HEAD : start * HEAD + width]
    return odd_ref[head, :, (start - 1) * HEAD : (start - 1) * HEAD + width]


def band_product(band_ref, band_head, even_ref, odd_ref, head, slots, width):
    span = slots * TILE
    tile = jnp.concatenate(
        [band_ref[band_head, :, LANES : LANES + span], band_ref[band_head, :, :span]], axis=0
    )
    data = jnp.concatenate(
        [window(even_ref, odd_ref, head, slot, width) for slot in range(slots)], axis=0
    )
    return jnp.dot(tile, data, preferred_element_type=jnp.float32)


def token_blocks(first, second):
    low = lane_iota(TILE) < HEAD
    blocks = []
    for tile in range(first.shape[1] // LANES):
        cols = slice(tile * LANES, (tile + 1) * LANES)
        one, two = first[:, cols], second[:, cols]
        blocks.append(jnp.where(low, one, pltpu.roll(two, HEAD, 1)))
        blocks.append(jnp.where(low, pltpu.roll(one, HEAD, 1), two))
    return blocks


def last_term(band_ref, pair, last):
    low = lane_iota(TILE) < HEAD
    at = jnp.where(odd_device(), band_ref.shape[2] - LANES - TILE, 0)
    parts = []
    for half in range(2):
        head = 2 * pair + half
        tile = jnp.concatenate(
            [
                band_ref[head, :, pl.ds(pl.multiple_of(at + LANES, LANES), TILE)],
                band_ref[head, :, pl.ds(pl.multiple_of(at, LANES), TILE)],
            ],
            axis=0,
        )
        parts.append(jnp.dot(tile, last, preferred_element_type=jnp.float32))
    return jnp.where(low, *parts)


def split_body(value_ref, *refs):
    chunk_refs, sems = refs[:CHUNKS], refs[CHUNKS]
    copies = []
    for chunk, ref in enumerate(chunk_refs):
        copies.append(
            pltpu.make_async_copy(
                value_ref.at[pl.ds(own_row(chunk), TILE), :], ref, sems.at[chunk]
            )
        )
        copies[-1].start()
    for copy in copies:
        copy.wait()


def split(value):
    rows, width = value.shape
    return pl.pallas_call(
        split_body,
        in_specs=[pl.BlockSpec(memory_space=pltpu.HBM)],
        out_specs=[VMEM] * CHUNKS,
        out_shape=[pltpu.VMEM((TILE, width), value.dtype)] * CHUNKS,
        scratch_shapes=[pltpu.SemaphoreType.DMA((CHUNKS,))],
        compiler_params=pltpu.CompilerParams(vmem_limit_bytes=2 * MIB),
        cost_estimate=cost(0, 4 * rows * width),
        name="split",
    )(pltpu.with_memory_space_constraint(value, pltpu.HBM))


def product_flops(rows, width, lag):
    return 2 * (width // HEAD) * TILE * (TILE + 2 * lag) * rows // TILE * HEAD


def token_sums(square_ref, inner_ref, sums_ref, start):
    for at in range(0, square_ref.shape[0], LANES):
        rows = slice(at, at + LANES)
        cols = pl.ds(pl.multiple_of(start + at, LANES), LANES)
        sums_ref[0:1, cols] = jnp.sum(square_ref[rows, :].T, axis=0, keepdims=True)
        sums_ref[1:2, cols] = jnp.sum(inner_ref[rows, :].T, axis=0, keepdims=True)


def add_sums(mixed, gate, grad, gain, square_ref, inner_ref, at):
    hidden = gate.astype(jnp.float32) * mixed
    square_ref[at, :] += hidden * hidden
    inner_ref[at, :] += gain * grad.astype(jnp.float32) * hidden


def forward_body(slots, band_ref, own_ref, gate_ref, grad_ref, gain_ref, *refs):
    near_refs, far_refs, refs = refs[:CHUNKS], refs[CHUNKS : 2 * CHUNKS - 1], refs[2 * CHUNKS - 1 :]
    mixed_ref, sums_ref, even_ref, odd_ref, square_ref, inner_ref = refs
    pair = pl.program_id(0)
    heads = (2 * pair, 2 * pair + 1)

    @pl.when(pair == 0)
    def _():
        square_ref[...] = jnp.zeros_like(square_ref)
        inner_ref[...] = jnp.zeros_like(inner_ref)

    blocks = extended(rows_of(own_ref, pair), at_pair(near_refs, pair), at_pair(far_refs, pair))
    lay_out(blocks, even_ref, odd_ref, 2 * pair)
    width = mixed_ref.shape[0] // TILE * HEAD
    results = [band_product(band_ref, h, even_ref, odd_ref, h, slots, width) for h in heads]
    lanes = slab(pair)
    for index, mixed in enumerate(token_blocks(*results)):
        at = slice(index * TILE, (index + 1) * TILE)
        mixed_ref[at, lanes] = mixed
        add_sums(
            mixed, gate_ref[at, lanes], grad_ref[at, lanes], gain_ref[:, lanes], square_ref, inner_ref, at
        )

    @pl.when(pair == pl.num_programs(0) - 1)
    def _():
        token_sums(square_ref, inner_ref, sums_ref, 0)


def forward(band, own, near, far, gate, grad, gain, lag):
    rows, width = gate.shape
    slots = 1 + 2 * lag // TILE
    operands = held(band, own, gate, grad, gain, *near, *far)
    return pl.pallas_call(
        functools.partial(forward_body, slots),
        grid=(width // LANES,),
        in_specs=[VMEM] * len(operands),
        out_specs=[VMEM] * 4,
        out_shape=[
            pltpu.VMEM((rows, width), jnp.float32),
            pltpu.VMEM((2, rows), jnp.float32),
            *layout_scratch(rows, lag, width // HEAD),
        ],
        scratch_shapes=[pltpu.VMEM((rows, LANES), jnp.float32)] * 2,
        compiler_params=params(9),
        cost_estimate=cost(product_flops(rows, width, lag), 16 * rows * width),
        name="forward",
    )(*operands)


def forward_last_body(band_ref, last_ref, gate_ref, grad_ref, gain_ref, mixed_ref, sums_ref, *refs):
    first_ref, out_ref, square_ref, inner_ref = refs
    pair = pl.program_id(0)

    @pl.when(pair == 0)
    def _():
        square_ref[...] = jnp.zeros_like(square_ref)
        inner_ref[...] = jnp.zeros_like(inner_ref)
        out_ref[...] = sums_ref[...]

    lanes, rows = slab(pair), pl.ds(own_row(0), TILE)
    mixed = mixed_ref[rows, lanes] + last_term(band_ref, pair, last_ref[:, lanes])
    first_ref[:, lanes] = mixed
    add_sums(
        mixed,
        gate_ref[rows, lanes],
        grad_ref[rows, lanes],
        gain_ref[:, lanes],
        square_ref,
        inner_ref,
        slice(None),
    )

    @pl.when(pair == pl.num_programs(0) - 1)
    def _():
        token_sums(square_ref, inner_ref, out_ref, own_row(0))


def forward_last(band, last, gate, grad, gain, mixed, sums):
    rows, width = gate.shape
    operands = held(band, last, gate, grad, gain, mixed, sums)
    return pl.pallas_call(
        forward_last_body,
        grid=(width // LANES,),
        in_specs=[VMEM] * len(operands),
        out_specs=[VMEM] * 2,
        out_shape=[
            pltpu.VMEM((TILE, width), jnp.float32),
            pltpu.VMEM((2, rows), jnp.float32),
        ],
        scratch_shapes=[pltpu.VMEM((TILE, LANES), jnp.float32)] * 2,
        compiler_params=params(6),
        cost_estimate=cost(8 * TILE * TILE * width, 6 * TILE * width),
        name="forward_last",
    )(*operands)


def token_columns(full_width, sums_ref, tokens):
    scale = lax.rsqrt(sums_ref[0:1, tokens] / full_width + norm_eps)
    pull = scale * scale * sums_ref[1:2, tokens] / full_width
    return (
        jnp.broadcast_to(scale, (LANES, LANES)).T,
        jnp.broadcast_to(pull, (LANES, LANES)).T,
    )


def mix_grad_body(full_width, sums_ref, mixed_ref, first_ref, gate_ref, grad_ref, gain_ref, *refs):
    out_refs, gain_grad_ref, total_ref = refs[:-2], refs[-2], refs[-1]
    total_ref[...] = jnp.zeros_like(total_ref)
    for chunk, out_ref in enumerate(out_refs):
        for at in range(0, TILE, LANES):
            tokens = pl.ds(pl.multiple_of(own_row(chunk) + at, LANES), LANES)
            rows = slice(at, at + LANES)
            scale, pull = token_columns(full_width, sums_ref, tokens)
            for lane in range(0, mixed_ref.shape[1], LANES):
                cols = slice(lane, lane + LANES)
                gate = gate_ref[tokens, cols].astype(jnp.float32)
                grad = grad_ref[tokens, cols].astype(jnp.float32)
                mixed = mixed_ref[tokens, cols] if chunk else first_ref[rows, cols]
                hidden = gate * mixed
                hidden_grad = scale * (gain_ref[:, cols] * grad - hidden * pull)
                out_ref[rows, cols] = (hidden_grad * gate).astype(out_ref.dtype)
                total_ref[:, cols] += jnp.sum(
                    (grad * (hidden * scale)).reshape(LANES // 8, 8, LANES), axis=0
                )
    gain_grad_ref[...] = jnp.sum(total_ref[...], axis=0, keepdims=True)


def mix_grad_of(full_width, *operands):
    rows, width = operands[1].shape
    operands = held(*operands)
    *chunks, gain_sums = pl.pallas_call(
        functools.partial(mix_grad_body, full_width),
        in_specs=[VMEM] * len(operands),
        out_specs=[VMEM] * (CHUNKS + 1),
        out_shape=[pltpu.VMEM((TILE, width), jnp.bfloat16)] * CHUNKS
        + [pltpu.VMEM((1, width), jnp.float32)],
        scratch_shapes=[pltpu.VMEM((8, width), jnp.float32)],
        compiler_params=pltpu.CompilerParams(vmem_limit_bytes=4 * MIB),
        cost_estimate=cost(14 * rows * width, 10 * rows * width),
        name="mix_grad",
    )(*operands)
    return chunks, gain_sums


def norm_body(full_width, sums_ref, mixed_ref, first_ref, gate_ref, grad_ref, gain_ref, *refs):
    normed_ref, gate_grad_ref = refs
    start = pl.program_id(0) * LANES
    tokens = pl.ds(pl.multiple_of(start, LANES), LANES)
    within = pl.ds(pl.multiple_of(lax.rem(start, TILE), LANES), LANES)
    first = start // TILE == own_row(0) // TILE
    scale, pull = token_columns(full_width, sums_ref, tokens)
    for lane in range(0, mixed_ref.shape[1], LANES):
        cols = slice(lane, lane + LANES)
        gain = gain_ref[:, cols]
        gate = gate_ref[tokens, cols].astype(jnp.float32)
        mixed = jnp.where(first, first_ref[within, cols], mixed_ref[tokens, cols])
        grad = grad_ref[tokens, cols].astype(jnp.float32)
        hidden = gate * mixed
        normed_ref[:, cols] = (hidden * scale * gain).astype(normed_ref.dtype)
        hidden_grad = scale * (gain * grad - hidden * pull)
        gate_grad_ref[:, cols] = (hidden_grad * mixed).astype(gate_grad_ref.dtype)


def norm(full_width, *operands):
    rows, width = operands[1].shape
    operands = held(*operands)
    big = jax.ShapeDtypeStruct((rows, width), jnp.bfloat16)
    return pl.pallas_call(
        functools.partial(norm_body, full_width),
        grid=(rows // LANES,),
        in_specs=[VMEM] * len(operands),
        out_specs=[pl.BlockSpec((LANES, width), lambda g: (g, 0))] * 2,
        out_shape=[big, big],
        compiler_params=params(6),
        cost_estimate=cost(14 * rows * width, 12 * rows * width),
        name="norm",
    )(*operands)


def patched(even_ref, head, half, slot, slots, width, last):
    data = even_ref[head, :, slot * HEAD : slot * HEAD + width]
    low = lane_iota(TILE) < HEAD
    turned = pltpu.roll(last, HEAD, 1)
    if slot == 0:
        tile = data[:, :LANES]
        put = jnp.where(low, last if half == 0 else turned, tile)
        return jnp.concatenate([jnp.where(odd_device(), tile, put), data[:, LANES:]], axis=1)
    if slot == slots - 1:
        tile = data[:, width - LANES :]
        put = jnp.where(low, tile, turned if half == 0 else last)
        return jnp.concatenate([data[:, : width - LANES], jnp.where(odd_device(), put, tile)], axis=1)
    return data


def kernel_grad_body(slots, gain_ref, even_ref, odd_ref, last_ref, *refs):
    mix_refs, (out_ref, mix_even_ref, cells_ref) = refs[:CHUNKS], refs[CHUNKS:]
    pair = pl.program_id(0)
    last = last_ref[:, slab(pair)]
    blocks = natural(at_pair(mix_refs, pair))
    lay_out(blocks, mix_even_ref, None)
    width = len(blocks) * HEAD
    span = cells_ref.shape[1]
    lags = span - LANES
    gains = gain_ref[:, slab(pair)]
    for half in range(2):
        mix = mix_even_ref[half].T
        carry = None
        for lag_slot in range(slots):
            slot, head = slots - 1 - lag_slot, 2 * pair + half
            if slot % 2 == 0:
                data = patched(even_ref, head, half, slot, slots, width, last)
            else:
                data = window(even_ref, odd_ref, head, slot, width)
            cross = jnp.dot(data, mix, preferred_element_type=jnp.float32)
            at = 2 * lag_slot * LANES
            upper, lower = cross[:LANES], cross[LANES:]
            if carry is not None:
                cells_ref[:, at - LANES : at] = carry + lower[:, :LANES]
            cells_ref[:, at : at + LANES] = upper[:, :LANES] + lower[:, LANES:]
            carry = upper[:, LANES:]
        total = cells_ref[0:8, :]
        for group in range(1, LANES // 8):
            total += pltpu.roll(cells_ref[8 * group : 8 * group + 8, :], span - 8 * group, 1)
        row = lax.broadcasted_iota(jnp.int32, (8, span), 0)
        for bit in (1, 2, 4):
            total = jnp.where((row & bit) != 0, pltpu.roll(total, span - bit, 1), total)
        sums = jnp.concatenate(
            [
                jnp.sum(total, axis=0, keepdims=True)[:, :lags],
                gains if half == 0 else pltpu.roll(gains, HEAD, 1),
            ],
            axis=1,
        )
        tall = min(8, out_ref.shape[0])
        row = 2 * pair + half
        group = pl.ds(pl.multiple_of(row // tall * tall, tall), tall)
        here = lax.broadcasted_iota(jnp.int32, (tall, out_ref.shape[1]), 0) == lax.rem(row, tall)
        out_ref[group, :] = jnp.where(here, sums, out_ref[group, :])


def kernel_grad_local(gain_sums, even, odd, last, mix_grad, lag):
    rows, width = len(mix_grad) * TILE, last.shape[1]
    pairs = width // LANES
    slots = 1 + 2 * lag // TILE
    operands = held(gain_sums, even, odd, last, *mix_grad)
    return pl.pallas_call(
        functools.partial(kernel_grad_body, slots),
        grid=(pairs,),
        in_specs=[VMEM] * len(operands),
        out_specs=VMEM,
        out_shape=pltpu.VMEM((2 * pairs, 2 * lag + LANES), jnp.float32),
        scratch_shapes=[
            pltpu.VMEM((2, TILE, rows // TILE * HEAD), jnp.bfloat16),
            pltpu.VMEM((LANES, 2 * lag + LANES), jnp.float32),
        ],
        compiler_params=params(8),
        cost_estimate=cost(product_flops(rows, width, lag), 8 * rows * width),
        name="kernel_grad",
    )(*operands)


def value_grad_body(slots, band_ref, *refs):
    own_refs, near_refs, refs = refs[:CHUNKS], refs[CHUNKS : 2 * CHUNKS], refs[2 * CHUNKS :]
    far_refs, (out_ref, first_ref, even_ref, odd_ref) = refs[: CHUNKS - 1], refs[CHUNKS - 1 :]
    pair = pl.program_id(0)
    own = natural(at_pair(own_refs, pair))
    blocks = extended(own, at_pair(near_refs, pair), at_pair(far_refs, pair))
    lay_out(blocks, even_ref, odd_ref)
    width = len(own) * HEAD
    results = [
        band_product(band_ref, 2 * pair + half, even_ref, odd_ref, half, slots, width)
        for half in range(2)
    ]
    blocks = token_blocks(*results)
    first_ref[:, slab(pair)] = jnp.where(odd_device(), blocks[-1], blocks[0])
    for index, block in enumerate(blocks):
        out_ref[index * TILE : (index + 1) * TILE, :] = block.astype(out_ref.dtype)


def value_grad_of(band, own, near, far, lag):
    rows, width = len(own) * TILE, own[0].shape[1]
    slots = 1 + 2 * lag // TILE
    operands = held(band, *own, *near, *far)
    return pl.pallas_call(
        functools.partial(value_grad_body, slots),
        grid=(width // LANES,),
        in_specs=[VMEM] * len(operands),
        out_specs=[pl.BlockSpec((rows, LANES), lambda g: (0, g)), VMEM],
        out_shape=[
            jax.ShapeDtypeStruct((rows, width), jnp.bfloat16),
            pltpu.VMEM((TILE, width), jnp.float32),
        ],
        scratch_shapes=layout_scratch(rows, lag),
        compiler_params=params(10),
        cost_estimate=cost(product_flops(rows, width, lag), 12 * rows * width),
        name="value_grad",
    )(*operands)


def value_grad_last_body(band_ref, last_ref, first_ref, rest_ref, out_ref, block_ref, sem):
    pair = pl.program_id(0)
    lanes = slab(pair)
    block = first_ref[:, lanes] + last_term(band_ref, pair, last_ref[:, lanes])
    block_ref[:, lanes] = block.astype(block_ref.dtype)

    @pl.when(pair == pl.num_programs(0) - 1)
    def _():
        copy = pltpu.make_async_copy(block_ref, out_ref.at[pl.ds(own_row(0), TILE), :], sem)
        copy.start()
        copy.wait()


def value_grad_last(band, last, first, rest):
    width = first.shape[1]
    operands = held(band, last, first)
    return pl.pallas_call(
        value_grad_last_body,
        grid=(width // LANES,),
        in_specs=[VMEM] * len(operands) + [pl.BlockSpec(memory_space=pl.ANY)],
        out_specs=pl.BlockSpec(memory_space=pl.ANY),
        out_shape=jax.ShapeDtypeStruct(rest.shape, rest.dtype),
        input_output_aliases={len(operands): 0},
        scratch_shapes=[pltpu.VMEM((TILE, width), jnp.bfloat16), pltpu.SemaphoreType.DMA(())],
        compiler_params=params(6),
        cost_estimate=cost(8 * TILE * TILE * width, 6 * TILE * width),
        name="value_grad_last",
    )(*operands, rest)


def swapped(chunk):
    count = lax.axis_size("seq")
    return lax.ppermute(chunk, "seq", [(i, i ^ 1) for i in range(count)])


def relayed(chunk):
    count = lax.axis_size("seq")
    pairs = [(i, i + 2) if i % 2 == 0 else (i, i - 2) for i in range(count)]
    return lax.ppermute(chunk, "seq", [(i, j) for i, j in pairs if 0 <= j < count])


def terms_over_bits(value, bits):
    count = lax.axis_size("seq")
    terms = []
    for mask in range(1, 1 << len(bits)):
        flip = sum(1 << bit for at, bit in enumerate(bits) if mask >> at & 1)
        terms.append(lax.ppermute(value, "seq", [(i, i ^ flip) for i in range(count)]))
    return terms


def sum_over(value, axis):
    count = lax.axis_size(axis)
    if count & (count - 1):
        return lax.psum(value, axis)
    for bit in range(count.bit_length() - 1):
        value += lax.ppermute(value, axis, [(i, i ^ (1 << bit)) for i in range(count)])
    return value


def on_device(gate_acts, value_acts, kernel, norm_gain, out_grad):
    rows, width = value_acts.shape
    heads = kernel.shape[0]
    lag = kernel.shape[1] // 2
    count = lax.axis_size("seq")
    assert width == heads * HEAD and rows == lag == CHUNKS * TILE
    assert count & (count - 1) == 0
    full_width = width * lax.axis_size("chan")
    gain = norm_gain.reshape(1, width)
    taps = kernel.astype(jnp.float32)

    ahead, behind = lax.optimization_barrier(
        (band_rows(taps[:, ::-1], 1, TILE - 1), band_rows(taps, 0, TILE))
    )
    band = bands(ahead)
    *chunks, last = split(value_acts)
    near = [swapped(chunk) for chunk in [*chunks, after(last, band)]]
    far = [relayed(chunk) for chunk in near]
    mixed, sums, even, odd = forward(
        band, value_acts, near, far[:-1], gate_acts, out_grad, gain, lag
    )
    first, sums = forward_last(band, far[-1], gate_acts, out_grad, gain, mixed, sums)
    sums = sum_over(sums, "chan")
    args = (mixed, first, gate_acts, out_grad, gain)
    mix_grad, gain_sums = mix_grad_of(full_width, sums, *args)

    grad_near = [swapped(part) for part in mix_grad]
    totals = kernel_grad_local(gain_sums, even, odd, far[-1], mix_grad, lag)
    normed, gate_grad = norm(full_width, after(sums, grad_near[0]), *args)
    back_band = bands(after(behind, grad_near[1]))
    grad_near[0], totals = lax.optimization_barrier((grad_near[0], totals))
    grad_near[3], normed, gate_grad, back_band = lax.optimization_barrier(
        (grad_near[3], normed, gate_grad, back_band)
    )
    bits = list(range(count.bit_length() - 1))
    totals += terms_over_bits(totals, bits[2:3])[0]
    grad_near[1], totals = lax.optimization_barrier((grad_near[1], totals))
    grad_far = [relayed(chunk) for chunk in grad_near[:2]]
    grad_near[2], totals, grad_far[0] = lax.optimization_barrier(
        (grad_near[2], totals, grad_far[0])
    )
    grad_far += [relayed(chunk) for chunk in grad_near[2:]]
    term = terms_over_bits(after(totals, grad_near[3]), bits[:1])[0]
    value_grad, first = value_grad_of(back_band, mix_grad, grad_near, grad_far[:-1], lag)
    totals, term, first = lax.optimization_barrier((totals, term, first))
    totals += term
    for bit in bits[4:]:
        totals += terms_over_bits(totals, [bit])[0]
    terms = [totals] + terms_over_bits(totals, bits[1:2] + bits[3:4])
    value_grad = value_grad_last(back_band, grad_far[-1], first, value_grad)
    value_grad, *terms = lax.optimization_barrier((value_grad, *terms))
    totals = sum(terms[1:], terms[0])
    tokens = rows * count
    kernel_grad = totals[:, : 2 * lag] / math.sqrt(tokens * HEAD)
    gain_grad = totals[:, 2 * lag : 2 * lag + HEAD].reshape(width) / math.sqrt(tokens)
    return (normed, gate_grad, value_grad, kernel_grad, gain_grad)


def solution(mesh):
    placed = (P("seq", "chan"), P("seq", "chan"), P("chan", None), P("chan"), P("seq", "chan"))
    return jax.shard_map(
        on_device,
        mesh=mesh,
        in_specs=placed,
        out_specs=(
            P("seq", "chan"),
            P("seq", "chan"),
            P("seq", "chan"),
            P("chan", None),
            P("chan"),
        ),
        check_vma=False,
    )
```

```python
import functools
import math

import jax
import jax.numpy as jnp
from jax import lax
from jax.experimental import pallas as pl
from jax.experimental.pallas import tpu as pltpu
from jax.sharding import PartitionSpec as P

norm_eps = 1e-06
TILE = 256
LANES = 128
HEAD = 64
CHUNKS = 4
MIB = 1 << 20


def params(mib):
    return pltpu.CompilerParams(
        vmem_limit_bytes=mib * MIB, dimension_semantics=("arbitrary",)
    )


def cost(flops, moved):
    return pl.CostEstimate(flops=flops, bytes_accessed=moved, transcendentals=0)


def lane_iota(rows):
    return lax.broadcasted_iota(jnp.int32, (rows, LANES), 1)


def slab(pair):
    return pl.ds(pl.multiple_of(pair * LANES, LANES), LANES)


def odd_device():
    return lax.axis_index("seq") % 2 == 1


def own_row(chunk):
    row = jnp.where(odd_device(), (CHUNKS - 1 - chunk) * TILE, chunk * TILE)
    return pl.multiple_of(row, TILE)


VMEM = pl.BlockSpec(memory_space=pltpu.VMEM)


def held(*arrays):
    return [pltpu.with_memory_space_constraint(array, pltpu.VMEM) for array in arrays]


def after(value, *others):
    return lax.optimization_barrier((value, *others))[0]


def band_body(row_ref, band_ref):
    tiles = row_ref.shape[2] // LANES
    step = pl.program_id(0)
    upper = lane_iota(LANES) >= lax.broadcasted_iota(jnp.int32, (LANES, LANES), 0)
    for half in range(2):
        head = 2 * step + half
        before = jnp.zeros((LANES, LANES), jnp.float32)
        band_ref[head, :, :LANES] = before.astype(band_ref.dtype)
        for tile in range(tiles):
            segment = row_ref[step, half : half + 1, tile * LANES : (tile + 1) * LANES]
            turned = pltpu.roll(
                jnp.broadcast_to(segment, (LANES, LANES)), 0, 1, stride=1, stride_axis=0
            )
            cell = jnp.where(upper, turned, before)
            band_ref[head, :, (tile + 1) * LANES : (tile + 2) * LANES] = cell.astype(
                band_ref.dtype
            )
            before = turned


def band_rows(taps, low, high):
    heads = taps.shape[0]
    return jnp.pad(taps, ((0, 0), (low, high))).reshape(heads // 2, 2, -1)


def bands(rows):
    heads, length = 2 * rows.shape[0], rows.shape[2]
    return pl.pallas_call(
        band_body,
        grid=(heads // 2,),
        in_specs=[VMEM],
        out_specs=VMEM,
        out_shape=pltpu.VMEM((heads, LANES, length + LANES), jnp.bfloat16),
        compiler_params=params(4),
        cost_estimate=cost(heads * LANES * length, 2 * heads * LANES * length),
        name="bands",
    )(*held(rows))


def natural(chunks):
    return [jnp.where(odd_device(), *pair) for pair in zip(chunks[::-1], chunks)]


def extended(own, near, far):
    if len(far) < CHUNKS:
        far = [*far, jnp.zeros_like(near[0])]
    odd = odd_device()
    left = [jnp.where(odd, n, f) for n, f in zip(near, far[::-1])]
    right = [jnp.where(odd, f, n) for n, f in zip(near[::-1], far)]
    return left + own + right


def at_pair(refs, pair):
    return [ref[:, slab(pair)] for ref in refs]


def rows_of(ref, pair):
    return [ref[at : at + TILE, slab(pair)] for at in range(0, ref.shape[0], TILE)]


def layout_scratch(rows, lag, heads=2):
    wide = (rows + 2 * lag) // TILE * HEAD
    return [
        pltpu.VMEM((heads, TILE, wide), jnp.bfloat16),
        pltpu.VMEM((heads, TILE, wide - LANES), jnp.bfloat16),
    ]


def lay_out(blocks, even_ref, odd_ref, base=0):
    low = lane_iota(TILE) < HEAD
    turned = [pltpu.roll(block, HEAD, 1) for block in blocks]
    for tile in range(len(blocks) // 2):
        cols = slice(tile * LANES, (tile + 1) * LANES)
        first, second = 2 * tile, 2 * tile + 1
        even_ref[base, :, cols] = jnp.where(low, blocks[first], turned[second])
        even_ref[base + 1, :, cols] = jnp.where(low, turned[first], blocks[second])
        if odd_ref is not None and second + 1 < len(blocks):
            odd_ref[base, :, cols] = jnp.where(low, blocks[second], turned[second + 1])
            odd_ref[base + 1, :, cols] = jnp.where(low, turned[second], blocks[second + 1])


def window(even_ref, odd_ref, head, start, width):
    if start % 2 == 0:
        return even_ref[head, :, start * HEAD : start * HEAD + width]
    return odd_ref[head, :, (start - 1) * HEAD : (start - 1) * HEAD + width]


def band_product(band_ref, band_head, even_ref, odd_ref, head, slots, width):
    span = slots * TILE
    tile = jnp.concatenate(
        [band_ref[band_head, :, LANES : LANES + span], band_ref[band_head, :, :span]], axis=0
    )
    data = jnp.concatenate(
        [window(even_ref, odd_ref, head, slot, width) for slot in range(slots)], axis=0
    )
    return jnp.dot(tile, data, preferred_element_type=jnp.float32)


def token_blocks(first, second):
    low = lane_iota(TILE) < HEAD
    blocks = []
    for tile in range(first.shape[1] // LANES):
        cols = slice(tile * LANES, (tile + 1) * LANES)
        one, two = first[:, cols], second[:, cols]
        blocks.append(jnp.where(low, one, pltpu.roll(two, HEAD, 1)))
        blocks.append(jnp.where(low, pltpu.roll(one, HEAD, 1), two))
    return blocks


def last_term(band_ref, pair, last):
    low = lane_iota(TILE) < HEAD
    at = jnp.where(odd_device(), band_ref.shape[2] - LANES - TILE, 0)
    parts = []
    for half in range(2):
        head = 2 * pair + half
        tile = jnp.concatenate(
            [
                band_ref[head, :, pl.ds(pl.multiple_of(at + LANES, LANES), TILE)],
                band_ref[head, :, pl.ds(pl.multiple_of(at, LANES), TILE)],
            ],
            axis=0,
        )
        parts.append(jnp.dot(tile, last, preferred_element_type=jnp.float32))
    return jnp.where(low, *parts)


def split_body(value_ref, *refs):
    chunk_refs, sems = refs[:CHUNKS], refs[CHUNKS]
    copies = []
    for chunk, ref in enumerate(chunk_refs):
        copies.append(
            pltpu.make_async_copy(
                value_ref.at[pl.ds(own_row(chunk), TILE), :], ref, sems.at[chunk]
            )
        )
        copies[-1].start()
    for copy in copies:
        copy.wait()


def split(value):
    rows, width = value.shape
    return pl.pallas_call(
        split_body,
        in_specs=[pl.BlockSpec(memory_space=pltpu.HBM)],
        out_specs=[VMEM] * CHUNKS,
        out_shape=[pltpu.VMEM((TILE, width), value.dtype)] * CHUNKS,
        scratch_shapes=[pltpu.SemaphoreType.DMA((CHUNKS,))],
        compiler_params=pltpu.CompilerParams(vmem_limit_bytes=2 * MIB),
        cost_estimate=cost(0, 4 * rows * width),
        name="split",
    )(pltpu.with_memory_space_constraint(value, pltpu.HBM))


def product_flops(rows, width, lag):
    return 2 * (width // HEAD) * TILE * (TILE + 2 * lag) * rows // TILE * HEAD


def token_sums(square_ref, inner_ref, sums_ref, start):
    for at in range(0, square_ref.shape[0], LANES):
        rows = slice(at, at + LANES)
        cols = pl.ds(pl.multiple_of(start + at, LANES), LANES)
        sums_ref[0:1, cols] = jnp.sum(square_ref[rows, :].T, axis=0, keepdims=True)
        sums_ref[1:2, cols] = jnp.sum(inner_ref[rows, :].T, axis=0, keepdims=True)


def add_sums(mixed, gate, grad, gain, square_ref, inner_ref, at):
    hidden = gate.astype(jnp.float32) * mixed
    square_ref[at, :] += hidden * hidden
    inner_ref[at, :] += gain * grad.astype(jnp.float32) * hidden


def forward_body(slots, band_ref, own_ref, gate_ref, grad_ref, gain_ref, *refs):
    near_refs, far_refs, refs = refs[:CHUNKS], refs[CHUNKS : 2 * CHUNKS - 1], refs[2 * CHUNKS - 1 :]
    mixed_ref, sums_ref, even_ref, odd_ref, square_ref, inner_ref = refs
    pair = pl.program_id(0)
    heads = (2 * pair, 2 * pair + 1)

    @pl.when(pair == 0)
    def _():
        square_ref[...] = jnp.zeros_like(square_ref)
        inner_ref[...] = jnp.zeros_like(inner_ref)

    blocks = extended(rows_of(own_ref, pair), at_pair(near_refs, pair), at_pair(far_refs, pair))
    lay_out(blocks, even_ref, odd_ref, 2 * pair)
    width = mixed_ref.shape[0] // TILE * HEAD
    results = [band_product(band_ref, h, even_ref, odd_ref, h, slots, width) for h in heads]
    lanes = slab(pair)
    for index, mixed in enumerate(token_blocks(*results)):
        at = slice(index * TILE, (index + 1) * TILE)
        mixed_ref[at, lanes] = mixed
        add_sums(
            mixed, gate_ref[at, lanes], grad_ref[at, lanes], gain_ref[:, lanes], square_ref, inner_ref, at
        )

    @pl.when(pair == pl.num_programs(0) - 1)
    def _():
        token_sums(square_ref, inner_ref, sums_ref, 0)


def forward(band, own, near, far, gate, grad, gain, lag):
    rows, width = gate.shape
    slots = 1 + 2 * lag // TILE
    operands = held(band, own, gate, grad, gain, *near, *far)
    return pl.pallas_call(
        functools.partial(forward_body, slots),
        grid=(width // LANES,),
        in_specs=[VMEM] * len(operands),
        out_specs=[VMEM] * 4,
        out_shape=[
            pltpu.VMEM((rows, width), jnp.float32),
            pltpu.VMEM((2, rows), jnp.float32),
            *layout_scratch(rows, lag, width // HEAD),
        ],
        scratch_shapes=[pltpu.VMEM((rows, LANES), jnp.float32)] * 2,
        compiler_params=params(9),
        cost_estimate=cost(product_flops(rows, width, lag), 16 * rows * width),
        name="forward",
    )(*operands)


def forward_last_body(band_ref, last_ref, gate_ref, grad_ref, gain_ref, mixed_ref, sums_ref, *refs):
    first_ref, out_ref, square_ref, inner_ref = refs
    pair = pl.program_id(0)

    @pl.when(pair == 0)
    def _():
        square_ref[...] = jnp.zeros_like(square_ref)
        inner_ref[...] = jnp.zeros_like(inner_ref)
        out_ref[...] = sums_ref[...]

    lanes, rows = slab(pair), pl.ds(own_row(0), TILE)
    mixed = mixed_ref[rows, lanes] + last_term(band_ref, pair, last_ref[:, lanes])
    first_ref[:, lanes] = mixed
    add_sums(
        mixed,
        gate_ref[rows, lanes],
        grad_ref[rows, lanes],
        gain_ref[:, lanes],
        square_ref,
        inner_ref,
        slice(None),
    )

    @pl.when(pair == pl.num_programs(0) - 1)
    def _():
        token_sums(square_ref, inner_ref, out_ref, own_row(0))


def forward_last(band, last, gate, grad, gain, mixed, sums):
    rows, width = gate.shape
    operands = held(band, last, gate, grad, gain, mixed, sums)
    return pl.pallas_call(
        forward_last_body,
        grid=(width // LANES,),
        in_specs=[VMEM] * len(operands),
        out_specs=[VMEM] * 2,
        out_shape=[
            pltpu.VMEM((TILE, width), jnp.float32),
            pltpu.VMEM((2, rows), jnp.float32),
        ],
        scratch_shapes=[pltpu.VMEM((TILE, LANES), jnp.float32)] * 2,
        compiler_params=params(6),
        cost_estimate=cost(8 * TILE * TILE * width, 6 * TILE * width),
        name="forward_last",
    )(*operands)


def token_columns(full_width, sums_ref, tokens):
    scale = lax.rsqrt(sums_ref[0:1, tokens] / full_width + norm_eps)
    pull = scale * scale * sums_ref[1:2, tokens] / full_width
    return (
        jnp.broadcast_to(scale, (LANES, LANES)).T,
        jnp.broadcast_to(pull, (LANES, LANES)).T,
    )


def mix_grad_body(full_width, sums_ref, mixed_ref, first_ref, gate_ref, grad_ref, gain_ref, *refs):
    out_refs, gain_grad_ref, total_ref = refs[:-2], refs[-2], refs[-1]
    total_ref[...] = jnp.zeros_like(total_ref)
    for chunk, out_ref in enumerate(out_refs):
        for at in range(0, TILE, LANES):
            tokens = pl.ds(pl.multiple_of(own_row(chunk) + at, LANES), LANES)
            rows = slice(at, at + LANES)
            scale, pull = token_columns(full_width, sums_ref, tokens)
            for lane in range(0, mixed_ref.shape[1], LANES):
                cols = slice(lane, lane + LANES)
                gate = gate_ref[tokens, cols].astype(jnp.float32)
                grad = grad_ref[tokens, cols].astype(jnp.float32)
                mixed = mixed_ref[tokens, cols] if chunk else first_ref[rows, cols]
                hidden = gate * mixed
                hidden_grad = scale * (gain_ref[:, cols] * grad - hidden * pull)
                out_ref[rows, cols] = (hidden_grad * gate).astype(out_ref.dtype)
                total_ref[:, cols] += jnp.sum(
                    (grad * (hidden * scale)).reshape(LANES // 8, 8, LANES), axis=0
                )
    gain_grad_ref[...] = jnp.sum(total_ref[...], axis=0, keepdims=True)


def mix_grad_of(full_width, *operands):
    rows, width = operands[1].shape
    operands = held(*operands)
    *chunks, gain_sums = pl.pallas_call(
        functools.partial(mix_grad_body, full_width),
        in_specs=[VMEM] * len(operands),
        out_specs=[VMEM] * (CHUNKS + 1),
        out_shape=[pltpu.VMEM((TILE, width), jnp.bfloat16)] * CHUNKS
        + [pltpu.VMEM((1, width), jnp.float32)],
        scratch_shapes=[pltpu.VMEM((8, width), jnp.float32)],
        compiler_params=pltpu.CompilerParams(vmem_limit_bytes=4 * MIB),
        cost_estimate=cost(14 * rows * width, 10 * rows * width),
        name="mix_grad",
    )(*operands)
    return chunks, gain_sums


def norm_body(full_width, sums_ref, mixed_ref, first_ref, gate_ref, grad_ref, gain_ref, *refs):
    normed_ref, gate_grad_ref = refs
    start = pl.program_id(0) * LANES
    tokens = pl.ds(pl.multiple_of(start, LANES), LANES)
    within = pl.ds(pl.multiple_of(lax.rem(start, TILE), LANES), LANES)
    first = start // TILE == own_row(0) // TILE
    scale, pull = token_columns(full_width, sums_ref, tokens)
    for lane in range(0, mixed_ref.shape[1], LANES):
        cols = slice(lane, lane + LANES)
        gain = gain_ref[:, cols]
        gate = gate_ref[tokens, cols].astype(jnp.float32)
        mixed = jnp.where(first, first_ref[within, cols], mixed_ref[tokens, cols])
        grad = grad_ref[tokens, cols].astype(jnp.float32)
        hidden = gate * mixed
        normed_ref[:, cols] = (hidden * scale * gain).astype(normed_ref.dtype)
        hidden_grad = scale * (gain * grad - hidden * pull)
        gate_grad_ref[:, cols] = (hidden_grad * mixed).astype(gate_grad_ref.dtype)


def norm(full_width, *operands):
    rows, width = operands[1].shape
    operands = held(*operands)
    big = jax.ShapeDtypeStruct((rows, width), jnp.bfloat16)
    return pl.pallas_call(
        functools.partial(norm_body, full_width),
        grid=(rows // LANES,),
        in_specs=[VMEM] * len(operands),
        out_specs=[pl.BlockSpec((LANES, width), lambda g: (g, 0))] * 2,
        out_shape=[big, big],
        compiler_params=params(6),
        cost_estimate=cost(14 * rows * width, 12 * rows * width),
        name="norm",
    )(*operands)


def patched(even_ref, head, half, slot, slots, width, last):
    data = even_ref[head, :, slot * HEAD : slot * HEAD + width]
    low = lane_iota(TILE) < HEAD
    turned = pltpu.roll(last, HEAD, 1)
    if slot == 0:
        tile = data[:, :LANES]
        put = jnp.where(low, last if half == 0 else turned, tile)
        return jnp.concatenate([jnp.where(odd_device(), tile, put), data[:, LANES:]], axis=1)
    if slot == slots - 1:
        tile = data[:, width - LANES :]
        put = jnp.where(low, tile, turned if half == 0 else last)
        return jnp.concatenate([data[:, : width - LANES], jnp.where(odd_device(), put, tile)], axis=1)
    return data


def kernel_grad_body(slots, gain_ref, even_ref, odd_ref, last_ref, *refs):
    mix_refs, (out_ref, mix_even_ref, cells_ref) = refs[:CHUNKS], refs[CHUNKS:]
    pair = pl.program_id(0)
    last = last_ref[:, slab(pair)]
    blocks = natural(at_pair(mix_refs, pair))
    lay_out(blocks, mix_even_ref, None)
    width = len(blocks) * HEAD
    span = cells_ref.shape[1]
    lags = span - LANES
    gains = gain_ref[:, slab(pair)]
    for half in range(2):
        mix = mix_even_ref[half].T
        carry = None
        for lag_slot in range(slots):
            slot, head = slots - 1 - lag_slot, 2 * pair + half
            if slot % 2 == 0:
                data = patched(even_ref, head, half, slot, slots, width, last)
            else:
                data = window(even_ref, odd_ref, head, slot, width)
            cross = jnp.dot(data, mix, preferred_element_type=jnp.float32)
            at = 2 * lag_slot * LANES
            upper, lower = cross[:LANES], cross[LANES:]
            if carry is not None:
                cells_ref[:, at - LANES : at] = carry + lower[:, :LANES]
            cells_ref[:, at : at + LANES] = upper[:, :LANES] + lower[:, LANES:]
            carry = upper[:, LANES:]
        total = cells_ref[0:8, :]
        for group in range(1, LANES // 8):
            total += pltpu.roll(cells_ref[8 * group : 8 * group + 8, :], span - 8 * group, 1)
        row = lax.broadcasted_iota(jnp.int32, (8, span), 0)
        for bit in (1, 2, 4):
            total = jnp.where((row & bit) != 0, pltpu.roll(total, span - bit, 1), total)
        sums = jnp.concatenate(
            [
                jnp.sum(total, axis=0, keepdims=True)[:, :lags],
                gains if half == 0 else pltpu.roll(gains, HEAD, 1),
            ],
            axis=1,
        )
        tall = min(8, out_ref.shape[0])
        row = 2 * pair + half
        group = pl.ds(pl.multiple_of(row // tall * tall, tall), tall)
        here = lax.broadcasted_iota(jnp.int32, (tall, out_ref.shape[1]), 0) == lax.rem(row, tall)
        out_ref[group, :] = jnp.where(here, sums, out_ref[group, :])


def kernel_grad_local(gain_sums, even, odd, last, mix_grad, lag):
    rows, width = len(mix_grad) * TILE, last.shape[1]
    pairs = width // LANES
    slots = 1 + 2 * lag // TILE
    operands = held(gain_sums, even, odd, last, *mix_grad)
    return pl.pallas_call(
        functools.partial(kernel_grad_body, slots),
        grid=(pairs,),
        in_specs=[VMEM] * len(operands),
        out_specs=VMEM,
        out_shape=pltpu.VMEM((2 * pairs, 2 * lag + LANES), jnp.float32),
        scratch_shapes=[
            pltpu.VMEM((2, TILE, rows // TILE * HEAD), jnp.bfloat16),
            pltpu.VMEM((LANES, 2 * lag + LANES), jnp.float32),
        ],
        compiler_params=params(8),
        cost_estimate=cost(product_flops(rows, width, lag), 8 * rows * width),
        name="kernel_grad",
    )(*operands)


def value_grad_body(slots, band_ref, *refs):
    own_refs, near_refs, refs = refs[:CHUNKS], refs[CHUNKS : 2 * CHUNKS], refs[2 * CHUNKS :]
    far_refs, (out_ref, first_ref, even_ref, odd_ref) = refs[: CHUNKS - 1], refs[CHUNKS - 1 :]
    pair = pl.program_id(0)
    own = natural(at_pair(own_refs, pair))
    blocks = extended(own, at_pair(near_refs, pair), at_pair(far_refs, pair))
    lay_out(blocks, even_ref, odd_ref)
    width = len(own) * HEAD
    results = [
        band_product(band_ref, 2 * pair + half, even_ref, odd_ref, half, slots, width)
        for half in range(2)
    ]
    blocks = token_blocks(*results)
    first_ref[:, slab(pair)] = jnp.where(odd_device(), blocks[-1], blocks[0])
    for index, block in enumerate(blocks):
        out_ref[index * TILE : (index + 1) * TILE, :] = block.astype(out_ref.dtype)


def value_grad_of(band, own, near, far, lag):
    rows, width = len(own) * TILE, own[0].shape[1]
    slots = 1 + 2 * lag // TILE
    operands = held(band, *own, *near, *far)
    return pl.pallas_call(
        functools.partial(value_grad_body, slots),
        grid=(width // LANES,),
        in_specs=[VMEM] * len(operands),
        out_specs=[pl.BlockSpec((rows, LANES), lambda g: (0, g)), VMEM],
        out_shape=[
            jax.ShapeDtypeStruct((rows, width), jnp.bfloat16),
            pltpu.VMEM((TILE, width), jnp.float32),
        ],
        scratch_shapes=layout_scratch(rows, lag),
        compiler_params=params(10),
        cost_estimate=cost(product_flops(rows, width, lag), 12 * rows * width),
        name="value_grad",
    )(*operands)


def value_grad_last_body(band_ref, last_ref, first_ref, rest_ref, out_ref, block_ref, sem):
    pair = pl.program_id(0)
    lanes = slab(pair)
    block = first_ref[:, lanes] + last_term(band_ref, pair, last_ref[:, lanes])
    block_ref[:, lanes] = block.astype(block_ref.dtype)

    @pl.when(pair == pl.num_programs(0) - 1)
    def _():
        copy = pltpu.make_async_copy(block_ref, out_ref.at[pl.ds(own_row(0), TILE), :], sem)
        copy.start()
        copy.wait()


def value_grad_last(band, last, first, rest):
    width = first.shape[1]
    operands = held(band, last, first)
    return pl.pallas_call(
        value_grad_last_body,
        grid=(width // LANES,),
        in_specs=[VMEM] * len(operands) + [pl.BlockSpec(memory_space=pl.ANY)],
        out_specs=pl.BlockSpec(memory_space=pl.ANY),
        out_shape=jax.ShapeDtypeStruct(rest.shape, rest.dtype),
        input_output_aliases={len(operands): 0},
        scratch_shapes=[pltpu.VMEM((TILE, width), jnp.bfloat16), pltpu.SemaphoreType.DMA(())],
        compiler_params=params(6),
        cost_estimate=cost(8 * TILE * TILE * width, 6 * TILE * width),
        name="value_grad_last",
    )(*operands, rest)


def swapped(chunk):
    count = lax.axis_size("seq")
    return lax.ppermute(chunk, "seq", [(i, i ^ 1) for i in range(count)])


def relayed(chunk):
    count = lax.axis_size("seq")
    pairs = [(i, i + 2) if i % 2 == 0 else (i, i - 2) for i in range(count)]
    return lax.ppermute(chunk, "seq", [(i, j) for i, j in pairs if 0 <= j < count])


def terms_over_bits(value, bits):
    count = lax.axis_size("seq")
    terms = []
    for mask in range(1, 1 << len(bits)):
        flip = sum(1 << bit for at, bit in enumerate(bits) if mask >> at & 1)
        terms.append(lax.ppermute(value, "seq", [(i, i ^ flip) for i in range(count)]))
    return terms


def sum_over(value, axis):
    count = lax.axis_size(axis)
    if count & (count - 1):
        return lax.psum(value, axis)
    for bit in range(count.bit_length() - 1):
        value += lax.ppermute(value, axis, [(i, i ^ (1 << bit)) for i in range(count)])
    return value


def on_device(gate_acts, value_acts, kernel, norm_gain, out_grad):
    rows, width = value_acts.shape
    heads = kernel.shape[0]
    lag = kernel.shape[1] // 2
    count = lax.axis_size("seq")
    assert width == heads * HEAD and rows == lag == CHUNKS * TILE
    assert count & (count - 1) == 0
    full_width = width * lax.axis_size("chan")
    gain = norm_gain.reshape(1, width)
    taps = kernel.astype(jnp.float32)

    ahead, behind = lax.optimization_barrier(
        (band_rows(taps[:, ::-1], 1, TILE - 1), band_rows(taps, 0, TILE))
    )
    band = bands(ahead)
    *chunks, last = split(value_acts)
    near = [swapped(chunk) for chunk in [*chunks, after(last, band)]]
    far = [relayed(chunk) for chunk in near]
    mixed, sums, even, odd = forward(
        band, value_acts, near, far[:-1], gate_acts, out_grad, gain, lag
    )
    first, sums = forward_last(band, far[-1], gate_acts, out_grad, gain, mixed, sums)
    sums = sum_over(sums, "chan")
    args = (mixed, first, gate_acts, out_grad, gain)
    mix_grad, gain_sums = mix_grad_of(full_width, sums, *args)

    grad_near = [swapped(part) for part in mix_grad]
    totals = kernel_grad_local(gain_sums, even, odd, far[-1], mix_grad, lag)
    normed, gate_grad = norm(full_width, after(sums, grad_near[0]), *args)
    back_band = bands(after(behind, grad_near[1]))
    grad_near[0], totals = lax.optimization_barrier((grad_near[0], totals))
    grad_near[3], normed, gate_grad, back_band = lax.optimization_barrier(
        (grad_near[3], normed, gate_grad, back_band)
    )
    bits = list(range(count.bit_length() - 1))
    totals += terms_over_bits(totals, bits[2:3])[0]
    for chunk in (1, 2):
        grad_near[chunk], totals = lax.optimization_barrier((grad_near[chunk], totals))
    for bit in bits[3:]:
        totals += terms_over_bits(totals, [bit])[0]
    grad_far = [relayed(chunk) for chunk in grad_near]
    totals, *grad_far[:2] = lax.optimization_barrier((totals, *grad_far[:2]))
    value_grad, first = value_grad_of(back_band, mix_grad, grad_near, grad_far[:-1], lag)
    totals, first = lax.optimization_barrier((totals, first))
    terms = [totals] + terms_over_bits(totals, bits[:2])
    value_grad = value_grad_last(back_band, grad_far[-1], first, value_grad)
    value_grad, *terms = lax.optimization_barrier((value_grad, *terms))
    totals = sum(terms[1:], terms[0])
    tokens = rows * count
    kernel_grad = totals[:, : 2 * lag] / math.sqrt(tokens * HEAD)
    gain_grad = totals[:, 2 * lag : 2 * lag + HEAD].reshape(width) / math.sqrt(tokens)
    return (normed, gate_grad, value_grad, kernel_grad, gain_grad)


def solution(mesh):
    placed = (P("seq", "chan"), P("seq", "chan"), P("chan", None), P("chan"), P("seq", "chan"))
    return jax.shard_map(
        on_device,
        mesh=mesh,
        in_specs=placed,
        out_specs=(
            P("seq", "chan"),
            P("seq", "chan"),
            P("seq", "chan"),
            P("chan", None),
            P("chan"),
        ),
        check_vma=False,
    )
```

```python
import functools
import math

import jax
import jax.numpy as jnp
from jax import lax
from jax.experimental import pallas as pl
from jax.experimental.pallas import tpu as pltpu
from jax.sharding import PartitionSpec as P

norm_eps = 1e-06
TILE = 256
LANES = 128
HEAD = 64
CHUNKS = 4
MIB = 1 << 20


def params(mib):
    return pltpu.CompilerParams(
        vmem_limit_bytes=mib * MIB, dimension_semantics=("arbitrary",)
    )


def cost(flops, moved):
    return pl.CostEstimate(flops=flops, bytes_accessed=moved, transcendentals=0)


def lane_iota(rows):
    return lax.broadcasted_iota(jnp.int32, (rows, LANES), 1)


def slab(pair):
    return pl.ds(pl.multiple_of(pair * LANES, LANES), LANES)


def odd_device():
    return lax.axis_index("seq") % 2 == 1


def own_row(chunk):
    row = jnp.where(odd_device(), (CHUNKS - 1 - chunk) * TILE, chunk * TILE)
    return pl.multiple_of(row, TILE)


VMEM = pl.BlockSpec(memory_space=pltpu.VMEM)


def held(*arrays):
    return [pltpu.with_memory_space_constraint(array, pltpu.VMEM) for array in arrays]


def after(value, *others):
    return lax.optimization_barrier((value, *others))[0]


def band_body(row_ref, band_ref):
    tiles = row_ref.shape[2] // LANES
    step = pl.program_id(0)
    upper = lane_iota(LANES) >= lax.broadcasted_iota(jnp.int32, (LANES, LANES), 0)
    for half in range(2):
        head = 2 * step + half
        before = jnp.zeros((LANES, LANES), jnp.float32)
        band_ref[head, :, :LANES] = before.astype(band_ref.dtype)
        for tile in range(tiles):
            segment = row_ref[step, half : half + 1, tile * LANES : (tile + 1) * LANES]
            turned = pltpu.roll(
                jnp.broadcast_to(segment, (LANES, LANES)), 0, 1, stride=1, stride_axis=0
            )
            cell = jnp.where(upper, turned, before)
            band_ref[head, :, (tile + 1) * LANES : (tile + 2) * LANES] = cell.astype(
                band_ref.dtype
            )
            before = turned


def band_rows(taps, low, high):
    heads = taps.shape[0]
    return jnp.pad(taps, ((0, 0), (low, high))).reshape(heads // 2, 2, -1)


def bands(rows):
    heads, length = 2 * rows.shape[0], rows.shape[2]
    return pl.pallas_call(
        band_body,
        grid=(heads // 2,),
        in_specs=[VMEM],
        out_specs=VMEM,
        out_shape=pltpu.VMEM((heads, LANES, length + LANES), jnp.bfloat16),
        compiler_params=params(4),
        cost_estimate=cost(heads * LANES * length, 2 * heads * LANES * length),
        name="bands",
    )(*held(rows))


def natural(chunks):
    return [jnp.where(odd_device(), *pair) for pair in zip(chunks[::-1], chunks)]


def extended(own, near, far):
    if len(far) < CHUNKS:
        far = [*far, jnp.zeros_like(near[0])]
    odd = odd_device()
    left = [jnp.where(odd, n, f) for n, f in zip(near, far[::-1])]
    right = [jnp.where(odd, f, n) for n, f in zip(near[::-1], far)]
    return left + own + right


def at_pair(refs, pair):
    return [ref[:, slab(pair)] for ref in refs]


def rows_of(ref, pair):
    return [ref[at : at + TILE, slab(pair)] for at in range(0, ref.shape[0], TILE)]


def layout_scratch(rows, lag, heads=2):
    wide = (rows + 2 * lag) // TILE * HEAD
    return [
        pltpu.VMEM((heads, TILE, wide), jnp.bfloat16),
        pltpu.VMEM((heads, TILE, wide - LANES), jnp.bfloat16),
    ]


def lay_out(blocks, even_ref, odd_ref, base=0):
    low = lane_iota(TILE) < HEAD
    turned = [pltpu.roll(block, HEAD, 1) for block in blocks]
    for tile in range(len(blocks) // 2):
        cols = slice(tile * LANES, (tile + 1) * LANES)
        first, second = 2 * tile, 2 * tile + 1
        even_ref[base, :, cols] = jnp.where(low, blocks[first], turned[second])
        even_ref[base + 1, :, cols] = jnp.where(low, turned[first], blocks[second])
        if odd_ref is not None and second + 1 < len(blocks):
            odd_ref[base, :, cols] = jnp.where(low, blocks[second], turned[second + 1])
            odd_ref[base + 1, :, cols] = jnp.where(low, turned[second], blocks[second + 1])


def window(even_ref, odd_ref, head, start, width):
    if start % 2 == 0:
        return even_ref[head, :, start * HEAD : start * HEAD + width]
    return odd_ref[head, :, (start - 1) * HEAD : (start - 1) * HEAD + width]


def band_product(band_ref, band_head, even_ref, odd_ref, head, slots, width):
    span = slots * TILE
    tile = jnp.concatenate(
        [band_ref[band_head, :, LANES : LANES + span], band_ref[band_head, :, :span]], axis=0
    )
    data = jnp.concatenate(
        [window(even_ref, odd_ref, head, slot, width) for slot in range(slots)], axis=0
    )
    return jnp.dot(tile, data, preferred_element_type=jnp.float32)


def token_blocks(first, second):
    low = lane_iota(TILE) < HEAD
    blocks = []
    for tile in range(first.shape[1] // LANES):
        cols = slice(tile * LANES, (tile + 1) * LANES)
        one, two = first[:, cols], second[:, cols]
        blocks.append(jnp.where(low, one, pltpu.roll(two, HEAD, 1)))
        blocks.append(jnp.where(low, pltpu.roll(one, HEAD, 1), two))
    return blocks


def last_term(band_ref, pair, last):
    low = lane_iota(TILE) < HEAD
    at = jnp.where(odd_device(), band_ref.shape[2] - LANES - TILE, 0)
    parts = []
    for half in range(2):
        head = 2 * pair + half
        tile = jnp.concatenate(
            [
                band_ref[head, :, pl.ds(pl.multiple_of(at + LANES, LANES), TILE)],
                band_ref[head, :, pl.ds(pl.multiple_of(at, LANES), TILE)],
            ],
            axis=0,
        )
        parts.append(jnp.dot(tile, last, preferred_element_type=jnp.float32))
    return jnp.where(low, *parts)


def split_body(value_ref, *refs):
    chunk_refs, sems = refs[:CHUNKS], refs[CHUNKS]
    copies = []
    for chunk, ref in enumerate(chunk_refs):
        copies.append(
            pltpu.make_async_copy(
                value_ref.at[pl.ds(own_row(chunk), TILE), :], ref, sems.at[chunk]
            )
        )
        copies[-1].start()
    for copy in copies:
        copy.wait()


def split(value):
    rows, width = value.shape
    return pl.pallas_call(
        split_body,
        in_specs=[pl.BlockSpec(memory_space=pltpu.HBM)],
        out_specs=[VMEM] * CHUNKS,
        out_shape=[pltpu.VMEM((TILE, width), value.dtype)] * CHUNKS,
        scratch_shapes=[pltpu.SemaphoreType.DMA((CHUNKS,))],
        compiler_params=pltpu.CompilerParams(vmem_limit_bytes=2 * MIB),
        cost_estimate=cost(0, 4 * rows * width),
        name="split",
    )(pltpu.with_memory_space_constraint(value, pltpu.HBM))


def product_flops(rows, width, lag):
    return 2 * (width // HEAD) * TILE * (TILE + 2 * lag) * rows // TILE * HEAD


def token_sums(square_ref, inner_ref, sums_ref, start):
    for at in range(0, square_ref.shape[0], LANES):
        rows = slice(at, at + LANES)
        cols = pl.ds(pl.multiple_of(start + at, LANES), LANES)
        sums_ref[0:1, cols] = jnp.sum(square_ref[rows, :].T, axis=0, keepdims=True)
        sums_ref[1:2, cols] = jnp.sum(inner_ref[rows, :].T, axis=0, keepdims=True)


def add_sums(mixed, gate, grad, gain, square_ref, inner_ref, at):
    hidden = gate.astype(jnp.float32) * mixed
    square_ref[at, :] += hidden * hidden
    inner_ref[at, :] += gain * grad.astype(jnp.float32) * hidden


def forward_body(slots, band_ref, own_ref, gate_ref, grad_ref, gain_ref, *refs):
    near_refs, far_refs, refs = refs[:CHUNKS], refs[CHUNKS : 2 * CHUNKS - 1], refs[2 * CHUNKS - 1 :]
    mixed_ref, sums_ref, even_ref, odd_ref, square_ref, inner_ref = refs
    pair = pl.program_id(0)
    heads = (2 * pair, 2 * pair + 1)

    @pl.when(pair == 0)
    def _():
        square_ref[...] = jnp.zeros_like(square_ref)
        inner_ref[...] = jnp.zeros_like(inner_ref)

    blocks = extended(rows_of(own_ref, pair), at_pair(near_refs, pair), at_pair(far_refs, pair))
    lay_out(blocks, even_ref, odd_ref, 2 * pair)
    width = mixed_ref.shape[0] // TILE * HEAD
    results = [band_product(band_ref, h, even_ref, odd_ref, h, slots, width) for h in heads]
    lanes = slab(pair)
    for index, mixed in enumerate(token_blocks(*results)):
        at = slice(index * TILE, (index + 1) * TILE)
        mixed_ref[at, lanes] = mixed
        add_sums(
            mixed, gate_ref[at, lanes], grad_ref[at, lanes], gain_ref[:, lanes], square_ref, inner_ref, at
        )

    @pl.when(pair == pl.num_programs(0) - 1)
    def _():
        token_sums(square_ref, inner_ref, sums_ref, 0)


def forward(band, own, near, far, gate, grad, gain, lag):
    rows, width = gate.shape
    slots = 1 + 2 * lag // TILE
    operands = held(band, own, gate, grad, gain, *near, *far)
    return pl.pallas_call(
        functools.partial(forward_body, slots),
        grid=(width // LANES,),
        in_specs=[VMEM] * len(operands),
        out_specs=[VMEM] * 4,
        out_shape=[
            pltpu.VMEM((rows, width), jnp.float32),
            pltpu.VMEM((2, rows), jnp.float32),
            *layout_scratch(rows, lag, width // HEAD),
        ],
        scratch_shapes=[pltpu.VMEM((rows, LANES), jnp.float32)] * 2,
        compiler_params=params(9),
        cost_estimate=cost(product_flops(rows, width, lag), 16 * rows * width),
        name="forward",
    )(*operands)


def forward_last_body(band_ref, last_ref, gate_ref, grad_ref, gain_ref, mixed_ref, sums_ref, *refs):
    first_ref, out_ref, square_ref, inner_ref = refs
    pair = pl.program_id(0)

    @pl.when(pair == 0)
    def _():
        square_ref[...] = jnp.zeros_like(square_ref)
        inner_ref[...] = jnp.zeros_like(inner_ref)
        out_ref[...] = sums_ref[...]

    lanes, rows = slab(pair), pl.ds(own_row(0), TILE)
    mixed = mixed_ref[rows, lanes] + last_term(band_ref, pair, last_ref[:, lanes])
    first_ref[:, lanes] = mixed
    add_sums(
        mixed,
        gate_ref[rows, lanes],
        grad_ref[rows, lanes],
        gain_ref[:, lanes],
        square_ref,
        inner_ref,
        slice(None),
    )

    @pl.when(pair == pl.num_programs(0) - 1)
    def _():
        token_sums(square_ref, inner_ref, out_ref, own_row(0))


def forward_last(band, last, gate, grad, gain, mixed, sums):
    rows, width = gate.shape
    operands = held(band, last, gate, grad, gain, mixed, sums)
    return pl.pallas_call(
        forward_last_body,
        grid=(width // LANES,),
        in_specs=[VMEM] * len(operands),
        out_specs=[VMEM] * 2,
        out_shape=[
            pltpu.VMEM((TILE, width), jnp.float32),
            pltpu.VMEM((2, rows), jnp.float32),
        ],
        scratch_shapes=[pltpu.VMEM((TILE, LANES), jnp.float32)] * 2,
        compiler_params=params(6),
        cost_estimate=cost(8 * TILE * TILE * width, 6 * TILE * width),
        name="forward_last",
    )(*operands)


def token_columns(full_width, sums_ref, tokens):
    scale = lax.rsqrt(sums_ref[0:1, tokens] / full_width + norm_eps)
    pull = scale * scale * sums_ref[1:2, tokens] / full_width
    return (
        jnp.broadcast_to(scale, (LANES, LANES)).T,
        jnp.broadcast_to(pull, (LANES, LANES)).T,
    )


def mix_grad_body(full_width, sums_ref, mixed_ref, first_ref, gate_ref, grad_ref, gain_ref, *refs):
    out_refs, gain_grad_ref, total_ref = refs[:-2], refs[-2], refs[-1]
    total_ref[...] = jnp.zeros_like(total_ref)
    for chunk, out_ref in enumerate(out_refs):
        for at in range(0, TILE, LANES):
            tokens = pl.ds(pl.multiple_of(own_row(chunk) + at, LANES), LANES)
            rows = slice(at, at + LANES)
            scale, pull = token_columns(full_width, sums_ref, tokens)
            for lane in range(0, mixed_ref.shape[1], LANES):
                cols = slice(lane, lane + LANES)
                gate = gate_ref[tokens, cols].astype(jnp.float32)
                grad = grad_ref[tokens, cols].astype(jnp.float32)
                mixed = mixed_ref[tokens, cols] if chunk else first_ref[rows, cols]
                hidden = gate * mixed
                hidden_grad = scale * (gain_ref[:, cols] * grad - hidden * pull)
                out_ref[rows, cols] = (hidden_grad * gate).astype(out_ref.dtype)
                total_ref[:, cols] += jnp.sum(
                    (grad * (hidden * scale)).reshape(LANES // 8, 8, LANES), axis=0
                )
    gain_grad_ref[...] = jnp.sum(total_ref[...], axis=0, keepdims=True)


def mix_grad_of(full_width, *operands):
    rows, width = operands[1].shape
    operands = held(*operands)
    *chunks, gain_sums = pl.pallas_call(
        functools.partial(mix_grad_body, full_width),
        in_specs=[VMEM] * len(operands),
        out_specs=[VMEM] * (CHUNKS + 1),
        out_shape=[pltpu.VMEM((TILE, width), jnp.bfloat16)] * CHUNKS
        + [pltpu.VMEM((1, width), jnp.float32)],
        scratch_shapes=[pltpu.VMEM((8, width), jnp.float32)],
        compiler_params=pltpu.CompilerParams(vmem_limit_bytes=4 * MIB),
        cost_estimate=cost(14 * rows * width, 10 * rows * width),
        name="mix_grad",
    )(*operands)
    return chunks, gain_sums


def norm_body(full_width, sums_ref, mixed_ref, first_ref, gate_ref, grad_ref, gain_ref, *refs):
    normed_ref, gate_grad_ref = refs
    start = pl.program_id(0) * LANES
    tokens = pl.ds(pl.multiple_of(start, LANES), LANES)
    within = pl.ds(pl.multiple_of(lax.rem(start, TILE), LANES), LANES)
    first = start // TILE == own_row(0) // TILE
    scale, pull = token_columns(full_width, sums_ref, tokens)
    for lane in range(0, mixed_ref.shape[1], LANES):
        cols = slice(lane, lane + LANES)
        gain = gain_ref[:, cols]
        gate = gate_ref[tokens, cols].astype(jnp.float32)
        mixed = jnp.where(first, first_ref[within, cols], mixed_ref[tokens, cols])
        grad = grad_ref[tokens, cols].astype(jnp.float32)
        hidden = gate * mixed
        normed_ref[:, cols] = (hidden * scale * gain).astype(normed_ref.dtype)
        hidden_grad = scale * (gain * grad - hidden * pull)
        gate_grad_ref[:, cols] = (hidden_grad * mixed).astype(gate_grad_ref.dtype)


def norm(full_width, *operands):
    rows, width = operands[1].shape
    operands = held(*operands)
    big = jax.ShapeDtypeStruct((rows, width), jnp.bfloat16)
    return pl.pallas_call(
        functools.partial(norm_body, full_width),
        grid=(rows // LANES,),
        in_specs=[VMEM] * len(operands),
        out_specs=[pl.BlockSpec((LANES, width), lambda g: (g, 0))] * 2,
        out_shape=[big, big],
        compiler_params=params(6),
        cost_estimate=cost(14 * rows * width, 12 * rows * width),
        name="norm",
    )(*operands)


def patched(even_ref, head, half, slot, slots, width, last):
    data = even_ref[head, :, slot * HEAD : slot * HEAD + width]
    low = lane_iota(TILE) < HEAD
    turned = pltpu.roll(last, HEAD, 1)
    if slot == 0:
        tile = data[:, :LANES]
        put = jnp.where(low, last if half == 0 else turned, tile)
        return jnp.concatenate([jnp.where(odd_device(), tile, put), data[:, LANES:]], axis=1)
    if slot == slots - 1:
        tile = data[:, width - LANES :]
        put = jnp.where(low, tile, turned if half == 0 else last)
        return jnp.concatenate([data[:, : width - LANES], jnp.where(odd_device(), put, tile)], axis=1)
    return data


def kernel_grad_body(slots, gain_ref, even_ref, odd_ref, last_ref, *refs):
    mix_refs, (out_ref, mix_even_ref, cells_ref) = refs[:CHUNKS], refs[CHUNKS:]
    pair = pl.program_id(0)
    last = last_ref[:, slab(pair)]
    blocks = natural(at_pair(mix_refs, pair))
    lay_out(blocks, mix_even_ref, None)
    width = len(blocks) * HEAD
    span = cells_ref.shape[1]
    lags = span - LANES
    gains = gain_ref[:, slab(pair)]
    for half in range(2):
        mix = mix_even_ref[half].T
        carry = None
        for lag_slot in range(slots):
            slot, head = slots - 1 - lag_slot, 2 * pair + half
            if slot % 2 == 0:
                data = patched(even_ref, head, half, slot, slots, width, last)
            else:
                data = window(even_ref, odd_ref, head, slot, width)
            cross = jnp.dot(data, mix, preferred_element_type=jnp.float32)
            at = 2 * lag_slot * LANES
            upper, lower = cross[:LANES], cross[LANES:]
            if carry is not None:
                cells_ref[:, at - LANES : at] = carry + lower[:, :LANES]
            cells_ref[:, at : at + LANES] = upper[:, :LANES] + lower[:, LANES:]
            carry = upper[:, LANES:]
        total = cells_ref[0:8, :]
        for group in range(1, LANES // 8):
            total += pltpu.roll(cells_ref[8 * group : 8 * group + 8, :], span - 8 * group, 1)
        row = lax.broadcasted_iota(jnp.int32, (8, span), 0)
        for bit in (1, 2, 4):
            total = jnp.where((row & bit) != 0, pltpu.roll(total, span - bit, 1), total)
        sums = jnp.concatenate(
            [
                jnp.sum(total, axis=0, keepdims=True)[:, :lags],
                gains if half == 0 else pltpu.roll(gains, HEAD, 1),
            ],
            axis=1,
        )
        tall = min(8, out_ref.shape[0])
        row = 2 * pair + half
        group = pl.ds(pl.multiple_of(row // tall * tall, tall), tall)
        here = lax.broadcasted_iota(jnp.int32, (tall, out_ref.shape[1]), 0) == lax.rem(row, tall)
        out_ref[group, :] = jnp.where(here, sums, out_ref[group, :])


def kernel_grad_local(gain_sums, even, odd, last, mix_grad, lag):
    rows, width = len(mix_grad) * TILE, last.shape[1]
    pairs = width // LANES
    slots = 1 + 2 * lag // TILE
    operands = held(gain_sums, even, odd, last, *mix_grad)
    return pl.pallas_call(
        functools.partial(kernel_grad_body, slots),
        grid=(pairs,),
        in_specs=[VMEM] * len(operands),
        out_specs=VMEM,
        out_shape=pltpu.VMEM((2 * pairs, 2 * lag + LANES), jnp.float32),
        scratch_shapes=[
            pltpu.VMEM((2, TILE, rows // TILE * HEAD), jnp.bfloat16),
            pltpu.VMEM((LANES, 2 * lag + LANES), jnp.float32),
        ],
        compiler_params=params(8),
        cost_estimate=cost(product_flops(rows, width, lag), 8 * rows * width),
        name="kernel_grad",
    )(*operands)


def value_grad_body(slots, band_ref, *refs):
    own_refs, near_refs, refs = refs[:CHUNKS], refs[CHUNKS : 2 * CHUNKS], refs[2 * CHUNKS :]
    far_refs, (out_ref, first_ref, even_ref, odd_ref) = refs[: CHUNKS - 1], refs[CHUNKS - 1 :]
    pair = pl.program_id(0)
    own = natural(at_pair(own_refs, pair))
    blocks = extended(own, at_pair(near_refs, pair), at_pair(far_refs, pair))
    lay_out(blocks, even_ref, odd_ref)
    width = len(own) * HEAD
    results = [
        band_product(band_ref, 2 * pair + half, even_ref, odd_ref, half, slots, width)
        for half in range(2)
    ]
    blocks = token_blocks(*results)
    first_ref[:, slab(pair)] = jnp.where(odd_device(), blocks[-1], blocks[0])
    for index, block in enumerate(blocks):
        out_ref[index * TILE : (index + 1) * TILE, :] = block.astype(out_ref.dtype)


def value_grad_of(band, own, near, far, lag):
    rows, width = len(own) * TILE, own[0].shape[1]
    slots = 1 + 2 * lag // TILE
    operands = held(band, *own, *near, *far)
    return pl.pallas_call(
        functools.partial(value_grad_body, slots),
        grid=(width // LANES,),
        in_specs=[VMEM] * len(operands),
        out_specs=[pl.BlockSpec((rows, LANES), lambda g: (0, g)), VMEM],
        out_shape=[
            jax.ShapeDtypeStruct((rows, width), jnp.bfloat16),
            pltpu.VMEM((TILE, width), jnp.float32),
        ],
        scratch_shapes=layout_scratch(rows, lag),
        compiler_params=params(10),
        cost_estimate=cost(product_flops(rows, width, lag), 12 * rows * width),
        name="value_grad",
    )(*operands)


def value_grad_last_body(band_ref, last_ref, first_ref, rest_ref, out_ref, block_ref, sem):
    pair = pl.program_id(0)
    lanes = slab(pair)
    block = first_ref[:, lanes] + last_term(band_ref, pair, last_ref[:, lanes])
    block_ref[:, lanes] = block.astype(block_ref.dtype)

    @pl.when(pair == pl.num_programs(0) - 1)
    def _():
        copy = pltpu.make_async_copy(block_ref, out_ref.at[pl.ds(own_row(0), TILE), :], sem)
        copy.start()
        copy.wait()


def value_grad_last(band, last, first, rest):
    width = first.shape[1]
    operands = held(band, last, first)
    return pl.pallas_call(
        value_grad_last_body,
        grid=(width // LANES,),
        in_specs=[VMEM] * len(operands) + [pl.BlockSpec(memory_space=pl.ANY)],
        out_specs=pl.BlockSpec(memory_space=pl.ANY),
        out_shape=jax.ShapeDtypeStruct(rest.shape, rest.dtype),
        input_output_aliases={len(operands): 0},
        scratch_shapes=[pltpu.VMEM((TILE, width), jnp.bfloat16), pltpu.SemaphoreType.DMA(())],
        compiler_params=params(6),
        cost_estimate=cost(8 * TILE * TILE * width, 6 * TILE * width),
        name="value_grad_last",
    )(*operands, rest)


def swapped(chunk):
    count = lax.axis_size("seq")
    return lax.ppermute(chunk, "seq", [(i, i ^ 1) for i in range(count)])


def relayed(chunk):
    count = lax.axis_size("seq")
    pairs = [(i, i + 2) if i % 2 == 0 else (i, i - 2) for i in range(count)]
    return lax.ppermute(chunk, "seq", [(i, j) for i, j in pairs if 0 <= j < count])


def terms_over_bits(value, bits):
    count = lax.axis_size("seq")
    terms = []
    for mask in range(1, 1 << len(bits)):
        flip = sum(1 << bit for at, bit in enumerate(bits) if mask >> at & 1)
        terms.append(lax.ppermute(value, "seq", [(i, i ^ flip) for i in range(count)]))
    return terms


def sum_over(value, axis):
    count = lax.axis_size(axis)
    if count & (count - 1):
        return lax.psum(value, axis)
    for bit in range(count.bit_length() - 1):
        value += lax.ppermute(value, axis, [(i, i ^ (1 << bit)) for i in range(count)])
    return value


def on_device(gate_acts, value_acts, kernel, norm_gain, out_grad):
    rows, width = value_acts.shape
    heads = kernel.shape[0]
    lag = kernel.shape[1] // 2
    count = lax.axis_size("seq")
    assert width == heads * HEAD and rows == lag == CHUNKS * TILE
    assert count & (count - 1) == 0
    full_width = width * lax.axis_size("chan")
    gain = norm_gain.reshape(1, width)
    taps = kernel.astype(jnp.float32)

    ahead, behind = lax.optimization_barrier(
        (band_rows(taps[:, ::-1], 1, TILE - 1), band_rows(taps, 0, TILE))
    )
    band = bands(ahead)
    *chunks, last = split(value_acts)
    near = [swapped(chunk) for chunk in [*chunks, after(last, band)]]
    far = [relayed(chunk) for chunk in near]
    mixed, sums, even, odd = forward(
        band, value_acts, near, far[:-1], gate_acts, out_grad, gain, lag
    )
    first, sums = forward_last(band, far[-1], gate_acts, out_grad, gain, mixed, sums)
    sums = sum_over(sums, "chan")
    args = (mixed, first, gate_acts, out_grad, gain)
    mix_grad, gain_sums = mix_grad_of(full_width, sums, *args)

    grad_near = [swapped(part) for part in mix_grad]
    totals = kernel_grad_local(gain_sums, even, odd, far[-1], mix_grad, lag)
    normed, gate_grad = norm(full_width, after(sums, grad_near[0]), *args)
    back_band = bands(after(behind, grad_near[1]))
    grad_near[0], totals = lax.optimization_barrier((grad_near[0], totals))
    grad_near[3], normed, gate_grad, back_band = lax.optimization_barrier(
        (grad_near[3], normed, gate_grad, back_band)
    )
    bits = list(range(count.bit_length() - 1))
    totals += terms_over_bits(totals, bits[2:3])[0]
    for chunk in (1, 2):
        grad_near[chunk], totals = lax.optimization_barrier((grad_near[chunk], totals))
    for bit in bits[3:]:
        totals += terms_over_bits(totals, [bit])[0]
    grad_far = [relayed(chunk) for chunk in grad_near]
    totals, *grad_far[:2] = lax.optimization_barrier((totals, *grad_far[:2]))
    value_grad, first = value_grad_of(back_band, mix_grad, grad_near, grad_far[:-1], lag)
    value_grad = value_grad_last(back_band, grad_far[-1], first, value_grad)
    totals, value_grad = lax.optimization_barrier((totals, value_grad))
    terms = [totals] + terms_over_bits(totals, bits[:2])
    totals = sum(terms[1:], terms[0])
    tokens = rows * count
    kernel_grad = totals[:, : 2 * lag] / math.sqrt(tokens * HEAD)
    gain_grad = totals[:, 2 * lag : 2 * lag + HEAD].reshape(width) / math.sqrt(tokens)
    return (normed, gate_grad, value_grad, kernel_grad, gain_grad)


def solution(mesh):
    placed = (P("seq", "chan"), P("seq", "chan"), P("chan", None), P("chan"), P("seq", "chan"))
    return jax.shard_map(
        on_device,
        mesh=mesh,
        in_specs=placed,
        out_specs=(
            P("seq", "chan"),
            P("seq", "chan"),
            P("seq", "chan"),
            P("chan", None),
            P("chan"),
        ),
        check_vma=False,
    )
```

```python
import functools
import math

import jax
import jax.numpy as jnp
from jax import lax
from jax.experimental import pallas as pl
from jax.experimental.pallas import tpu as pltpu
from jax.sharding import PartitionSpec as P

norm_eps = 1e-06
TILE = 256
LANES = 128
HEAD = 64
CHUNKS = 4
MIB = 1 << 20


def params(mib):
    return pltpu.CompilerParams(
        vmem_limit_bytes=mib * MIB, dimension_semantics=("arbitrary",)
    )


def cost(flops, moved):
    return pl.CostEstimate(flops=flops, bytes_accessed=moved, transcendentals=0)


def lane_iota(rows):
    return lax.broadcasted_iota(jnp.int32, (rows, LANES), 1)


def slab(pair):
    return pl.ds(pl.multiple_of(pair * LANES, LANES), LANES)


def odd_device():
    return lax.axis_index("seq") % 2 == 1


def own_row(chunk):
    row = jnp.where(odd_device(), (CHUNKS - 1 - chunk) * TILE, chunk * TILE)
    return pl.multiple_of(row, TILE)


VMEM = pl.BlockSpec(memory_space=pltpu.VMEM)


def held(*arrays):
    return [pltpu.with_memory_space_constraint(array, pltpu.VMEM) for array in arrays]


def after(value, *others):
    return lax.optimization_barrier((value, *others))[0]


def band_body(row_ref, band_ref):
    tiles = row_ref.shape[2] // LANES
    step = pl.program_id(0)
    upper = lane_iota(LANES) >= lax.broadcasted_iota(jnp.int32, (LANES, LANES), 0)
    for half in range(2):
        head = 2 * step + half
        before = jnp.zeros((LANES, LANES), jnp.float32)
        band_ref[head, :, :LANES] = before.astype(band_ref.dtype)
        for tile in range(tiles):
            segment = row_ref[step, half : half + 1, tile * LANES : (tile + 1) * LANES]
            turned = pltpu.roll(
                jnp.broadcast_to(segment, (LANES, LANES)), 0, 1, stride=1, stride_axis=0
            )
            cell = jnp.where(upper, turned, before)
            band_ref[head, :, (tile + 1) * LANES : (tile + 2) * LANES] = cell.astype(
                band_ref.dtype
            )
            before = turned


def band_rows(taps, low, high):
    heads = taps.shape[0]
    return jnp.pad(taps, ((0, 0), (low, high))).reshape(heads // 2, 2, -1)


def bands(rows):
    heads, length = 2 * rows.shape[0], rows.shape[2]
    return pl.pallas_call(
        band_body,
        grid=(heads // 2,),
        in_specs=[VMEM],
        out_specs=VMEM,
        out_shape=pltpu.VMEM((heads, LANES, length + LANES), jnp.bfloat16),
        compiler_params=params(4),
        cost_estimate=cost(heads * LANES * length, 2 * heads * LANES * length),
        name="bands",
    )(*held(rows))


def natural(chunks):
    return [jnp.where(odd_device(), *pair) for pair in zip(chunks[::-1], chunks)]


def extended(own, near, far):
    if len(far) < CHUNKS:
        far = [*far, jnp.zeros_like(near[0])]
    odd = odd_device()
    left = [jnp.where(odd, n, f) for n, f in zip(near, far[::-1])]
    right = [jnp.where(odd, f, n) for n, f in zip(near[::-1], far)]
    return left + own + right


def at_pair(refs, pair):
    return [ref[:, slab(pair)] for ref in refs]


def rows_of(ref, pair):
    return [ref[at : at + TILE, slab(pair)] for at in range(0, ref.shape[0], TILE)]


def layout_scratch(rows, lag, heads=2):
    wide = (rows + 2 * lag) // TILE * HEAD
    return [
        pltpu.VMEM((heads, TILE, wide), jnp.bfloat16),
        pltpu.VMEM((heads, TILE, wide - LANES), jnp.bfloat16),
    ]


def lay_out(blocks, even_ref, odd_ref, base=0):
    low = lane_iota(TILE) < HEAD
    turned = [pltpu.roll(block, HEAD, 1) for block in blocks]
    for tile in range(len(blocks) // 2):
        cols = slice(tile * LANES, (tile + 1) * LANES)
        first, second = 2 * tile, 2 * tile + 1
        even_ref[base, :, cols] = jnp.where(low, blocks[first], turned[second])
        even_ref[base + 1, :, cols] = jnp.where(low, turned[first], blocks[second])
        if odd_ref is not None and second + 1 < len(blocks):
            odd_ref[base, :, cols] = jnp.where(low, blocks[second], turned[second + 1])
            odd_ref[base + 1, :, cols] = jnp.where(low, turned[second], blocks[second + 1])


def window(even_ref, odd_ref, head, start, width):
    if start % 2 == 0:
        return even_ref[head, :, start * HEAD : start * HEAD + width]
    return odd_ref[head, :, (start - 1) * HEAD : (start - 1) * HEAD + width]


def band_product(band_ref, band_head, even_ref, odd_ref, head, slots, width):
    span = slots * TILE
    tile = jnp.concatenate(
        [band_ref[band_head, :, LANES : LANES + span], band_ref[band_head, :, :span]], axis=0
    )
    data = jnp.concatenate(
        [window(even_ref, odd_ref, head, slot, width) for slot in range(slots)], axis=0
    )
    return jnp.dot(tile, data, preferred_element_type=jnp.float32)


def token_blocks(first, second):
    low = lane_iota(TILE) < HEAD
    blocks = []
    for tile in range(first.shape[1] // LANES):
        cols = slice(tile * LANES, (tile + 1) * LANES)
        one, two = first[:, cols], second[:, cols]
        blocks.append(jnp.where(low, one, pltpu.roll(two, HEAD, 1)))
        blocks.append(jnp.where(low, pltpu.roll(one, HEAD, 1), two))
    return blocks


def last_term(band_ref, pair, last):
    low = lane_iota(TILE) < HEAD
    at = jnp.where(odd_device(), band_ref.shape[2] - LANES - TILE, 0)
    parts = []
    for half in range(2):
        head = 2 * pair + half
        tile = jnp.concatenate(
            [
                band_ref[head, :, pl.ds(pl.multiple_of(at + LANES, LANES), TILE)],
                band_ref[head, :, pl.ds(pl.multiple_of(at, LANES), TILE)],
            ],
            axis=0,
        )
        parts.append(jnp.dot(tile, last, preferred_element_type=jnp.float32))
    return jnp.where(low, *parts)


def split_body(value_ref, *refs):
    chunk_refs, sems = refs[:CHUNKS], refs[CHUNKS]
    copies = []
    for chunk, ref in enumerate(chunk_refs):
        copies.append(
            pltpu.make_async_copy(
                value_ref.at[pl.ds(own_row(chunk), TILE), :], ref, sems.at[chunk]
            )
        )
        copies[-1].start()
    for copy in copies:
        copy.wait()


def split(value):
    rows, width = value.shape
    return pl.pallas_call(
        split_body,
        in_specs=[pl.BlockSpec(memory_space=pltpu.HBM)],
        out_specs=[VMEM] * CHUNKS,
        out_shape=[pltpu.VMEM((TILE, width), value.dtype)] * CHUNKS,
        scratch_shapes=[pltpu.SemaphoreType.DMA((CHUNKS,))],
        compiler_params=pltpu.CompilerParams(vmem_limit_bytes=2 * MIB),
        cost_estimate=cost(0, 4 * rows * width),
        name="split",
    )(pltpu.with_memory_space_constraint(value, pltpu.HBM))


def product_flops(rows, width, lag):
    return 2 * (width // HEAD) * TILE * (TILE + 2 * lag) * rows // TILE * HEAD


def token_sums(square_ref, inner_ref, sums_ref, start):
    for at in range(0, square_ref.shape[0], LANES):
        rows = slice(at, at + LANES)
        cols = pl.ds(pl.multiple_of(start + at, LANES), LANES)
        sums_ref[0:1, cols] = jnp.sum(square_ref[rows, :].T, axis=0, keepdims=True)
        sums_ref[1:2, cols] = jnp.sum(inner_ref[rows, :].T, axis=0, keepdims=True)


def add_sums(mixed, gate, grad, gain, square_ref, inner_ref, at):
    hidden = gate.astype(jnp.float32) * mixed
    square_ref[at, :] += hidden * hidden
    inner_ref[at, :] += gain * grad.astype(jnp.float32) * hidden


def forward_body(slots, band_ref, own_ref, gate_ref, grad_ref, gain_ref, *refs):
    near_refs, far_refs, refs = refs[:CHUNKS], refs[CHUNKS : 2 * CHUNKS - 1], refs[2 * CHUNKS - 1 :]
    mixed_ref, sums_ref, even_ref, odd_ref, square_ref, inner_ref = refs
    pair = pl.program_id(0)
    heads = (2 * pair, 2 * pair + 1)

    @pl.when(pair == 0)
    def _():
        square_ref[...] = jnp.zeros_like(square_ref)
        inner_ref[...] = jnp.zeros_like(inner_ref)

    blocks = extended(rows_of(own_ref, pair), at_pair(near_refs, pair), at_pair(far_refs, pair))
    lay_out(blocks, even_ref, odd_ref, 2 * pair)
    width = mixed_ref.shape[0] // TILE * HEAD
    results = [band_product(band_ref, h, even_ref, odd_ref, h, slots, width) for h in heads]
    lanes = slab(pair)
    for index, mixed in enumerate(token_blocks(*results)):
        at = slice(index * TILE, (index + 1) * TILE)
        mixed_ref[at, lanes] = mixed
        add_sums(
            mixed, gate_ref[at, lanes], grad_ref[at, lanes], gain_ref[:, lanes], square_ref, inner_ref, at
        )

    @pl.when(pair == pl.num_programs(0) - 1)
    def _():
        token_sums(square_ref, inner_ref, sums_ref, 0)


def forward(band, own, near, far, gate, grad, gain, lag):
    rows, width = gate.shape
    slots = 1 + 2 * lag // TILE
    operands = held(band, own, gate, grad, gain, *near, *far)
    return pl.pallas_call(
        functools.partial(forward_body, slots),
        grid=(width // LANES,),
        in_specs=[VMEM] * len(operands),
        out_specs=[VMEM] * 4,
        out_shape=[
            pltpu.VMEM((rows, width), jnp.float32),
            pltpu.VMEM((2, rows), jnp.float32),
            *layout_scratch(rows, lag, width // HEAD),
        ],
        scratch_shapes=[pltpu.VMEM((rows, LANES), jnp.float32)] * 2,
        compiler_params=params(9),
        cost_estimate=cost(product_flops(rows, width, lag), 16 * rows * width),
        name="forward",
    )(*operands)


def forward_last_body(band_ref, last_ref, gate_ref, grad_ref, gain_ref, mixed_ref, sums_ref, *refs):
    first_ref, out_ref, square_ref, inner_ref = refs
    pair = pl.program_id(0)

    @pl.when(pair == 0)
    def _():
        square_ref[...] = jnp.zeros_like(square_ref)
        inner_ref[...] = jnp.zeros_like(inner_ref)
        out_ref[...] = sums_ref[...]

    lanes, rows = slab(pair), pl.ds(own_row(0), TILE)
    mixed = mixed_ref[rows, lanes] + last_term(band_ref, pair, last_ref[:, lanes])
    first_ref[:, lanes] = mixed
    add_sums(
        mixed,
        gate_ref[rows, lanes],
        grad_ref[rows, lanes],
        gain_ref[:, lanes],
        square_ref,
        inner_ref,
        slice(None),
    )

    @pl.when(pair == pl.num_programs(0) - 1)
    def _():
        token_sums(square_ref, inner_ref, out_ref, own_row(0))


def forward_last(band, last, gate, grad, gain, mixed, sums):
    rows, width = gate.shape
    operands = held(band, last, gate, grad, gain, mixed, sums)
    return pl.pallas_call(
        forward_last_body,
        grid=(width // LANES,),
        in_specs=[VMEM] * len(operands),
        out_specs=[VMEM] * 2,
        out_shape=[
            pltpu.VMEM((TILE, width), jnp.float32),
            pltpu.VMEM((2, rows), jnp.float32),
        ],
        scratch_shapes=[pltpu.VMEM((TILE, LANES), jnp.float32)] * 2,
        compiler_params=params(6),
        cost_estimate=cost(8 * TILE * TILE * width, 6 * TILE * width),
        name="forward_last",
    )(*operands)


def token_columns(full_width, sums_ref, tokens):
    scale = lax.rsqrt(sums_ref[0:1, tokens] / full_width + norm_eps)
    pull = scale * scale * sums_ref[1:2, tokens] / full_width
    return (
        jnp.broadcast_to(scale, (LANES, LANES)).T,
        jnp.broadcast_to(pull, (LANES, LANES)).T,
    )


def mix_grad_body(full_width, sums_ref, mixed_ref, first_ref, gate_ref, grad_ref, gain_ref, *refs):
    out_refs, gain_grad_ref, total_ref = refs[:-2], refs[-2], refs[-1]
    total_ref[...] = jnp.zeros_like(total_ref)
    for chunk, out_ref in enumerate(out_refs):
        for at in range(0, TILE, LANES):
            tokens = pl.ds(pl.multiple_of(own_row(chunk) + at, LANES), LANES)
            rows = slice(at, at + LANES)
            scale, pull = token_columns(full_width, sums_ref, tokens)
            for lane in range(0, mixed_ref.shape[1], LANES):
                cols = slice(lane, lane + LANES)
                gate = gate_ref[tokens, cols].astype(jnp.float32)
                grad = grad_ref[tokens, cols].astype(jnp.float32)
                mixed = mixed_ref[tokens, cols] if chunk else first_ref[rows, cols]
                hidden = gate * mixed
                hidden_grad = scale * (gain_ref[:, cols] * grad - hidden * pull)
                out_ref[rows, cols] = (hidden_grad * gate).astype(out_ref.dtype)
                total_ref[:, cols] += jnp.sum(
                    (grad * (hidden * scale)).reshape(LANES // 8, 8, LANES), axis=0
                )
    gain_grad_ref[...] = jnp.sum(total_ref[...], axis=0, keepdims=True)


def mix_grad_of(full_width, *operands):
    rows, width = operands[1].shape
    operands = held(*operands)
    *chunks, gain_sums = pl.pallas_call(
        functools.partial(mix_grad_body, full_width),
        in_specs=[VMEM] * len(operands),
        out_specs=[VMEM] * (CHUNKS + 1),
        out_shape=[pltpu.VMEM((TILE, width), jnp.bfloat16)] * CHUNKS
        + [pltpu.VMEM((1, width), jnp.float32)],
        scratch_shapes=[pltpu.VMEM((8, width), jnp.float32)],
        compiler_params=pltpu.CompilerParams(vmem_limit_bytes=4 * MIB),
        cost_estimate=cost(14 * rows * width, 10 * rows * width),
        name="mix_grad",
    )(*operands)
    return chunks, gain_sums


def norm_body(full_width, sums_ref, mixed_ref, first_ref, gate_ref, grad_ref, gain_ref, *refs):
    normed_ref, gate_grad_ref = refs
    start = pl.program_id(0) * LANES
    tokens = pl.ds(pl.multiple_of(start, LANES), LANES)
    within = pl.ds(pl.multiple_of(lax.rem(start, TILE), LANES), LANES)
    first = start // TILE == own_row(0) // TILE
    scale, pull = token_columns(full_width, sums_ref, tokens)
    for lane in range(0, mixed_ref.shape[1], LANES):
        cols = slice(lane, lane + LANES)
        gain = gain_ref[:, cols]
        gate = gate_ref[tokens, cols].astype(jnp.float32)
        mixed = jnp.where(first, first_ref[within, cols], mixed_ref[tokens, cols])
        grad = grad_ref[tokens, cols].astype(jnp.float32)
        hidden = gate * mixed
        normed_ref[:, cols] = (hidden * scale * gain).astype(normed_ref.dtype)
        hidden_grad = scale * (gain * grad - hidden * pull)
        gate_grad_ref[:, cols] = (hidden_grad * mixed).astype(gate_grad_ref.dtype)


def norm(full_width, *operands):
    rows, width = operands[1].shape
    operands = held(*operands)
    big = jax.ShapeDtypeStruct((rows, width), jnp.bfloat16)
    return pl.pallas_call(
        functools.partial(norm_body, full_width),
        grid=(rows // LANES,),
        in_specs=[VMEM] * len(operands),
        out_specs=[pl.BlockSpec((LANES, width), lambda g: (g, 0))] * 2,
        out_shape=[big, big],
        compiler_params=params(6),
        cost_estimate=cost(14 * rows * width, 12 * rows * width),
        name="norm",
    )(*operands)


def patched(even_ref, head, half, slot, slots, width, last):
    data = even_ref[head, :, slot * HEAD : slot * HEAD + width]
    low = lane_iota(TILE) < HEAD
    turned = pltpu.roll(last, HEAD, 1)
    if slot == 0:
        tile = data[:, :LANES]
        put = jnp.where(low, last if half == 0 else turned, tile)
        return jnp.concatenate([jnp.where(odd_device(), tile, put), data[:, LANES:]], axis=1)
    if slot == slots - 1:
        tile = data[:, width - LANES :]
        put = jnp.where(low, tile, turned if half == 0 else last)
        return jnp.concatenate([data[:, : width - LANES], jnp.where(odd_device(), put, tile)], axis=1)
    return data


def kernel_grad_body(slots, gain_ref, even_ref, odd_ref, last_ref, *refs):
    mix_refs, (out_ref, mix_even_ref, cells_ref) = refs[:CHUNKS], refs[CHUNKS:]
    pair = pl.program_id(0)
    last = last_ref[:, slab(pair)]
    blocks = natural(at_pair(mix_refs, pair))
    lay_out(blocks, mix_even_ref, None)
    width = len(blocks) * HEAD
    span = cells_ref.shape[1]
    lags = span - LANES
    gains = gain_ref[:, slab(pair)]
    for half in range(2):
        mix = mix_even_ref[half].T
        carry = None
        for lag_slot in range(slots):
            slot, head = slots - 1 - lag_slot, 2 * pair + half
            if slot % 2 == 0:
                data = patched(even_ref, head, half, slot, slots, width, last)
            else:
                data = window(even_ref, odd_ref, head, slot, width)
            cross = jnp.dot(data, mix, preferred_element_type=jnp.float32)
            at = 2 * lag_slot * LANES
            upper, lower = cross[:LANES], cross[LANES:]
            if carry is not None:
                cells_ref[:, at - LANES : at] = carry + lower[:, :LANES]
            cells_ref[:, at : at + LANES] = upper[:, :LANES] + lower[:, LANES:]
            carry = upper[:, LANES:]
        total = cells_ref[0:8, :]
        for group in range(1, LANES // 8):
            total += pltpu.roll(cells_ref[8 * group : 8 * group + 8, :], span - 8 * group, 1)
        row = lax.broadcasted_iota(jnp.int32, (8, span), 0)
        for bit in (1, 2, 4):
            total = jnp.where((row & bit) != 0, pltpu.roll(total, span - bit, 1), total)
        sums = jnp.concatenate(
            [
                jnp.sum(total, axis=0, keepdims=True)[:, :lags],
                gains if half == 0 else pltpu.roll(gains, HEAD, 1),
            ],
            axis=1,
        )
        tall = min(8, out_ref.shape[0])
        row = 2 * pair + half
        group = pl.ds(pl.multiple_of(row // tall * tall, tall), tall)
        here = lax.broadcasted_iota(jnp.int32, (tall, out_ref.shape[1]), 0) == lax.rem(row, tall)
        out_ref[group, :] = jnp.where(here, sums, out_ref[group, :])


def kernel_grad_local(gain_sums, even, odd, last, mix_grad, lag):
    rows, width = len(mix_grad) * TILE, last.shape[1]
    pairs = width // LANES
    slots = 1 + 2 * lag // TILE
    operands = held(gain_sums, even, odd, last, *mix_grad)
    return pl.pallas_call(
        functools.partial(kernel_grad_body, slots),
        grid=(pairs,),
        in_specs=[VMEM] * len(operands),
        out_specs=VMEM,
        out_shape=pltpu.VMEM((2 * pairs, 2 * lag + LANES), jnp.float32),
        scratch_shapes=[
            pltpu.VMEM((2, TILE, rows // TILE * HEAD), jnp.bfloat16),
            pltpu.VMEM((LANES, 2 * lag + LANES), jnp.float32),
        ],
        compiler_params=params(8),
        cost_estimate=cost(product_flops(rows, width, lag), 8 * rows * width),
        name="kernel_grad",
    )(*operands)


def value_grad_body(slots, band_ref, *refs):
    own_refs, near_refs, refs = refs[:CHUNKS], refs[CHUNKS : 2 * CHUNKS], refs[2 * CHUNKS :]
    far_refs, (out_ref, first_ref, even_ref, odd_ref) = refs[: CHUNKS - 1], refs[CHUNKS - 1 :]
    pair = pl.program_id(0)
    own = natural(at_pair(own_refs, pair))
    blocks = extended(own, at_pair(near_refs, pair), at_pair(far_refs, pair))
    lay_out(blocks, even_ref, odd_ref)
    width = len(own) * HEAD
    results = [
        band_product(band_ref, 2 * pair + half, even_ref, odd_ref, half, slots, width)
        for half in range(2)
    ]
    blocks = token_blocks(*results)
    first_ref[:, slab(pair)] = jnp.where(odd_device(), blocks[-1], blocks[0])
    for index, block in enumerate(blocks):
        out_ref[index * TILE : (index + 1) * TILE, :] = block.astype(out_ref.dtype)


def value_grad_of(band, own, near, far, lag):
    rows, width = len(own) * TILE, own[0].shape[1]
    slots = 1 + 2 * lag // TILE
    operands = held(band, *own, *near, *far)
    return pl.pallas_call(
        functools.partial(value_grad_body, slots),
        grid=(width // LANES,),
        in_specs=[VMEM] * len(operands),
        out_specs=[pl.BlockSpec((rows, LANES), lambda g: (0, g)), VMEM],
        out_shape=[
            jax.ShapeDtypeStruct((rows, width), jnp.bfloat16),
            pltpu.VMEM((TILE, width), jnp.float32),
        ],
        scratch_shapes=layout_scratch(rows, lag),
        compiler_params=params(10),
        cost_estimate=cost(product_flops(rows, width, lag), 12 * rows * width),
        name="value_grad",
    )(*operands)


def value_grad_last_body(band_ref, last_ref, first_ref, rest_ref, out_ref, block_ref, sem):
    pair = pl.program_id(0)
    lanes = slab(pair)
    block = first_ref[:, lanes] + last_term(band_ref, pair, last_ref[:, lanes])
    block_ref[:, lanes] = block.astype(block_ref.dtype)

    @pl.when(pair == pl.num_programs(0) - 1)
    def _():
        copy = pltpu.make_async_copy(block_ref, out_ref.at[pl.ds(own_row(0), TILE), :], sem)
        copy.start()
        copy.wait()


def value_grad_last(band, last, first, rest):
    width = first.shape[1]
    operands = held(band, last, first)
    return pl.pallas_call(
        value_grad_last_body,
        grid=(width // LANES,),
        in_specs=[VMEM] * len(operands) + [pl.BlockSpec(memory_space=pl.ANY)],
        out_specs=pl.BlockSpec(memory_space=pl.ANY),
        out_shape=jax.ShapeDtypeStruct(rest.shape, rest.dtype),
        input_output_aliases={len(operands): 0},
        scratch_shapes=[pltpu.VMEM((TILE, width), jnp.bfloat16), pltpu.SemaphoreType.DMA(())],
        compiler_params=params(6),
        cost_estimate=cost(8 * TILE * TILE * width, 6 * TILE * width),
        name="value_grad_last",
    )(*operands, rest)


def swapped(chunk):
    count = lax.axis_size("seq")
    return lax.ppermute(chunk, "seq", [(i, i ^ 1) for i in range(count)])


def relayed(chunk):
    count = lax.axis_size("seq")
    pairs = [(i, i + 2) if i % 2 == 0 else (i, i - 2) for i in range(count)]
    return lax.ppermute(chunk, "seq", [(i, j) for i, j in pairs if 0 <= j < count])


def terms_over_bits(value, bits):
    count = lax.axis_size("seq")
    terms = []
    for mask in range(1, 1 << len(bits)):
        flip = sum(1 << bit for at, bit in enumerate(bits) if mask >> at & 1)
        terms.append(lax.ppermute(value, "seq", [(i, i ^ flip) for i in range(count)]))
    return terms


def sum_over(value, axis):
    count = lax.axis_size(axis)
    if count & (count - 1):
        return lax.psum(value, axis)
    for bit in range(count.bit_length() - 1):
        value += lax.ppermute(value, axis, [(i, i ^ (1 << bit)) for i in range(count)])
    return value


def on_device(gate_acts, value_acts, kernel, norm_gain, out_grad):
    rows, width = value_acts.shape
    heads = kernel.shape[0]
    lag = kernel.shape[1] // 2
    count = lax.axis_size("seq")
    assert width == heads * HEAD and rows == lag == CHUNKS * TILE
    assert count & (count - 1) == 0
    full_width = width * lax.axis_size("chan")
    gain = norm_gain.reshape(1, width)
    taps = kernel.astype(jnp.float32)

    ahead, behind = lax.optimization_barrier(
        (band_rows(taps[:, ::-1], 1, TILE - 1), band_rows(taps, 0, TILE))
    )
    band = bands(ahead)
    *chunks, last = split(value_acts)
    near = [swapped(chunk) for chunk in [*chunks, after(last, band)]]
    far = [relayed(chunk) for chunk in near]
    mixed, sums, even, odd = forward(
        band, value_acts, near, far[:-1], gate_acts, out_grad, gain, lag
    )
    first, sums = forward_last(band, far[-1], gate_acts, out_grad, gain, mixed, sums)
    sums = sum_over(sums, "chan")
    args = (mixed, first, gate_acts, out_grad, gain)
    mix_grad, gain_sums = mix_grad_of(full_width, sums, *args)

    grad_near = [swapped(part) for part in mix_grad]
    totals = kernel_grad_local(gain_sums, even, odd, far[-1], mix_grad, lag)
    normed, gate_grad = norm(full_width, after(sums, grad_near[0]), *args)
    back_band = bands(after(behind, grad_near[1]))
    grad_near[0], totals = lax.optimization_barrier((grad_near[0], totals))
    grad_near[3], normed, gate_grad, back_band = lax.optimization_barrier(
        (grad_near[3], normed, gate_grad, back_band)
    )
    bits = list(range(count.bit_length() - 1))
    for bit in bits[2:]:
        half = lax.optimization_barrier(totals.astype(jnp.bfloat16))
        other = terms_over_bits(half, [bit])[0]
        totals = half.astype(jnp.float32) + other.astype(jnp.float32)
    grad_near[1], totals = lax.optimization_barrier((grad_near[1], totals))
    grad_far = [relayed(chunk) for chunk in grad_near]
    totals, *grad_far[:2] = lax.optimization_barrier((totals, *grad_far[:2]))
    terms = [totals] + terms_over_bits(totals, bits[:2])
    value_grad, first = value_grad_of(back_band, mix_grad, grad_near, grad_far[:-1], lag)
    value_grad = value_grad_last(back_band, grad_far[-1], first, value_grad)
    value_grad, *terms = lax.optimization_barrier((value_grad, *terms))
    totals = sum(terms[1:], terms[0])
    tokens = rows * count
    kernel_grad = totals[:, : 2 * lag] / math.sqrt(tokens * HEAD)
    gain_grad = totals[:, 2 * lag : 2 * lag + HEAD].reshape(width) / math.sqrt(tokens)
    return (normed, gate_grad, value_grad, kernel_grad, gain_grad)


def solution(mesh):
    placed = (P("seq", "chan"), P("seq", "chan"), P("chan", None), P("chan"), P("seq", "chan"))
    return jax.shard_map(
        on_device,
        mesh=mesh,
        in_specs=placed,
        out_specs=(
            P("seq", "chan"),
            P("seq", "chan"),
            P("seq", "chan"),
            P("chan", None),
            P("chan"),
        ),
        check_vma=False,
    )
```
